32 devices in a mesh: dp: 16 (over z, y, x), head: 2 (over core).
Axes of the slice: x: 2, y: 2, z: 4, core: 2. Of those that a mesh axis runs over, the one named last changes fastest.
Arguments:
- tokens: bfloat16 [32768, 192], P(('dp', 'head')), may hold values from -6 to 6
- cotangent: bfloat16 [32768, 192], P(('dp', 'head')), may hold values from -6 to 6
- image_sides: int32 [32, 10], P(('dp', 'head')), may hold values from 0 to 18, as said below
- state_mixing: bfloat16 [12288], P(('dp', 'head')), may hold values from -0.1796875 to 0.1796875
- small_params: bfloat16 [512], P(('dp', 'head')), may hold values from 0.029 to 1.51
- project_in: bfloat16 [110592], P(('dp', 'head')), may hold values from -0.4375 to 0.4375
- project_out: bfloat16 [36864], P(('dp', 'head')), may hold values from -1.25 to 1.25
- expand_weight: bfloat16 [147456], P(('dp', 'head')), may hold values from -0.4375 to 0.4375
- shrink_weight: bfloat16 [147456], P(('dp', 'head')), may hold values from -0.21875 to 0.21875
Outputs:
- activations: bfloat16 [32768, 192], P(('dp', 'head'))
- grad_tokens: float32 [32768, 192], P(('dp', 'head'))
- penalty: float32 [], replicated
- grad_mixing: float32 [12288], P(('dp', 'head'))
- grad_small: float32 [512], P(('dp', 'head'))
- grad_project_in: float32 [110592], P(('dp', 'head'))
- grad_project_out: float32 [36864], P(('dp', 'head'))
- grad_expand: float32 [147456], P(('dp', 'head'))
- grad_shrink: float32 [147456], P(('dp', 'head'))
The draws below stay inside these ranges and needn't reach their ends.
Inputs may be any that keep to these rules, and one draw needn't show every extreme that they name: `image_sides`: row g lists, in packing order, the sides of the images on device g's canvas, each 10, 14 or 18, with 0 for an empty slot; the areas of a row add up to at most 1024, and in every draw some row adds up to exactly 1024.
All inputs are finite; a program needn't handle non-finite values.
Results may differ from the reference program's by a relative error of at most 0.007.
Values may be sent and summed in bfloat16 or wider, within the bound.
A program may use at most 448 MiB of HBM per device.

```python
import math
from functools import partial
import jax
import jax.numpy as jnp
from jax import lax

D = 192
HEADS = 3
HEAD_DIM = 64
FF = 768
STATES = 16
DIRS = 4
SIDE_S = 10
SIDE_M = 14
SIDE_L = 18
CANVAS = 1024
IMG_DEV = 10
TOKENS = 32768
DEVICES = 32


def draw_image_sides(key, part):
    key = jax.random.fold_in(key, 11)
    pick_key, limit_key, full_key = jax.random.split(key, 3)
    picks = jax.random.randint(pick_key, (IMG_DEV, DEVICES), 0, 3)
    candidate = jnp.where(picks == 0, SIDE_S, jnp.where(picks == 1, SIDE_M, SIDE_L)).astype(jnp.int32)
    rows = jnp.arange(DEVICES, dtype=jnp.int32)
    lowest = CANVAS // 3
    climb = lowest + rows * (CANVAS - lowest) // max(DEVICES - 1, 1)
    jitter = jax.random.randint(limit_key, (DEVICES,), 0, CANVAS // 8 + 1)
    limits = jnp.maximum(climb - jitter, CANVAS // 4).astype(jnp.int32)

    def place(used, sizes):
        area = sizes * sizes
        fits = used + area <= limits
        return (used + jnp.where(fits, area, 0), jnp.where(fits, sizes, 0).astype(jnp.int32))
    filled, chosen = lax.scan(place, jnp.zeros((DEVICES,), jnp.int32), candidate)
    slots = jnp.arange(IMG_DEV, dtype=jnp.int32)
    repeats = CANVAS // (SIDE_L * SIDE_L + 7 * SIDE_S * SIDE_S)
    pattern = jnp.where(slots < 8 * repeats, jnp.where(slots % 8 == 0, SIDE_L, SIDE_S), 0).astype(jnp.int32)
    full_device = jax.random.randint(full_key, (), 0, DEVICES)
    return jnp.where(rows[:, None] == full_device, pattern[None, :], chosen.T).astype(jnp.int32)


def draw_small_params(key, part):
    key = jax.random.fold_in(key, 5)
    rate_key, gain_key = jax.random.split(key, 2)
    count = 2 * DIRS * STATES
    rates = jnp.exp(jax.random.uniform(rate_key, (count,), jnp.float32, math.log(0.03), math.log(1.5)))
    gains = 1.0 + 0.1 * jnp.clip(jax.random.normal(gain_key, (2 * D,), jnp.float32), -4.0, 4.0)
    return jnp.concatenate([rates, gains]).astype(jnp.bfloat16)


def level_of(stream_key, shape, cuts, least, high):
    def one(axis_at, shards_of):
        steps = jax.random.uniform(jax.random.fold_in(jax.random.fold_in(stream_key, 6), axis_at), (shards_of,), jnp.float32, least / len(cuts), high / len(cuts))
        return jnp.repeat(jnp.exp(steps), shape[axis_at] // shards_of).reshape((-1,) + (1,) * (len(shape) - axis_at - 1))

    level = one(*cuts[0])
    for cut in cuts[1:]:
        level = level * one(*cut)
    return level


def scatter_about(stream_key, dims, width, most, cuts=(), held_as=jnp.bfloat16):
    factor_of = level_of(stream_key, dims, cuts, -0.22, 0.18) if cuts else 1.0
    drawn = jax.random.normal(stream_key, dims, jnp.float32) * width * factor_of
    return jnp.minimum(jnp.maximum(drawn, -most), most).astype(held_as)


def setup_inputs(seed: int = 0) -> dict:
    seeds = jax.random.split(jax.random.key(seed), 10)
    return {
        "tokens": scatter_about(seeds[0], (TOKENS, D), 1.0, 6.0, ((0, 32),)),
        "cotangent": scatter_about(seeds[1], (TOKENS, D), 1.0, 6.0, ((0, 32),)),
        "image_sides": draw_image_sides(jax.random.fold_in(seeds[9], 71), 0),
        "state_mixing": scatter_about(seeds[3], (DIRS * STATES * D,), 0.03, 0.1796875, ((0, 32),)),
        "small_params": draw_small_params(jax.random.fold_in(seeds[9], 71), 0),
        "project_in": scatter_about(seeds[5], (3 * D * D,), D ** -0.5, 0.4375, ((0, 32),)),
        "project_out": scatter_about(seeds[6], (D * D,), (D // 8) ** -0.5, 1.25, ((0, 32),)),
        "expand_weight": scatter_about(seeds[7], (D * FF,), D ** -0.5, 0.4375, ((0, 32),)),
        "shrink_weight": scatter_about(seeds[8], (FF * D,), FF ** -0.5, 0.21875, ((0, 32),)),
    }


SIGNS = ((1, 1), (1, -1), (-1, 1), (-1, -1))
HIGH = lax.Precision.HIGHEST

@jax.custom_vjp
def low(v):
    return lax.optimization_barrier(v.astype(jnp.bfloat16)).astype(jnp.float32)

@jax.custom_vjp
def low_back(v):
    return v

def low_keep(v):
    return (low(v), None)

def low_pass(kept, grad):
    return (grad,)

def back_keep(v):
    return (v, None)

def back_low(kept, grad):
    return (low(grad),)
low.defvjp(low_keep, low_pass)
low_back.defvjp(back_keep, back_low)

def geometry(side_row, canvas):
    slots = side_row.shape[0]
    areas = side_row * side_row
    ends = jnp.cumsum(areas).astype(jnp.int32)
    starts = ends - areas
    places = jnp.arange(canvas, dtype=jnp.int32)
    segment = lax.optimization_barrier(jnp.sum((ends[None, :] <= places[:, None]).astype(jnp.int32), axis=1)).astype(jnp.int32)
    onehot = (segment[:, None] == jnp.arange(slots, dtype=jnp.int32)[None, :]).astype(jnp.int32)
    begin = lax.optimization_barrier(jnp.sum(onehot * starts[None, :], axis=1)).astype(jnp.int32)
    extent = jnp.maximum(lax.optimization_barrier(jnp.sum(onehot * side_row[None, :], axis=1)), 1).astype(jnp.int32)
    offset = places - begin
    return (segment, segment < slots, offset // extent, offset % extent)

def quadrant(segment, live, row_pos, col_pos, row_sign, col_sign):
    row_gap = row_pos[:, None] - row_pos[None, :]
    col_gap = col_pos[:, None] - col_pos[None, :]
    inside = (segment[:, None] == segment[None, :]) & live[:, None] & live[None, :]
    inside = inside & (row_sign * row_gap >= 0) & (col_sign * col_gap >= 0)
    return (inside, jnp.abs(row_gap).astype(jnp.float32), jnp.abs(col_gap).astype(jnp.float32))

def layer_unit(values):
    centered = values - lax.optimization_barrier(jnp.mean(values, axis=-1, keepdims=True))
    spread = lax.optimization_barrier(jnp.mean(centered * centered, axis=-1, keepdims=True))
    return centered * lax.rsqrt(spread + 1e-05)

def block(inputs, segment, live, row_pos, col_pos, mixing, rate_row, rate_col, gain_one, gain_two, weight_in, weight_out, weight_up, weight_down):
    canvas = inputs.shape[0]
    live_col = live.astype(jnp.float32)[:, None]
    normed = low(layer_unit(inputs) * gain_one)
    mixed_sum = jnp.zeros((canvas, D), jnp.float32)
    squares = []
    for direction in range(DIRS):
        inside, row_far, col_far = quadrant(segment, live, row_pos, col_pos, SIGNS[direction][0], SIGNS[direction][1])
        decay = jnp.where(inside[None], jnp.exp(-rate_row[direction][:, None, None] * row_far[None] - rate_col[direction][:, None, None] * col_far[None]), 0.0)
        images = low_back(jnp.einsum('ntu,uc->ntc', low(decay), normed, precision=HIGH))
        branch_sum = lax.optimization_barrier(jnp.sum(images * mixing[direction][:, None, :], axis=0))
        squares.append(jnp.sum(live_col * branch_sum * branch_sum))
        mixed_sum = mixed_sum + branch_sum
    mixed = low(mixed_sum)
    triple = low(low_back(jnp.dot(mixed, weight_in, precision=HIGH)))
    queries = triple[:, :D].reshape(canvas, HEADS, HEAD_DIM)
    keys_all = triple[:, D:2 * D].reshape(canvas, HEADS, HEAD_DIM)
    values_all = triple[:, 2 * D:].reshape(canvas, HEADS, HEAD_DIM)
    attend = segment[:, None] == segment[None, :]
    scores = low_back(jnp.einsum('thd,uhd->htu', queries, keys_all, precision=HIGH) * (1.0 / math.sqrt(HEAD_DIM)))
    masked = jnp.where(attend[None], scores, -1e+30)
    top = lax.optimization_barrier(jnp.max(masked, axis=-1, keepdims=True))
    expo = jnp.exp(masked - top)
    probs = expo / lax.optimization_barrier(jnp.sum(expo, axis=-1, keepdims=True))
    heads_out = jnp.einsum('htu,uhd->thd', low(probs), values_all, precision=HIGH).reshape(canvas, D)
    heads_out = low(low_back(heads_out))
    after = inputs + live_col * low_back(jnp.dot(heads_out, weight_out, precision=HIGH))
    normed_two = low(layer_unit(after) * gain_two)
    hidden_pre = low_back(jnp.dot(normed_two, weight_up, precision=HIGH))
    activation = low(0.5 * hidden_pre * (1.0 + lax.erf(hidden_pre * (1.0 / math.sqrt(2.0)))))
    output = after + live_col * low_back(jnp.dot(activation, weight_down, precision=HIGH))
    return (output, jnp.stack(squares))

def reference(tokens, cotangent, image_sides, state_mixing, small_params, project_in, project_out, expand_weight, shrink_weight):
    segment, live, row_pos, col_pos = jax.vmap(partial(geometry, canvas=CANVAS))(image_sides)
    spread_in = tokens.astype(jnp.float32).reshape(DEVICES, CANVAS, D)
    count = DIRS * STATES

    def forward(inputs, mixing_flat, small_flat, in_flat, out_flat, up_flat, down_flat):
        mixing = mixing_flat.reshape(DIRS, STATES, D)
        rate_row = small_flat[:count].reshape(DIRS, STATES)
        rate_col = small_flat[count:2 * count].reshape(DIRS, STATES)
        gain_one = small_flat[2 * count:2 * count + D]
        gain_two = small_flat[2 * count + D:]
        weight_in = in_flat.reshape(D, 3 * D)
        weight_out = out_flat.reshape(D, D)
        weight_up = up_flat.reshape(D, FF)
        weight_down = down_flat.reshape(FF, D)
        run_block = jax.checkpoint(block)

        def step(carry, pieces):
            canvas_in, seg_row, live_row, rows, cols = pieces
            output, squares = run_block(canvas_in, seg_row, live_row, rows, cols, mixing, rate_row, rate_col, gain_one, gain_two, weight_in, weight_out, weight_up, weight_down)
            return (carry + squares, output)
        totals, outputs = lax.scan(step, jnp.zeros((DIRS,), jnp.float32), (inputs, segment, live, row_pos, col_pos))
        return (outputs, totals)
    (outputs, totals), pull = jax.vjp(forward, spread_in, state_mixing.astype(jnp.float32), small_params.astype(jnp.float32), project_in.astype(jnp.float32), project_out.astype(jnp.float32), expand_weight.astype(jnp.float32), shrink_weight.astype(jnp.float32))
    grads = pull((cotangent.astype(jnp.float32).reshape(DEVICES, CANVAS, D), jnp.zeros((DIRS,), jnp.float32)))
    penalty = jnp.sum(jnp.sqrt(totals / (TOKENS * D) + 1e-06))
    return (outputs.reshape(TOKENS, D).astype(jnp.bfloat16), grads[0].reshape(TOKENS, D), penalty, grads[1], grads[2], grads[3], grads[4], grads[5], grads[6])
```

```python
import functools
import math

import jax
import jax.numpy as jnp
from jax import lax
from jax.experimental import pallas as pl
from jax.experimental.pallas import tpu as pltpu
from jax.sharding import PartitionSpec as P

D=192; STATES=16; D2=2*D; SMAX=18; SLOTS=10
EPSILON=1e-5
F32=jnp.float32; BF=jnp.bfloat16
PADC={10:16,14:16,18:24}

def col_matrix(rate_lane, swap):
    width=rate_lane.shape[1]
    rows=lax.broadcasted_iota(jnp.int32,(48,width),0)
    first=rows<24
    c=jnp.where(first,rows,rows-24)
    u=lax.broadcasted_iota(jnp.int32,(48,width),1)//16
    gap=(c-u) if not swap else (u-c)
    sign=jnp.where(first,1,-1)
    rate=jnp.where(first,rate_lane[0:1],rate_lane[1:2])
    far=jnp.abs(gap).astype(F32)
    value=jnp.exp(-rate*far)
    return jnp.where(sign*gap>=0,value,0.0), far

def norm_rows(t):
    x=t.astype(F32)
    cen=x-jnp.mean(x,axis=-1,keepdims=True)
    sc=lax.rsqrt(jnp.mean(cen*cen,axis=-1,keepdims=True)+EPSILON)
    return cen*sc, sc

def lane_pair(two):
    lane=lax.broadcasted_iota(jnp.int32,(16,D2),1)
    return jnp.where(lane<D,two[:,0:1],two[:,1:2])

def fwd_body(sides, tok, gain, mix, rrow, rcol, mixed, squares, xx, ssm, sq, ypad, w, cm):
    canvas=tok.shape[0]
    unit,_=norm_rows(tok[...])
    normed=(unit*gain[...]).astype(BF).astype(F32)
    xx[:,0:D]=normed
    xx[:,D:D2]=normed
    ssm[...]=jnp.zeros_like(ssm)
    sq[...]=jnp.zeros_like(sq)
    for p in range(2):
        cm[p]=col_matrix(rcol[p],False)[0].astype(BF)
    def image(s,start):
        sp=PADC[s]; depth=s*16
        for p in range(2):
            m=mix[p].astype(F32); a=lane_pair(jnp.exp(-rrow[p]))
            def scan(j,_):
                for h in range(2):
                    c=2*j+h
                    state=None
                    for step in range(s):
                        r=step if p==0 else s-1-step
                        x=xx[pl.ds(start+r*s+c,1),:]
                        term=m*x
                        state=term if state is None else state*a+term
                        w[r,pl.ds(pl.multiple_of(c*16,16),16),:]=state.astype(BF)
                return 0
            lax.fori_loop(0,s//2,scan,0)
            left=cm[p]
            if s!=18:
                left=jnp.concatenate([left[0:16,0:depth],left[24:40,0:depth]],axis=0)
            def rows(j,_):
                for h in range(2):
                    r=2*j+h
                    out=jnp.dot(left,w[r,0:depth,:],preferred_element_type=F32)
                    y0=out[0:s,0:D]
                    y1=out[sp:sp+s,D:D2]
                    sq[2*p,0:s]+=y0*y0
                    sq[2*p+1,0:s]+=y1*y1
                    if p==0: ypad[r,0:s]=y0+y1
                    else: ypad[r,0:s]+=y0+y1
                return 0
            lax.fori_loop(0,s//2,rows,0)
        def place(r,_):
            for c in range(s):
                ssm[pl.ds(start+r*s+c,1),:]=ypad[r,pl.ds(c,1),:]
            return 0
        lax.fori_loop(0,s,place,0)
    def each(k,start):
        side=sides[0,k]
        for s in (10,14,18):
            @pl.when(side==s)
            def _(): image(s,start)
        return start+side*side
    lax.fori_loop(0,SLOTS,each,0)
    mixed[...]=ssm[0:canvas,:].astype(BF)
    squares[...]=jnp.sum(jnp.sum(sq[...],axis=2),axis=1,keepdims=True)

def ssm_forward(sides, tok, gain, mix, rrow, rcol):
    canvas=tok.shape[0]
    vm=pl.BlockSpec(memory_space=pltpu.VMEM)
    return pl.pallas_call(fwd_body,
        out_shape=(jax.ShapeDtypeStruct((canvas,D),BF),jax.ShapeDtypeStruct((4,1),F32)),
        in_specs=[pl.BlockSpec(memory_space=pltpu.SMEM)]+[vm]*5, out_specs=(vm,vm),
        scratch_shapes=[pltpu.VMEM((canvas,D2),F32),pltpu.VMEM((canvas+24,D),F32),pltpu.VMEM((4,24,D),F32),pltpu.VMEM((SMAX,24,D),F32),
            pltpu.VMEM((SMAX,SMAX*16,D2),BF),pltpu.VMEM((2,48,SMAX*16),BF)],
        compiler_params=pltpu.CompilerParams(vmem_limit_bytes=50<<20))(sides,tok,gain,mix,rrow,rcol)

def prep(mixing, rate_row, rate_col):
    mix=mixing.reshape(2,2,16,D).transpose(0,2,1,3).reshape(2,16,D2)
    rrow=rate_row.astype(F32).reshape(2,2,16).transpose(0,2,1)
    rcol=jnp.tile(rate_col.astype(F32).reshape(2,2,1,16),(1,1,SMAX,1)).reshape(2,2,SMAX*16)
    return mix,rrow,rcol

def bwd_body(sides, tok, gain, gssm, gafter, mix, rrow, rcol, gtok, gmix, grow, gcol, ggain,
             gg, canvas_out, ypad, bd, xi, xd, mb, c2, ct, cd, acc):
    canvas=tok.shape[0]
    unit,scale=norm_rows(tok[...])
    g=gssm[...]
    gg[0]=g[:,0:128]
    gg[1]=jnp.concatenate([g[:,128:D],g[:,0:64]],axis=1)
    gg[2]=g[:,64:D]
    canvas_out[0:canvas]=(unit*gain[...]).astype(BF).astype(F32)
    bd[...]=jnp.zeros_like(bd)
    acc[...]=jnp.zeros_like(acc)
    for p in range(2):
        value,far=col_matrix(rcol[p],True)
        c2[p]=value.astype(BF)
        ct[p]=value.T
        cd[p]=(value*far).T
    def image(s,start):
        sp=PADC[s]; depth=s*16
        lane=lax.broadcasted_iota(jnp.int32,(depth,48),1)
        keep=jnp.where(lane<24,lane,lane-24)<s
        def gather(r,_):
            for c in range(s):
                row=canvas_out[pl.ds(start+r*s+c,1),:]
                bd[r,pl.ds(c,1),0:D]=row
                bd[r,pl.ds(24+c,1),D:D2]=row
            return 0
        lax.fori_loop(0,s,gather,0)
        for p in range(2):
            left=jnp.where(keep,ct[p,0:depth],0.0).astype(BF)
            leftd=jnp.where(keep,cd[p,0:depth],0.0).astype(BF)
            def spread(j,_):
                for h in range(2):
                    r=2*j+h
                    b=bd[r].astype(BF)
                    xi[r,0:depth]=jnp.dot(left,b,preferred_element_type=F32)
                    xd[r,0:depth]=jnp.dot(leftd,b,preferred_element_type=F32)
                return 0
            lax.fori_loop(0,s//2,spread,0)
            for q in range(3):
                ch=slice(q*128,(q+1)*128)
                m=mix[p,:,ch].astype(F32); a=lane_pair(jnp.exp(-rrow[p]))[:,ch]
                def scan(j,sums):
                    s1,s2,s3=sums
                    for h in range(2):
                        c=2*j+h
                        at=pl.ds(pl.multiple_of(c*16,16),16)
                        mu=None
                        for step in range(s):
                            r=s-1-step if p==0 else step
                            gr=gg[q,pl.ds(start+r*s+c,1),:]
                            e=xi[r,at,ch]
                            if mu is None:
                                mu=jnp.broadcast_to(gr,(16,128))
                            else:
                                low=mu*a
                                nu=low if nu is None else nu*a+low
                                mu=gr+low
                                s2=s2+nu*e
                            if step==0: nu=None
                            s1=s1+mu*e
                            s3=s3+mu*xd[r,at,ch]
                            mb[r,at,ch]=(m*mu).astype(BF)
                    return s1,s2,s3
                sums=lax.fori_loop(0,s//2,scan,(acc[p,0,:,ch],acc[p,1,:,ch],acc[p,2,:,ch]))
                for i in range(3): acc[p,i,:,ch]=sums[i]
            left2=c2[p]
            if s!=18:
                left2=jnp.concatenate([left2[0:16,0:depth],left2[24:40,0:depth]],axis=0)
            def rows(j,_):
                for h in range(2):
                    r=2*j+h
                    out=jnp.dot(left2,mb[r,0:depth,:],preferred_element_type=F32)
                    y=out[0:s,0:D]+out[sp:sp+s,D:D2]
                    if p==0: ypad[r,0:s]=y
                    else: ypad[r,0:s]+=y
                return 0
            lax.fori_loop(0,s//2,rows,0)
        def place(r,_):
            for c in range(s):
                canvas_out[pl.ds(start+r*s+c,1),:]=ypad[r,pl.ds(c,1),:]
            return 0
        lax.fori_loop(0,s,place,0)
    def each(k,start):
        side=sides[0,k]
        for s in (10,14,18):
            @pl.when(side==s)
            def _(): image(s,start)
        return start+side*side
    end=lax.fori_loop(0,SLOTS,each,0)
    slot=lax.broadcasted_iota(jnp.int32,(canvas,1),0)
    gn=jnp.where(slot<end,canvas_out[0:canvas],0.0)
    ggain[...]=jnp.sum(gn*unit,axis=0,keepdims=True)
    scaled=gn*gain[...]
    inner=jnp.mean(scaled*unit,axis=-1,keepdims=True)
    gtok[...]=gafter[...]+scale*(scaled-jnp.mean(scaled,axis=-1,keepdims=True)-unit*inner)
    for p in range(2):
        m=mix[p].astype(F32)
        gmix[p]=acc[p,0]
        r2=m*acc[p,1]; r3=m*acc[p,2]
        for d in range(2):
            ch=slice(d*D,(d+1)*D)
            grow[p,:,d:d+1]=-jnp.sum(r2[:,ch],axis=1,keepdims=True)
            gcol[p,:,d:d+1]=-jnp.sum(r3[:,ch],axis=1,keepdims=True)

def ssm_backward(sides, tok, gain, gssm, gafter, mix, rrow, rcol):
    canvas=tok.shape[0]
    vm=pl.BlockSpec(memory_space=pltpu.VMEM)
    V=pltpu.VMEM
    sh=jax.ShapeDtypeStruct
    return pl.pallas_call(bwd_body,
        out_shape=(sh((canvas,D),F32),sh((2,16,D2),F32),sh((2,16,2),F32),sh((2,16,2),F32),sh((1,D),F32)),
        in_specs=[pl.BlockSpec(memory_space=pltpu.SMEM)]+[vm]*7, out_specs=(vm,)*5,
        scratch_shapes=[V((3,canvas,128),F32),V((canvas+24,D),F32),V((SMAX,24,D),F32),V((SMAX,48,D2),F32),
            V((SMAX,SMAX*16,D2),F32),V((SMAX,SMAX*16,D2),F32),V((SMAX,SMAX*16,D2),BF),
            V((2,48,SMAX*16),BF),V((2,SMAX*16,48),F32),V((2,SMAX*16,48),F32),V((2,3,16,D2),F32)],
        compiler_params=pltpu.CompilerParams(vmem_limit_bytes=56<<20))(sides,tok,gain,gssm,gafter,mix,rrow,rcol)

F32=jnp.float32; BF=jnp.bfloat16
AXES=("dp","head")

def digits(count):
    out=[]; weight=1
    while weight<count:
        radix=4 if weight*4<=count else 2
        out.append((weight,radix)); weight*=radix
    return out[::-1]

def greet(dp, head, offsets):
    barrier=pltpu.get_barrier_semaphore()
    peers=[(dp^off,head) for off in offsets]+[(dp,1-head)]
    for peer in peers:
        pl.semaphore_signal(barrier,inc=1,device_id=peer,device_id_type=pl.DeviceIdType.MESH)
    pl.semaphore_wait(barrier,len(peers))

def gather_body(count, x, buf, send, recv):
    dp=lax.axis_index("dp"); head=lax.axis_index("head")
    stages=digits(count)
    greet(dp,head,[w*k for w,r in stages for k in range(1,r)])
    mine=dp*2+head
    buf[pl.ds(mine,1)]=x[...][None]
    started=[]
    def push(off,off_to,h_to):
        block=buf.at[(dp^off)*2+head]
        n=len(started)
        peer=(dp,1-head) if h_to else (dp^off^off_to,head)
        copy=pltpu.make_async_remote_copy(src_ref=block,dst_ref=block,send_sem=send.at[n],
            recv_sem=recv.at[off_to+count*h_to],device_id=peer,device_id_type=pl.DeviceIdType.MESH)
        copy.start(); started.append(copy)
    def arrived(off,h):
        block=buf.at[(dp^off)*2+(1-head if h else head)]
        pltpu.make_async_remote_copy(src_ref=block,dst_ref=block,send_sem=send.at[0],
            recv_sem=recv.at[off+count*h],device_id=(dp,1-head),device_id_type=pl.DeviceIdType.MESH).wait_recv()
    held=[(0,0)]
    at=0
    while at<len(held):
        off,stage=held[at]; at+=1
        if off: arrived(off,0)
        for t in range(stage,len(stages)):
            w,r=stages[t]
            for k in range(1,r): push(off,off^(w*k),0)
        push(off,off,1)
        if off==0:
            order=[]
        for t in range(stage,len(stages)):
            w,r=stages[t]
            for k in range(1,r): held.append((off^(w*k),t+1))
    for off in range(count): arrived(off,1)
    for copy in started: copy.wait_send()

def gather(count, x):
    n=2*count
    return pl.pallas_call(functools.partial(gather_body,count),
        out_shape=jax.ShapeDtypeStruct((n,)+x.shape,x.dtype),
        in_specs=[pl.BlockSpec(memory_space=pltpu.VMEM)],out_specs=pl.BlockSpec(memory_space=pltpu.VMEM),
        scratch_shapes=[pltpu.SemaphoreType.DMA((n-1,)),pltpu.SemaphoreType.DMA((n,))],
        compiler_params=pltpu.CompilerParams(collective_id=0,has_side_effects=True))(x)

def scatter_body(count, kinds, *refs):
    m=len(kinds)
    xs=refs[0:m]; outs=refs[m:2*m]; accs=refs[2*m:3*m]; sends=refs[3*m:4*m]; lands=refs[4*m:5*m]
    send,recv=refs[5*m:]
    dp=lax.axis_index("dp"); head=lax.axis_index("head")
    stages=digits(count)[::-1]
    greet(dp,head,[w*k for w,r in stages for k in range(1,r)])
    started=[]
    slots={}
    for off in range(count): slots[(-1,off)]=len(slots)
    for t,(w,r) in enumerate(stages):
        for k in range(1,r):
            for high in range(0,count,w*r): slots[(t,k*w+high)]=len(slots)
    def push(t,off,peer,values):
        n=slots[(t,off)]
        for i in range(m):
            sends[i][n]=values[i].astype(kinds[i])
            copy=pltpu.make_async_remote_copy(src_ref=sends[i].at[n],dst_ref=lands[i].at[n],send_sem=send.at[i,n],
                recv_sem=recv.at[i,n],device_id=peer,device_id_type=pl.DeviceIdType.MESH)
            copy.start(); started.append(copy)
    def take(t,off):
        n=slots[(t,off)]
        out=[]
        for i in range(m):
            pltpu.make_async_remote_copy(src_ref=sends[i].at[n],dst_ref=lands[i].at[n],send_sem=send.at[i,n],
                recv_sem=recv.at[i,n],device_id=(dp,1-head),device_id_type=pl.DeviceIdType.MESH).wait_recv()
            out.append(lands[i][n].astype(F32))
        return out
    level={}
    def settle(off,t):
        if off not in level:
            got=take(-1,off)
            for i in range(m): accs[i][off]=xs[i][(dp^off)*2+head]+got[i]
            level[off]=0
        while level[off]<t:
            w,r=stages[level[off]]
            total=[accs[i][off] for i in range(m)]
            for k in range(1,r):
                got=take(level[off],off^(k*w))
                total=[a+b for a,b in zip(total,got)]
            for i in range(m): accs[i][off]=total[i]
            level[off]+=1
    def rank(off):
        return tuple(0 if (off//w)%r else 1 for w,r in stages)
    for off in sorted(range(count),key=rank):
        push(-1,off,(dp,1-head),[xs[i][(dp^off)*2+1-head] for i in range(m)])
    for t,(w,r) in enumerate(stages):
        for k in range(1,r):
            for high in range(0,count,w*r):
                off=k*w+high
                settle(off,t)
                push(t,off,(dp^(k*w),head),[accs[i][off] for i in range(m)])
    settle(0,len(stages))
    for i in range(m): outs[i][...]=accs[i][0]
    for copy in started: copy.wait_send()

def scatter(count, arrays, kinds):
    n=2*count; m=len(arrays)
    vm=pl.BlockSpec(memory_space=pltpu.VMEM)
    shapes=[a.shape[1:] for a in arrays]
    return pl.pallas_call(functools.partial(scatter_body,count,kinds),
        out_shape=tuple(jax.ShapeDtypeStruct(s,F32) for s in shapes),
        in_specs=[vm]*m,out_specs=(vm,)*m,
        scratch_shapes=[pltpu.VMEM((count,)+s,F32) for s in shapes]
            +[pltpu.VMEM((n-1,)+s,k) for s,k in zip(shapes,kinds)]
            +[pltpu.VMEM((n-1,)+s,k) for s,k in zip(shapes,kinds)]
            +[pltpu.SemaphoreType.DMA((m,n-1)),pltpu.SemaphoreType.DMA((m,n-1))],
        compiler_params=pltpu.CompilerParams(collective_id=1,has_side_effects=True))(*arrays)

HEADS = 3
HEAD_DIM = 64
FF = 768
DIRS = 4
ROOT_HALF = 1.0 / math.sqrt(2.0)
DENSITY = 1.0 / math.sqrt(2.0 * math.pi)


def geometry(side_row, canvas):
    slots = side_row.shape[0]
    ends = jnp.cumsum(side_row * side_row)
    places = jnp.arange(canvas, dtype=jnp.int32)
    segment = jnp.sum((ends[None, :] <= places[:, None]).astype(jnp.int32), axis=1)
    return segment, segment < slots


def normalize(values):
    centered = values - jnp.mean(values, axis=-1, keepdims=True)
    scale = lax.rsqrt(jnp.mean(centered * centered, axis=-1, keepdims=True) + EPSILON)
    return (centered * scale, scale)


def normalize_back(grad_norm, unit, scale, gain):
    grad_gain = jnp.sum(grad_norm * unit, axis=0)
    scaled = grad_norm * gain
    inner = jnp.mean(scaled * unit, axis=-1, keepdims=True)
    return (scale * (scaled - jnp.mean(scaled, axis=-1, keepdims=True) - unit * inner), grad_gain)


def gelu_value(values):
    return 0.5 * values * (1.0 + lax.erf(values * ROOT_HALF))


def gelu_slope(values):
    return (
        0.5 * (1.0 + lax.erf(values * ROOT_HALF))
        + values * jnp.exp(-0.5 * values * values) * DENSITY
    )


def matmul_first(left, right):
    return lax.dot_general(
        left, right, (((0,), (0,)), ((), ())), preferred_element_type=jnp.float32
    )


def matmul_second(left, right):
    return lax.dot_general(
        left, right, (((1,), (1,)), ((), ())), preferred_element_type=jnp.float32
    )


def rows_of(length, unit):
    return -(-length // (128 * unit)) * unit


def fill_rows(flat, unit):
    rows = rows_of(flat.shape[-1], unit)
    pad = [(0, 0)] * (flat.ndim - 1) + [(0, rows * 128 - flat.shape[-1])]
    return jnp.pad(flat, pad).reshape(flat.shape[:-1] + (rows, 128))


def per_device(
    count,
    tokens,
    cotangent,
    image_sides,
    state_mixing,
    small_params,
    project_in,
    project_out,
    expand_weight,
    shrink_weight,
):
    canvas = tokens.shape[0]
    devices = 2 * count
    segment, live = geometry(image_sides[0], canvas)
    live_col = live.astype(jnp.float32)[:, None]
    scale_attn = 1.0 / math.sqrt(HEAD_DIM)
    parts = (state_mixing, small_params, project_in, project_out, expand_weight, shrink_weight)
    whole = gather(count, fill_rows(jnp.concatenate(parts), 16)).reshape(devices, -1)
    flats = []
    at = 0
    for part in parts:
        flats.append(whole[:, at : at + part.shape[0]].reshape(-1))
        at += part.shape[0]
    mixing_flat, small_flat, in_flat, out_flat, up_flat, down_flat = flats
    states = DIRS * STATES
    small_values = small_flat.astype(jnp.float32)
    gain_one = small_values[2 * states : 2 * states + D]
    gain_two = small_values[2 * states + D :]
    weight_in = in_flat.reshape(D, 3 * D)
    weight_out = out_flat.reshape(D, D)
    weight_up = up_flat.reshape(D, FF)
    weight_down = down_flat.reshape(FF, D)
    mix, rrow, rcol = prep(
        mixing_flat.reshape(DIRS, STATES, D),
        small_values[:states].reshape(DIRS, STATES),
        small_values[states : 2 * states].reshape(DIRS, STATES),
    )
    mixed, squares = ssm_forward(image_sides, tokens, gain_one[None], mix, rrow, rcol)
    inputs = tokens.astype(jnp.float32)
    triple = jnp.dot(mixed, weight_in, preferred_element_type=jnp.float32).astype(jnp.bfloat16)
    triple = triple.reshape(canvas, 3, HEADS, HEAD_DIM)
    queries = triple[:, 0]
    keys_all = triple[:, 1]
    values_all = triple[:, 2]
    attend = segment[:, None] == segment[None, :]
    scores = (
        jnp.einsum("thd,uhd->htu", queries, keys_all, preferred_element_type=jnp.float32)
        * scale_attn
    )
    scores = jnp.where(attend[None], scores, -1e30)
    top = jnp.max(scores, axis=-1, keepdims=True)
    expo = jnp.exp(scores - top)
    total_exp = jnp.sum(expo, axis=-1, keepdims=True)
    log_total = top + jnp.log(total_exp)
    probs = expo / total_exp
    heads_out = (
        jnp.einsum(
            "htu,uhd->thd",
            probs.astype(jnp.bfloat16),
            values_all,
            preferred_element_type=jnp.float32,
        )
        .reshape(canvas, D)
        .astype(jnp.bfloat16)
    )
    after = inputs + live_col * jnp.dot(heads_out, weight_out, preferred_element_type=jnp.float32)
    unit_two, scale_two = normalize(after)
    normed_two = (unit_two * gain_two).astype(jnp.bfloat16)
    hidden_pre = jnp.dot(normed_two, weight_up, preferred_element_type=jnp.float32)
    activation = gelu_value(hidden_pre).astype(jnp.bfloat16)
    result = (
        after + live_col * jnp.dot(activation, weight_down, preferred_element_type=jnp.float32)
    ).astype(jnp.bfloat16)
    incoming = cotangent.astype(jnp.float32)
    grad_mlp = (live_col * incoming).astype(jnp.bfloat16)
    grad_down = matmul_first(activation, grad_mlp)
    grad_hidden = (matmul_second(grad_mlp, weight_down) * gelu_slope(hidden_pre)).astype(
        jnp.bfloat16
    )
    grad_up = matmul_first(normed_two, grad_hidden)
    grad_normed_two = matmul_second(grad_hidden, weight_up)
    grad_after, grad_gain_two = normalize_back(grad_normed_two, unit_two, scale_two, gain_two)
    grad_after = grad_after + incoming
    grad_branch = (live_col * grad_after).astype(jnp.bfloat16)
    grad_out = matmul_first(heads_out, grad_branch)
    grad_heads = (
        matmul_second(grad_branch, weight_out).astype(jnp.bfloat16).reshape(canvas, HEADS, HEAD_DIM)
    )
    again = (
        jnp.einsum("thd,uhd->htu", queries, keys_all, preferred_element_type=jnp.float32)
        * scale_attn
    )
    probs_back = jnp.where(attend[None], jnp.exp(again - log_total), 0.0)
    grad_values = jnp.einsum(
        "htu,thd->uhd",
        probs_back.astype(jnp.bfloat16),
        grad_heads,
        preferred_element_type=jnp.float32,
    )
    grad_probs = jnp.einsum(
        "thd,uhd->htu", grad_heads, values_all, preferred_element_type=jnp.float32
    )
    inner = jnp.sum(grad_probs * probs_back, axis=-1, keepdims=True)
    grad_scores = (probs_back * (grad_probs - inner)).astype(jnp.bfloat16)
    grad_queries = (
        jnp.einsum("htu,uhd->thd", grad_scores, keys_all, preferred_element_type=jnp.float32)
        * scale_attn
    )
    grad_keys = (
        jnp.einsum("htu,thd->uhd", grad_scores, queries, preferred_element_type=jnp.float32)
        * scale_attn
    )
    grad_triple = (
        jnp.stack([grad_queries, grad_keys, grad_values], axis=1)
        .reshape(canvas, 3 * D)
        .astype(jnp.bfloat16)
    )
    grad_in = matmul_first(mixed, grad_triple)
    grad_ssm = matmul_second(grad_triple, weight_in)
    grad_tokens, gmix, grow, gcol, grad_gain_one = ssm_backward(
        image_sides, tokens, gain_one[None], grad_ssm, grad_after, mix, rrow, rcol
    )
    grad_mixing = gmix.reshape(2, STATES, 2, D).transpose(0, 2, 1, 3).reshape(devices, -1)
    grad_small = jnp.concatenate(
        [
            grow.transpose(0, 2, 1).reshape(-1),
            gcol.transpose(0, 2, 1).reshape(-1),
            grad_gain_one[0],
            grad_gain_two,
        ]
    ).reshape(devices, -1)
    large = jnp.concatenate(
        [g.reshape(devices, -1) for g in (grad_in, grad_out, grad_up, grad_down)], axis=1
    )
    small = jnp.concatenate(
        [grad_mixing, grad_small, jnp.broadcast_to(squares[:, 0][None], (devices, DIRS))], axis=1
    )
    large_sum, small_sum = scatter(
        count, [fill_rows(large, 16), fill_rows(small, 8)], [jnp.bfloat16, jnp.float32]
    )
    large_sum = large_sum.reshape(-1)
    small_sum = small_sum.reshape(-1)
    outs = []
    at = 0
    for part in (state_mixing, small_params):
        outs.append(small_sum[at : at + part.shape[0]])
        at += part.shape[0]
    totals = small_sum[at : at + DIRS]
    penalty = jnp.sum(jnp.sqrt(totals / (canvas * devices * D) + 1e-06))
    at = 0
    for part in parts[2:]:
        outs.append(large_sum[at : at + part.shape[0]])
        at += part.shape[0]
    return (result, grad_tokens, penalty, *outs)


def solution(mesh):
    both = P(("dp", "head"))
    return jax.shard_map(
        functools.partial(per_device, mesh.shape["dp"]),
        mesh=mesh,
        in_specs=(P(("dp", "head"), None),) * 3 + (both,) * 6,
        out_specs=(P(("dp", "head"), None),) * 2 + (P(),) + (both,) * 6,
        check_vma=False,
    )
```

```python
import functools
import math

import jax
import jax.numpy as jnp
from jax import lax
from jax.experimental import pallas as pl
from jax.experimental.pallas import tpu as pltpu
from jax.sharding import PartitionSpec as P

D=192; STATES=16; D2=2*D; SMAX=18; SLOTS=10
EPSILON=1e-5
F32=jnp.float32; BF=jnp.bfloat16
UNROLL={10:10,14:14,18:18}
PADC={10:16,14:16,18:24}

def col_matrix(rate_lane, swap):
    width=rate_lane.shape[1]
    rows=lax.broadcasted_iota(jnp.int32,(48,width),0)
    first=rows<24
    c=jnp.where(first,rows,rows-24)
    u=lax.broadcasted_iota(jnp.int32,(48,width),1)//16
    gap=(c-u) if not swap else (u-c)
    sign=jnp.where(first,1,-1)
    rate=jnp.where(first,rate_lane[0:1],rate_lane[1:2])
    far=jnp.abs(gap).astype(F32)
    value=jnp.exp(-rate*far)
    return jnp.where(sign*gap>=0,value,0.0), far

def norm_rows(t):
    x=t.astype(F32)
    cen=x-jnp.mean(x,axis=-1,keepdims=True)
    sc=lax.rsqrt(jnp.mean(cen*cen,axis=-1,keepdims=True)+EPSILON)
    return cen*sc, sc

def lane_pair(two):
    lane=lax.broadcasted_iota(jnp.int32,(16,D2),1)
    return jnp.where(lane<D,two[:,0:1],two[:,1:2])

def fwd_body(sides, tok, gain, mix, rrow, rcol, mixed, squares, xx, ssm, sq, ypad, w, cm):
    canvas=tok.shape[0]
    unit,_=norm_rows(tok[...])
    normed=(unit*gain[...]).astype(BF).astype(F32)
    xx[:,0:D]=normed
    xx[:,D:D2]=normed
    ssm[...]=jnp.zeros_like(ssm)
    sq[...]=jnp.zeros_like(sq)
    for p in range(2):
        cm[p]=col_matrix(rcol[p],False)[0].astype(BF)
    def image(s,start):
        sp=PADC[s]; depth=s*16
        for p in range(2):
            m=mix[p].astype(F32); a=lane_pair(jnp.exp(-rrow[p]))
            def scan(j,_):
                for h in range(2):
                    c=2*j+h
                    state=None
                    for step in range(s):
                        r=step if p==0 else s-1-step
                        x=xx[pl.ds(start+r*s+c,1),:]
                        term=m*x
                        state=term if state is None else state*a+term
                        w[r,pl.ds(pl.multiple_of(c*16,16),16),:]=state.astype(BF)
                return 0
            lax.fori_loop(0,s//2,scan,0)
            left=cm[p]
            if s!=18:
                left=jnp.concatenate([left[0:16,0:depth],left[24:40,0:depth]],axis=0)
            def rows(j,_):
                for h in range(UNROLL[s]):
                    r=UNROLL[s]*j+h
                    out=jnp.dot(left,w[r,0:depth,:],preferred_element_type=F32)
                    y0=out[0:s,0:D]
                    y1=out[sp:sp+s,D:D2]
                    sq[2*p,0:s]+=y0*y0
                    sq[2*p+1,0:s]+=y1*y1
                    if p==0: ypad[r,0:s]=y0+y1
                    else: ypad[r,0:s]+=y0+y1
                return 0
            lax.fori_loop(0,s//UNROLL[s],rows,0)
        def place(r,_):
            for c in range(s):
                ssm[pl.ds(start+r*s+c,1),:]=ypad[r,pl.ds(c,1),:]
            return 0
        lax.fori_loop(0,s,place,0)
    def each(k,start):
        side=sides[0,k]
        for s in (10,14,18):
            @pl.when(side==s)
            def _(): image(s,start)
        return start+side*side
    lax.fori_loop(0,SLOTS,each,0)
    mixed[...]=ssm[0:canvas,:].astype(BF)
    squares[...]=jnp.sum(jnp.sum(sq[...],axis=2),axis=1,keepdims=True)

def ssm_forward(sides, tok, gain, mix, rrow, rcol):
    canvas=tok.shape[0]
    vm=pl.BlockSpec(memory_space=pltpu.VMEM)
    return pl.pallas_call(fwd_body,
        out_shape=(jax.ShapeDtypeStruct((canvas,D),BF),jax.ShapeDtypeStruct((4,1),F32)),
        in_specs=[pl.BlockSpec(memory_space=pltpu.SMEM)]+[vm]*5, out_specs=(vm,vm),
        scratch_shapes=[pltpu.VMEM((canvas,D2),F32),pltpu.VMEM((canvas+24,D),F32),pltpu.VMEM((4,24,D),F32),pltpu.VMEM((SMAX,24,D),F32),
            pltpu.VMEM((SMAX,SMAX*16,D2),BF),pltpu.VMEM((2,48,SMAX*16),BF)],
        compiler_params=pltpu.CompilerParams(vmem_limit_bytes=50<<20))(sides,tok,gain,mix,rrow,rcol)

def prep(mixing, rate_row, rate_col):
    mix=mixing.reshape(2,2,16,D).transpose(0,2,1,3).reshape(2,16,D2)
    rrow=rate_row.astype(F32).reshape(2,2,16).transpose(0,2,1)
    rcol=jnp.tile(rate_col.astype(F32).reshape(2,2,1,16),(1,1,SMAX,1)).reshape(2,2,SMAX*16)
    return mix,rrow,rcol

def bwd_body(sides, tok, gain, gssm, gafter, mix, rrow, rcol, gtok, gmix, grow, gcol, ggain,
             xx, gg, canvas_out, ypad, bd, xi, xd, mb, c2, ct, cd, acc):
    canvas=tok.shape[0]
    unit,scale=norm_rows(tok[...])
    g=gssm[...]
    gg[0]=g[:,0:128]
    gg[1]=jnp.concatenate([g[:,128:D],g[:,0:64]],axis=1)
    gg[2]=g[:,64:D]
    normed=(unit*gain[...]).astype(BF).astype(F32)
    xx[:,0:D]=normed
    xx[:,D:D2]=normed
    low_lane=lax.broadcasted_iota(jnp.int32,(24,D2),1)<D
    bd[...]=jnp.zeros_like(bd)
    acc[...]=jnp.zeros_like(acc)
    for p in range(2):
        value,far=col_matrix(rcol[p],True)
        c2[p]=value.astype(BF)
        ct[p]=value.T
        cd[p]=(value*far).T
    def image(s,start):
        sp=PADC[s]; depth=s*16
        lane=lax.broadcasted_iota(jnp.int32,(depth,48),1)
        keep=jnp.where(lane<24,lane,lane-24)<s
        def gather(r,_):
            for c in range(s):
                bd[r,pl.ds(c,1),:]=xx[pl.ds(start+r*s+c,1),:]
            return 0
        lax.fori_loop(0,s,gather,0)
        for p in range(2):
            left=jnp.where(keep,ct[p,0:depth],0.0).astype(BF)
            leftd=jnp.where(keep,cd[p,0:depth],0.0).astype(BF)
            def spread(j,_):
                for h in range(UNROLL[s]):
                    r=UNROLL[s]*j+h
                    b=bd[r]
                    b=jnp.concatenate([jnp.where(low_lane,b,0.0),jnp.where(low_lane,0.0,b)],axis=0).astype(BF)
                    xi[r,0:depth]=jnp.dot(left,b,preferred_element_type=F32)
                    xd[r,0:depth]=jnp.dot(leftd,b,preferred_element_type=F32)
                return 0
            lax.fori_loop(0,s//UNROLL[s],spread,0)
            for q in range(3):
                ch=slice(q*128,(q+1)*128)
                m=mix[p,:,ch].astype(F32); a=lane_pair(jnp.exp(-rrow[p]))[:,ch]
                def scan(j,sums):
                    s1,s2,s3=sums
                    for h in range(2):
                        c=2*j+h
                        at=pl.ds(pl.multiple_of(c*16,16),16)
                        mu=None
                        for step in range(s):
                            r=s-1-step if p==0 else step
                            gr=gg[q,pl.ds(start+r*s+c,1),:]
                            e=xi[r,at,ch]
                            if mu is None:
                                mu=jnp.broadcast_to(gr,(16,128))
                            else:
                                low=mu*a
                                nu=low if nu is None else nu*a+low
                                mu=gr+low
                                s2=s2+nu*e
                            if step==0: nu=None
                            s1=s1+mu*e
                            s3=s3+mu*xd[r,at,ch]
                            mb[r,at,ch]=(m*mu).astype(BF)
                    return s1,s2,s3
                sums=lax.fori_loop(0,s//2,scan,(acc[p,0,:,ch],acc[p,1,:,ch],acc[p,2,:,ch]))
                for i in range(3): acc[p,i,:,ch]=sums[i]
            left2=c2[p]
            if s!=18:
                left2=jnp.concatenate([left2[0:16,0:depth],left2[24:40,0:depth]],axis=0)
            def rows(j,_):
                for h in range(UNROLL[s]):
                    r=UNROLL[s]*j+h
                    out=jnp.dot(left2,mb[r,0:depth,:],preferred_element_type=F32)
                    y=out[0:s,0:D]+out[sp:sp+s,D:D2]
                    if p==0: ypad[r,0:s]=y
                    else: ypad[r,0:s]+=y
                return 0
            lax.fori_loop(0,s//UNROLL[s],rows,0)
        def place(r,_):
            for c in range(s):
                canvas_out[pl.ds(start+r*s+c,1),:]=ypad[r,pl.ds(c,1),:]
            return 0
        lax.fori_loop(0,s,place,0)
    def each(k,start):
        side=sides[0,k]
        for s in (10,14,18):
            @pl.when(side==s)
            def _(): image(s,start)
        return start+side*side
    end=lax.fori_loop(0,SLOTS,each,0)
    slot=lax.broadcasted_iota(jnp.int32,(canvas,1),0)
    gn=jnp.where(slot<end,canvas_out[0:canvas],0.0)
    ggain[...]=jnp.sum(gn*unit,axis=0,keepdims=True)
    scaled=gn*gain[...]
    inner=jnp.mean(scaled*unit,axis=-1,keepdims=True)
    gtok[...]=gafter[...]+scale*(scaled-jnp.mean(scaled,axis=-1,keepdims=True)-unit*inner)
    for p in range(2):
        m=mix[p].astype(F32)
        gmix[p]=acc[p,0]
        r2=m*acc[p,1]; r3=m*acc[p,2]
        for d in range(2):
            ch=slice(d*D,(d+1)*D)
            grow[p,:,d:d+1]=-jnp.sum(r2[:,ch],axis=1,keepdims=True)
            gcol[p,:,d:d+1]=-jnp.sum(r3[:,ch],axis=1,keepdims=True)

def ssm_backward(sides, tok, gain, gssm, gafter, mix, rrow, rcol):
    canvas=tok.shape[0]
    vm=pl.BlockSpec(memory_space=pltpu.VMEM)
    V=pltpu.VMEM
    sh=jax.ShapeDtypeStruct
    return pl.pallas_call(bwd_body,
        out_shape=(sh((canvas,D),F32),sh((2,16,D2),F32),sh((2,16,2),F32),sh((2,16,2),F32),sh((1,D),F32)),
        in_specs=[pl.BlockSpec(memory_space=pltpu.SMEM)]+[vm]*7, out_specs=(vm,)*5,
        scratch_shapes=[V((canvas,D2),F32),V((3,canvas,128),F32),V((canvas+24,D),F32),V((SMAX,24,D),F32),V((SMAX,24,D2),F32),
            V((SMAX,SMAX*16,D2),F32),V((SMAX,SMAX*16,D2),F32),V((SMAX,SMAX*16,D2),BF),
            V((2,48,SMAX*16),BF),V((2,SMAX*16,48),F32),V((2,SMAX*16,48),F32),V((2,3,16,D2),F32)],
        compiler_params=pltpu.CompilerParams(vmem_limit_bytes=56<<20))(sides,tok,gain,gssm,gafter,mix,rrow,rcol)

F32=jnp.float32; BF=jnp.bfloat16
AXES=("dp","head")

def digits(count):
    out=[]; weight=1
    while weight<count:
        radix=4 if weight*4<=count else 2
        out.append((weight,radix)); weight*=radix
    return out[::-1]

def greet(dp, head, offsets):
    barrier=pltpu.get_barrier_semaphore()
    peers=[(dp^off,head) for off in offsets]+[(dp,1-head)]
    for peer in peers:
        pl.semaphore_signal(barrier,inc=1,device_id=peer,device_id_type=pl.DeviceIdType.MESH)
    pl.semaphore_wait(barrier,len(peers))

def gather_body(count, x, buf, send, recv):
    dp=lax.axis_index("dp"); head=lax.axis_index("head")
    stages=digits(count)
    greet(dp,head,[w*k for w,r in stages for k in range(1,r)])
    mine=dp*2+head
    buf[pl.ds(mine,1)]=x[...][None]
    started=[]
    def push(off,off_to,h_to):
        block=buf.at[(dp^off)*2+head]
        n=len(started)
        peer=(dp,1-head) if h_to else (dp^off^off_to,head)
        copy=pltpu.make_async_remote_copy(src_ref=block,dst_ref=block,send_sem=send.at[n],
            recv_sem=recv.at[off_to+count*h_to],device_id=peer,device_id_type=pl.DeviceIdType.MESH)
        copy.start(); started.append(copy)
    def arrived(off,h):
        block=buf.at[(dp^off)*2+(1-head if h else head)]
        pltpu.make_async_remote_copy(src_ref=block,dst_ref=block,send_sem=send.at[0],
            recv_sem=recv.at[off+count*h],device_id=(dp,1-head),device_id_type=pl.DeviceIdType.MESH).wait_recv()
    held=[(0,0)]
    at=0
    while at<len(held):
        off,stage=held[at]; at+=1
        if off: arrived(off,0)
        for t in range(stage,len(stages)):
            w,r=stages[t]
            for k in range(1,r): push(off,off^(w*k),0)
        push(off,off,1)
        if off==0:
            order=[]
        for t in range(stage,len(stages)):
            w,r=stages[t]
            for k in range(1,r): held.append((off^(w*k),t+1))
    for off in range(count): arrived(off,1)
    for copy in started: copy.wait_send()

def gather(count, x):
    n=2*count
    return pl.pallas_call(functools.partial(gather_body,count),
        out_shape=jax.ShapeDtypeStruct((n,)+x.shape,x.dtype),
        in_specs=[pl.BlockSpec(memory_space=pltpu.VMEM)],out_specs=pl.BlockSpec(memory_space=pltpu.VMEM),
        scratch_shapes=[pltpu.SemaphoreType.DMA((n-1,)),pltpu.SemaphoreType.DMA((n,))],
        compiler_params=pltpu.CompilerParams(collective_id=0,has_side_effects=True))(x)

def scatter_body(count, kinds, *refs):
    m=len(kinds)
    xs=refs[0:m]; outs=refs[m:2*m]; accs=refs[2*m:3*m]; sends=refs[3*m:4*m]; lands=refs[4*m:5*m]
    send,recv=refs[5*m:]
    dp=lax.axis_index("dp"); head=lax.axis_index("head")
    stages=digits(count)[::-1]
    greet(dp,head,[w*k for w,r in stages for k in range(1,r)])
    started=[]
    slots={}
    for off in range(count): slots[(-1,off)]=len(slots)
    for t,(w,r) in enumerate(stages):
        for k in range(1,r):
            for high in range(0,count,w*r): slots[(t,k*w+high)]=len(slots)
    def push(t,off,peer,values):
        n=slots[(t,off)]
        for i in range(m):
            sends[i][n]=values[i].astype(kinds[i])
            copy=pltpu.make_async_remote_copy(src_ref=sends[i].at[n],dst_ref=lands[i].at[n],send_sem=send.at[i,n],
                recv_sem=recv.at[i,n],device_id=peer,device_id_type=pl.DeviceIdType.MESH)
            copy.start(); started.append(copy)
    def take(t,off):
        n=slots[(t,off)]
        out=[]
        for i in range(m):
            pltpu.make_async_remote_copy(src_ref=sends[i].at[n],dst_ref=lands[i].at[n],send_sem=send.at[i,n],
                recv_sem=recv.at[i,n],device_id=(dp,1-head),device_id_type=pl.DeviceIdType.MESH).wait_recv()
            out.append(lands[i][n].astype(F32))
        return out
    level={}
    def settle(off,t):
        if off not in level:
            got=take(-1,off)
            for i in range(m): accs[i][off]=xs[i][(dp^off)*2+head]+got[i]
            level[off]=0
        while level[off]<t:
            w,r=stages[level[off]]
            total=[accs[i][off] for i in range(m)]
            for k in range(1,r):
                got=take(level[off],off^(k*w))
                total=[a+b for a,b in zip(total,got)]
            for i in range(m): accs[i][off]=total[i]
            level[off]+=1
    def rank(off):
        return tuple(0 if (off//w)%r else 1 for w,r in stages)
    for off in sorted(range(count),key=rank):
        push(-1,off,(dp,1-head),[xs[i][(dp^off)*2+1-head] for i in range(m)])
    for t,(w,r) in enumerate(stages):
        for k in range(1,r):
            for high in range(0,count,w*r):
                off=k*w+high
                settle(off,t)
                push(t,off,(dp^(k*w),head),[accs[i][off] for i in range(m)])
    settle(0,len(stages))
    for i in range(m): outs[i][...]=accs[i][0]
    for copy in started: copy.wait_send()

def scatter(count, arrays, kinds):
    n=2*count; m=len(arrays)
    vm=pl.BlockSpec(memory_space=pltpu.VMEM)
    shapes=[a.shape[1:] for a in arrays]
    return pl.pallas_call(functools.partial(scatter_body,count,kinds),
        out_shape=tuple(jax.ShapeDtypeStruct(s,F32) for s in shapes),
        in_specs=[vm]*m,out_specs=(vm,)*m,
        scratch_shapes=[pltpu.VMEM((count,)+s,F32) for s in shapes]
            +[pltpu.VMEM((n-1,)+s,k) for s,k in zip(shapes,kinds)]
            +[pltpu.VMEM((n-1,)+s,k) for s,k in zip(shapes,kinds)]
            +[pltpu.SemaphoreType.DMA((m,n-1)),pltpu.SemaphoreType.DMA((m,n-1))],
        compiler_params=pltpu.CompilerParams(collective_id=1,has_side_effects=True))(*arrays)

HEADS = 3
HEAD_DIM = 64
FF = 768
DIRS = 4
ROOT_HALF = 1.0 / math.sqrt(2.0)
DENSITY = 1.0 / math.sqrt(2.0 * math.pi)


def geometry(side_row, canvas):
    slots = side_row.shape[0]
    ends = jnp.cumsum(side_row * side_row)
    places = jnp.arange(canvas, dtype=jnp.int32)
    segment = jnp.sum((ends[None, :] <= places[:, None]).astype(jnp.int32), axis=1)
    return segment, segment < slots


def normalize(values):
    centered = values - jnp.mean(values, axis=-1, keepdims=True)
    scale = lax.rsqrt(jnp.mean(centered * centered, axis=-1, keepdims=True) + EPSILON)
    return (centered * scale, scale)


def normalize_back(grad_norm, unit, scale, gain):
    grad_gain = jnp.sum(grad_norm * unit, axis=0)
    scaled = grad_norm * gain
    inner = jnp.mean(scaled * unit, axis=-1, keepdims=True)
    return (scale * (scaled - jnp.mean(scaled, axis=-1, keepdims=True) - unit * inner), grad_gain)


def gelu_value(values):
    return 0.5 * values * (1.0 + lax.erf(values * ROOT_HALF))


def gelu_slope(values):
    return (
        0.5 * (1.0 + lax.erf(values * ROOT_HALF))
        + values * jnp.exp(-0.5 * values * values) * DENSITY
    )


def matmul_first(left, right):
    return lax.dot_general(
        left, right, (((0,), (0,)), ((), ())), preferred_element_type=jnp.float32
    )


def matmul_second(left, right):
    return lax.dot_general(
        left, right, (((1,), (1,)), ((), ())), preferred_element_type=jnp.float32
    )


def rows_of(length, unit):
    return -(-length // (128 * unit)) * unit


def fill_rows(flat, unit):
    rows = rows_of(flat.shape[-1], unit)
    pad = [(0, 0)] * (flat.ndim - 1) + [(0, rows * 128 - flat.shape[-1])]
    return jnp.pad(flat, pad).reshape(flat.shape[:-1] + (rows, 128))


def per_device(
    count,
    tokens,
    cotangent,
    image_sides,
    state_mixing,
    small_params,
    project_in,
    project_out,
    expand_weight,
    shrink_weight,
):
    canvas = tokens.shape[0]
    devices = 2 * count
    segment, live = geometry(image_sides[0], canvas)
    live_col = live.astype(jnp.float32)[:, None]
    scale_attn = 1.0 / math.sqrt(HEAD_DIM)
    parts = (state_mixing, small_params, project_in, project_out, expand_weight, shrink_weight)
    whole = gather(count, fill_rows(jnp.concatenate(parts), 16)).reshape(devices, -1)
    flats = []
    at = 0
    for part in parts:
        flats.append(whole[:, at : at + part.shape[0]].reshape(-1))
        at += part.shape[0]
    mixing_flat, small_flat, in_flat, out_flat, up_flat, down_flat = flats
    states = DIRS * STATES
    small_values = small_flat.astype(jnp.float32)
    gain_one = small_values[2 * states : 2 * states + D]
    gain_two = small_values[2 * states + D :]
    weight_in = in_flat.reshape(D, 3 * D)
    weight_out = out_flat.reshape(D, D)
    weight_up = up_flat.reshape(D, FF)
    weight_down = down_flat.reshape(FF, D)
    mix, rrow, rcol = prep(
        mixing_flat.reshape(DIRS, STATES, D),
        small_values[:states].reshape(DIRS, STATES),
        small_values[states : 2 * states].reshape(DIRS, STATES),
    )
    mixed, squares = ssm_forward(image_sides, tokens, gain_one[None], mix, rrow, rcol)
    inputs = tokens.astype(jnp.float32)
    triple = jnp.dot(mixed, weight_in, preferred_element_type=jnp.float32).astype(jnp.bfloat16)
    triple = triple.reshape(canvas, 3, HEADS, HEAD_DIM)
    queries = triple[:, 0]
    keys_all = triple[:, 1]
    values_all = triple[:, 2]
    attend = segment[:, None] == segment[None, :]
    scores = (
        jnp.einsum("thd,uhd->htu", queries, keys_all, preferred_element_type=jnp.float32)
        * scale_attn
    )
    scores = jnp.where(attend[None], scores, -1e30)
    top = jnp.max(scores, axis=-1, keepdims=True)
    expo = jnp.exp(scores - top)
    total_exp = jnp.sum(expo, axis=-1, keepdims=True)
    log_total = top + jnp.log(total_exp)
    probs = expo / total_exp
    heads_out = (
        jnp.einsum(
            "htu,uhd->thd",
            probs.astype(jnp.bfloat16),
            values_all,
            preferred_element_type=jnp.float32,
        )
        .reshape(canvas, D)
        .astype(jnp.bfloat16)
    )
    after = inputs + live_col * jnp.dot(heads_out, weight_out, preferred_element_type=jnp.float32)
    unit_two, scale_two = normalize(after)
    normed_two = (unit_two * gain_two).astype(jnp.bfloat16)
    hidden_pre = jnp.dot(normed_two, weight_up, preferred_element_type=jnp.float32)
    activation = gelu_value(hidden_pre).astype(jnp.bfloat16)
    result = (
        after + live_col * jnp.dot(activation, weight_down, preferred_element_type=jnp.float32)
    ).astype(jnp.bfloat16)
    incoming = cotangent.astype(jnp.float32)
    grad_mlp = (live_col * incoming).astype(jnp.bfloat16)
    grad_down = matmul_first(activation, grad_mlp)
    grad_hidden = (matmul_second(grad_mlp, weight_down) * gelu_slope(hidden_pre)).astype(
        jnp.bfloat16
    )
    grad_up = matmul_first(normed_two, grad_hidden)
    grad_normed_two = matmul_second(grad_hidden, weight_up)
    grad_after, grad_gain_two = normalize_back(grad_normed_two, unit_two, scale_two, gain_two)
    grad_after = grad_after + incoming
    grad_branch = (live_col * grad_after).astype(jnp.bfloat16)
    grad_out = matmul_first(heads_out, grad_branch)
    grad_heads = (
        matmul_second(grad_branch, weight_out).astype(jnp.bfloat16).reshape(canvas, HEADS, HEAD_DIM)
    )
    again = (
        jnp.einsum("thd,uhd->htu", queries, keys_all, preferred_element_type=jnp.float32)
        * scale_attn
    )
    probs_back = jnp.where(attend[None], jnp.exp(again - log_total), 0.0)
    grad_values = jnp.einsum(
        "htu,thd->uhd",
        probs_back.astype(jnp.bfloat16),
        grad_heads,
        preferred_element_type=jnp.float32,
    )
    grad_probs = jnp.einsum(
        "thd,uhd->htu", grad_heads, values_all, preferred_element_type=jnp.float32
    )
    inner = jnp.sum(grad_probs * probs_back, axis=-1, keepdims=True)
    grad_scores = (probs_back * (grad_probs - inner)).astype(jnp.bfloat16)
    grad_queries = (
        jnp.einsum("htu,uhd->thd", grad_scores, keys_all, preferred_element_type=jnp.float32)
        * scale_attn
    )
    grad_keys = (
        jnp.einsum("htu,thd->uhd", grad_scores, queries, preferred_element_type=jnp.float32)
        * scale_attn
    )
    grad_triple = (
        jnp.stack([grad_queries, grad_keys, grad_values], axis=1)
        .reshape(canvas, 3 * D)
        .astype(jnp.bfloat16)
    )
    grad_in = matmul_first(mixed, grad_triple)
    grad_ssm = matmul_second(grad_triple, weight_in)
    grad_tokens, gmix, grow, gcol, grad_gain_one = ssm_backward(
        image_sides, tokens, gain_one[None], grad_ssm, grad_after, mix, rrow, rcol
    )
    grad_mixing = gmix.reshape(2, STATES, 2, D).transpose(0, 2, 1, 3).reshape(devices, -1)
    grad_small = jnp.concatenate(
        [
            grow.transpose(0, 2, 1).reshape(-1),
            gcol.transpose(0, 2, 1).reshape(-1),
            grad_gain_one[0],
            grad_gain_two,
        ]
    ).reshape(devices, -1)
    large = jnp.concatenate(
        [g.reshape(devices, -1) for g in (grad_in, grad_out, grad_up, grad_down)], axis=1
    )
    small = jnp.concatenate(
        [grad_mixing, grad_small, jnp.broadcast_to(squares[:, 0][None], (devices, DIRS))], axis=1
    )
    large_sum, small_sum = scatter(
        count, [fill_rows(large, 16), fill_rows(small, 8)], [jnp.bfloat16, jnp.float32]
    )
    large_sum = large_sum.reshape(-1)
    small_sum = small_sum.reshape(-1)
    outs = []
    at = 0
    for part in (state_mixing, small_params):
        outs.append(small_sum[at : at + part.shape[0]])
        at += part.shape[0]
    totals = small_sum[at : at + DIRS]
    penalty = jnp.sum(jnp.sqrt(totals / (canvas * devices * D) + 1e-06))
    at = 0
    for part in parts[2:]:
        outs.append(large_sum[at : at + part.shape[0]])
        at += part.shape[0]
    return (result, grad_tokens, penalty, *outs)


def solution(mesh):
    both = P(("dp", "head"))
    return jax.shard_map(
        functools.partial(per_device, mesh.shape["dp"]),
        mesh=mesh,
        in_specs=(P(("dp", "head"), None),) * 3 + (both,) * 6,
        out_specs=(P(("dp", "head"), None),) * 2 + (P(),) + (both,) * 6,
        check_vma=False,
    )
```

```python
import functools
import math

import jax
import jax.numpy as jnp
from jax import lax
from jax.experimental import pallas as pl
from jax.experimental.pallas import tpu as pltpu
from jax.sharding import PartitionSpec as P

D = 192
D2 = 2 * D
DIRS = 4
STATES = 16
HEADS = 3
HEAD_DIM = 64
FF = 768
SLOTS = 10
SMAX = 18
EPSILON = 1e-05
ROOT_HALF = 1.0 / math.sqrt(2.0)
DENSITY = 1.0 / math.sqrt(2.0 * math.pi)
F32 = jnp.float32
BF = jnp.bfloat16
PAD_ROWS = {10: 16, 14: 16, 18: 24}
WINDOW = {10: 128, 14: 256, 18: 384}
SPARE = 64
TILE = 256
PROB_ROWS = 4096


def contract_second(left, right):
    return lax.dot_general(left, right, (((1,), (1,)), ((), ())), preferred_element_type=F32)


def product(left, right):
    return jnp.dot(left, right, preferred_element_type=F32)


def iota(shape, axis):
    return lax.broadcasted_iota(jnp.int32, shape, axis)


def open_flat(flat, n, width, lanes):
    chunks = -(-width // 128)
    if width % 128 == 0:
        return jnp.concatenate(
            [flat[pl.ds(j, n, stride=chunks), :] for j in range(chunks)], axis=1
        )
    step = width // 64
    half = step // 2
    piece = [flat[pl.ds(j, n // 2, stride=step), :] for j in range(step)]
    piece.append(piece[-1])
    for c in range(chunks):
        lanes[c, pl.ds(0, n // 2, stride=2), :] = piece[c]
        lanes[c, pl.ds(1, n // 2, stride=2), :] = jnp.concatenate(
            [piece[half + c][:, 64:], piece[half + c + 1][:, :64]], axis=1
        )
    return jnp.concatenate([lanes[c, 0:n, :] for c in range(chunks)], axis=1)[:, 0:width]


def close_flat(flat, matrix, lanes):
    n, width = matrix.shape
    chunks = -(-width // 128)
    if width % 128 == 0:
        for j in range(chunks):
            flat[pl.ds(j, n, stride=chunks), :] = matrix[:, 128 * j : 128 * j + 128]
        return
    step = width // 64
    half = step // 2
    for c in range(chunks):
        part = matrix[:, 128 * c : min(width, 128 * c + 128)]
        lanes[c, 0:n, 0 : part.shape[1]] = part
    even = [lanes[c, pl.ds(0, n // 2, stride=2), :] for c in range(chunks)]
    odd = [lanes[c, pl.ds(1, n // 2, stride=2), :] for c in range(chunks)]
    piece = even[:half] + [jnp.concatenate([even[half][:, :64], odd[0][:, :64]], axis=1)]
    piece += [jnp.concatenate([odd[c][:, 64:], odd[c + 1][:, :64]], axis=1) for c in range(half)]
    for j in range(step):
        flat[pl.ds(j, n // 2, stride=step), :] = piece[j]


def as_column(row):
    return jnp.broadcast_to(row, (8, row.shape[1])).T[:, 0:1]


def as_row(column):
    return jnp.broadcast_to(column, (column.shape[0], 128)).T[0:1, :]


def state_column(row, at):
    hit = iota((STATES, 128), 1) == at + iota((STATES, 128), 0)
    return jnp.sum(jnp.where(hit, row, 0.0), axis=1, keepdims=True)


def state_row(column, at):
    hit = iota((STATES, 128), 1) == at + iota((STATES, 128), 0)
    return jnp.sum(jnp.where(hit, column, 0.0), axis=0, keepdims=True)


def pair_lanes(first, second):
    return jnp.where(iota((STATES, D2), 1) < D, first, second)


def column_decay(rates, swap):
    width = SMAX * STATES
    shape = (48, width)
    state = iota((STATES, width), 1) % STATES == iota((STATES, width), 0)
    spread = [jnp.sum(jnp.where(state, r, 0.0), axis=0, keepdims=True) for r in rates]
    rows = iota(shape, 0)
    first = rows < 24
    here = jnp.where(first, rows, rows - 24)
    there = iota(shape, 1) // STATES
    gap = there - here if swap else here - there
    far = jnp.abs(gap).astype(F32)
    value = jnp.exp(-jnp.where(first, spread[0], spread[1]) * far)
    return jnp.where(jnp.where(first, 1, -1) * gap >= 0, value, 0.0), far


def normalize(values):
    centered = values - jnp.mean(values, axis=0, keepdims=True)
    scale = lax.rsqrt(jnp.mean(centered * centered, axis=0, keepdims=True) + EPSILON)
    return centered * scale, scale


def normalize_back(grad, unit, scale, gain):
    scaled = grad * gain
    inner = jnp.mean(scaled * unit, axis=0, keepdims=True)
    return scale * (scaled - jnp.mean(scaled, axis=0, keepdims=True) - unit * inner)


def for_images(sides, body):
    def each(k, carry):
        start, row = carry
        side = sides[0, k]
        for s in (10, 14, 18):

            @pl.when(side == s)
            def _():
                body(s, start, row)

        used = jnp.where(side == 10, 128, jnp.where(side == 14, 256, 384)) * HEADS
        return start + side * side, row + jnp.where(side > 0, used, 0)

    return lax.fori_loop(0, SLOTS, each, (0, 0))[0]


def trim(matrix, s):
    if s == SMAX:
        return matrix
    depth = s * STATES
    return jnp.concatenate([matrix[0:16, 0:depth], matrix[24:40, 0:depth]], axis=0)


def state_forward(s, start, xx, mix, alpha, cols, work, ypad, sums, canvas):
    rows = PAD_ROWS[s]
    for p in range(2):
        m = mix[p]
        a = alpha[p]

        def scan(j, _):
            for h in range(2):
                c = 2 * j + h
                state = None
                for step in range(s):
                    r = step if p == 0 else s - 1 - step
                    term = m * xx[pl.ds(start + r * s + c, 1), :]
                    state = term if state is None else state * a + term
                    work[r, pl.ds(pl.multiple_of(c * STATES, STATES), STATES), :] = state.astype(BF)
            return 0

        lax.fori_loop(0, s // 2, scan, 0)
        left = trim(cols[p], s)
        for r in range(s):
            out = product(left, work[r, 0 : s * STATES, :])
            one = out[0:s, 0:D]
            two = out[rows : rows + s, D:D2]
            sums[2 * p, 0:s] += one * one
            sums[2 * p + 1, 0:s] += two * two
            if p == 0:
                ypad[r, 0:s] = one + two
            else:
                ypad[r, 0:s] += one + two
    place_rows(s, start, ypad, canvas)


def place_rows(s, start, ypad, canvas):
    def place(r, _):
        for c in range(s):
            canvas[pl.ds(start + r * s + c, 1), :] = ypad[r, pl.ds(c, 1), :]
        return 0

    lax.fori_loop(0, s, place, 0)


def state_backward(
    s, start, xx, gg, mix, alpha, back, fan, fan_far, blocks, xi, xd, work, ypad, acc, canvas
):
    rows = PAD_ROWS[s]
    depth = s * STATES
    lane = iota((depth, 48), 1)
    keep = jnp.where(lane < 24, lane, lane - 24) < s
    low = iota((24, D2), 1) < D

    def gather_rows(r, _):
        for c in range(s):
            blocks[r, pl.ds(c, 1), :] = xx[pl.ds(start + r * s + c, 1), :]
        return 0

    lax.fori_loop(0, s, gather_rows, 0)
    for p in range(2):
        left = jnp.where(keep, fan[p, 0:depth], 0.0).astype(BF)
        left_far = jnp.where(keep, fan_far[p, 0:depth], 0.0).astype(BF)
        for r in range(s):
            b = blocks[r]
            b = jnp.concatenate([jnp.where(low, b, 0.0), jnp.where(low, 0.0, b)], axis=0)
            b = b.astype(BF)
            xi[r, 0:depth] = product(left, b)
            xd[r, 0:depth] = product(left_far, b)
        for q in range(3):
            ch = slice(q * 128, (q + 1) * 128)
            m = mix[p, :, ch]
            a = alpha[p, :, ch]

            def scan(j, sums):
                one, two, three = sums
                for h in range(2):
                    c = 2 * j + h
                    at = pl.ds(pl.multiple_of(c * STATES, STATES), STATES)
                    mu = nu = None
                    for step in range(s):
                        r = s - 1 - step if p == 0 else step
                        g = gg[q, pl.ds(start + r * s + c, 1), :]
                        e = xi[r, at, ch]
                        if step == 0:
                            mu = jnp.broadcast_to(g, (STATES, 128))
                        else:
                            decayed = mu * a
                            nu = decayed if nu is None else nu * a + decayed
                            mu = g + decayed
                            two = two + nu * e
                        one = one + mu * e
                        three = three + mu * xd[r, at, ch]
                        work[r, at, ch] = (m * mu).astype(BF)
                return one, two, three

            sums = tuple(acc[p, i, :, ch] for i in range(3))
            sums = lax.fori_loop(0, s // 2, scan, sums)
            for i in range(3):
                acc[p, i, :, ch] = sums[i]
        left = trim(back[p], s)
        for r in range(s):
            out = product(left, work[r, 0:depth, :])
            y = out[0:s, 0:D] + out[rows : rows + s, D:D2]
            if p == 0:
                ypad[r, 0:s] = y
            else:
                ypad[r, 0:s] += y
    place_rows(s, start, ypad, canvas)


def head_lanes(shape, axis, h):
    return iota(shape, axis) // HEAD_DIM == h


def attend_forward(s, start, row, queries, keys, values, probs, heads):
    size = WINDOW[s]
    a = pl.multiple_of((start // 16) * 16, 16)
    rows = pl.ds(a, size)
    q = queries[rows, :]
    k = keys[rows, :]
    vt = values[rows, :].astype(F32).T
    column = a + iota((size, 1), 0)
    line = a + iota((1, size), 1)
    ok_u = (column >= start) & (column < start + s * s)
    ok_t = (line >= start) & (line < start + s * s)
    ps = []
    vs = []
    for h in range(HEADS):
        qh = jnp.where(head_lanes((size, D), 1, h), q, jnp.zeros_like(q))
        score = jnp.where(ok_u, contract_second(k, qh), -1e30)
        e = jnp.exp(score - jnp.max(score, axis=0, keepdims=True))
        p = e * jnp.where(ok_t, 1.0 / jnp.sum(e, axis=0, keepdims=True), 0.0)
        probs[pl.ds(pl.multiple_of(row + h * size, 128), size), 0:size] = p
        ps.append(p.astype(BF))
        vs.append(jnp.where(head_lanes((D, size), 0, h), vt, 0.0).astype(BF))
    out = product(jnp.concatenate(vs, axis=1), jnp.concatenate(ps, axis=0))
    heads[rows, :] += out.T


def attend_backward(s, start, row, queries, keys, values, probs, grads, gq, gk, gv):
    size = WINDOW[s]
    rows = pl.ds(pl.multiple_of((start // 16) * 16, 16), size)
    q = queries[rows, :]
    k = keys[rows, :]
    v = values[rows, :]
    g = grads[rows, :]
    kt = k.astype(F32).T
    zero = jnp.zeros_like(q)
    ps = []
    ds = []
    gs = []
    qs = []
    ks = []
    for h in range(HEADS):
        lanes = head_lanes((size, D), 1, h)
        p = probs[pl.ds(pl.multiple_of(row + h * size, 128), size), 0:size]
        dp = contract_second(jnp.where(lanes, v, zero), g)
        inner = jnp.sum(dp * p, axis=0, keepdims=True)
        ds.append((p * (dp - inner)).astype(BF))
        ps.append(p.astype(BF))
        gs.append(jnp.where(lanes, g, zero))
        qs.append(jnp.where(lanes, q, zero))
        ks.append(jnp.where(head_lanes((D, size), 0, h), kt, 0.0).astype(BF))
    gv[rows, :] += product(jnp.concatenate(ps, axis=1), jnp.concatenate(gs, axis=0))
    gk[rows, :] += product(jnp.concatenate(ds, axis=1), jnp.concatenate(qs, axis=0))
    out = product(jnp.concatenate(ks, axis=1), jnp.concatenate(ds, axis=0))
    gq[rows, :] += out.T * 0.125


def block_body(
    sides, tok, cot, mixing, small, f_in, f_out, f_up, f_down,
    result, gtok, o_mix, o_small, o_in, o_out, o_up, o_down,
    flat, lanes, mix, alpha, cols, back, fan, fan_far, unit_one, scale_one, xx, gg, canvas_buf,
    ypad, sums, blocks, xi, xd, work, acc, w_out_t, w_up_t, w_down_t,
    queries, keys, values, grads, heads, gq, gk, gv, probs, act, hid, nrm, gml, after_grad,
):
    canvas = tok.shape[1]
    small_values = small[...].astype(F32)
    rates = small_values[0:1]
    gain_one = as_column(
        jnp.concatenate([small_values[1:2], small_values[2:3, 0:64]], axis=1)
    )
    gain_two = as_column(
        jnp.concatenate([small_values[2:3, 64:128], small_values[3:4]], axis=1)
    )

    def opened(ref, n, width):
        rows = ref.shape[0]
        flat[0:rows] = ref[...].astype(F32)
        return open_flat(flat, n, width, lanes)

    coefficients = opened(mixing, DIRS * STATES, D)
    for p in range(2):
        at = 2 * p * STATES
        mix[p] = jnp.concatenate(
            [coefficients[at : at + STATES], coefficients[at + STATES : at + 2 * STATES]], axis=1
        )
        down = [state_column(rates, at + d * STATES) for d in range(2)]
        across = [state_column(rates, DIRS * STATES + at + d * STATES) for d in range(2)]
        alpha[p] = jnp.exp(-pair_lanes(down[0], down[1]))
        cols[p] = column_decay(across, False)[0].astype(BF)
        value, far = column_decay(across, True)
        back[p] = value.astype(BF)
        fan[p] = value.T
        fan_far[p] = (value * far).T
    unit, scale = normalize(tok[...].astype(F32))
    unit_one[...] = unit
    scale_one[...] = scale
    normed = (unit * gain_one).astype(BF).astype(F32).T
    xx[:, 0:D] = normed
    xx[:, D:D2] = normed
    canvas_buf[...] = jnp.zeros_like(canvas_buf)
    sums[...] = jnp.zeros_like(sums)
    end = for_images(
        sides,
        lambda s, start, row: state_forward(
            s, start, xx, mix, alpha, cols, work, ypad, sums, canvas_buf
        ),
    )
    mixed_values = canvas_buf[0:canvas, :]
    mixed = mixed_values.astype(BF)
    mixed_t = mixed_values.T.astype(BF)
    w_in = opened(f_in, D, 3 * D).astype(BF)
    w_q = w_in[:, 0:D]
    w_k = w_in[:, D : 2 * D]
    w_v = w_in[:, 2 * D : 3 * D]
    for ref in (queries, keys, values, grads):
        ref[canvas : canvas + SPARE, :] = jnp.zeros((SPARE, D), BF)
    for ref in (heads, gq, gk, gv):
        ref[...] = jnp.zeros_like(ref)
    queries[0:canvas, :] = (product(mixed, w_q).astype(BF) * 0.125).astype(BF)
    keys[0:canvas, :] = product(mixed, w_k).astype(BF)
    values[0:canvas, :] = product(mixed, w_v).astype(BF)
    for_images(
        sides,
        lambda s, start, row: attend_forward(
            s, start, row, queries, keys, values, probs, heads
        ),
    )
    heads_t = heads[0:canvas, :].T.astype(BF)
    w_out = opened(f_out, D, D)
    w_out_t[...] = w_out.T.astype(BF)
    w_out = w_out.astype(BF)
    w_up = opened(f_up, D, FF)
    w_up_t[...] = w_up.T.astype(BF)
    w_up = w_up.astype(BF)
    w_down = opened(f_down, FF, D)
    w_down_t[...] = w_down.T.astype(BF)
    w_down = w_down.astype(BF)
    grad_gain = jnp.zeros((D, 1), F32)
    for i in range(canvas // TILE):
        here = slice(i * TILE, (i + 1) * TILE)
        live = (i * TILE + iota((1, TILE), 1) < end).astype(F32)
        after = tok[:, here].astype(F32) + live * product(w_out_t[...], heads_t[:, here])
        unit, scale = normalize(after)
        n2 = (unit * gain_two).astype(BF)
        nrm[:, here] = n2
        pre = product(w_up_t[...], n2)
        half = 0.5 * (1.0 + lax.erf(pre * ROOT_HALF))
        bent = (pre * half).astype(BF)
        act[:, here] = bent
        result[:, here] = (after + live * product(w_down_t[...], bent)).astype(BF)
        incoming = cot[:, here].astype(F32)
        gm = (live * incoming).astype(BF)
        gml[:, here] = gm
        slope = half + pre * jnp.exp(-0.5 * pre * pre) * DENSITY
        gh = (product(w_down, gm) * slope).astype(BF)
        hid[:, here] = gh
        gn = product(w_up, gh)
        grad_gain += jnp.sum(gn * unit, axis=1, keepdims=True)
        after_grad[:, here] = incoming + normalize_back(gn, unit, scale, gain_two)
    rows_gain_two = as_row(grad_gain)
    close_flat(flat, contract_second(act[...], gml[...]), lanes)
    o_down[...] = flat[0 : o_down.shape[0]]
    close_flat(flat, contract_second(nrm[...], hid[...]), lanes)
    o_up[...] = flat[0 : o_up.shape[0]]
    branch = jnp.where(iota((1, canvas), 1) < end, after_grad[...], 0.0).astype(BF)
    close_flat(flat, contract_second(heads_t, branch), lanes)
    o_out[...] = flat[0 : o_out.shape[0]]
    grads[0:canvas, :] = product(w_out, branch).T.astype(BF)
    for_images(
        sides,
        lambda s, start, row: attend_backward(
            s, start, row, queries, keys, values, probs, grads, gq, gk, gv
        ),
    )
    gq_low = gq[0:canvas, :].astype(BF)
    gk_low = gk[0:canvas, :].astype(BF)
    gv_low = gv[0:canvas, :].astype(BF)
    grad_in = [product(mixed_t, part) for part in (gq_low, gk_low, gv_low)]
    close_flat(flat, jnp.concatenate(grad_in, axis=1), lanes)
    o_in[...] = flat[0 : o_in.shape[0]]
    g = contract_second(gq_low, w_q) + contract_second(gk_low, w_k) + contract_second(gv_low, w_v)
    gg[0] = g[:, 0:128]
    gg[1] = jnp.concatenate([g[:, 128:D], g[:, 0:64]], axis=1)
    gg[2] = g[:, 64:D]
    blocks[...] = jnp.zeros_like(blocks)
    acc[...] = jnp.zeros_like(acc)
    for_images(
        sides,
        lambda s, start, row: state_backward(
            s, start, xx, gg, mix, alpha, back, fan, fan_far, blocks, xi, xd, work, ypad, acc,
            canvas_buf,
        ),
    )
    gn = canvas_buf[0:canvas, :].T
    unit = unit_one[...]
    rows_gain_one = as_row(jnp.sum(gn * unit, axis=1, keepdims=True))
    gtok[...] = after_grad[...] + normalize_back(gn, unit, scale_one[...], gain_one)
    grad_mix = []
    rate_grads = jnp.zeros((1, 128), F32)
    for p in range(2):
        by_row = mix[p] * acc[p, 1]
        by_col = mix[p] * acc[p, 2]
        for d in range(2):
            ch = slice(d * D, (d + 1) * D)
            at = (2 * p + d) * STATES
            grad_mix.append(acc[p, 0, :, ch])
            rate_grads -= state_row(jnp.sum(by_row[:, ch], axis=1, keepdims=True), at)
            rate_grads -= state_row(
                jnp.sum(by_col[:, ch], axis=1, keepdims=True), DIRS * STATES + at
            )
    close_flat(flat, jnp.concatenate(grad_mix, axis=0), lanes)
    o_mix[...] = flat[0 : o_mix.shape[0]]
    o_small[0:1] = rate_grads
    o_small[1:2] = rows_gain_one[:, 0:128]
    o_small[2:3] = jnp.concatenate([rows_gain_one[:, 128:D], rows_gain_two[:, 0:64]], axis=1)
    o_small[3:4] = rows_gain_two[:, 64:D]
    lane = iota((1, 128), 1)
    total = jnp.zeros((1, 128), F32)
    for d in range(DIRS):
        square = jnp.sum(jnp.sum(sums[d], axis=1, keepdims=True), axis=0, keepdims=True)
        total += jnp.where(lane == d, square, 0.0)
    o_small[4:5] = total
    o_small[5:8] = jnp.zeros((3, 128), F32)


def run_block(sides, tok, cot, flats):
    canvas = tok.shape[1]
    vm = pl.BlockSpec(memory_space=pltpu.VMEM)
    V = pltpu.VMEM
    sh = jax.ShapeDtypeStruct
    tall = canvas + SPARE
    wide = SMAX * STATES
    most = max(f.shape[0] for f in flats)
    return pl.pallas_call(
        block_body,
        out_shape=(sh((D, canvas), BF), sh((D, canvas), F32), sh(flats[0].shape, F32), sh((8, 128), F32))
        + tuple(sh(f.shape, F32) for f in flats[2:]),
        in_specs=[pl.BlockSpec(memory_space=pltpu.SMEM)] + [vm] * 8,
        out_specs=(vm,) * 8,
        scratch_shapes=[
            V((most, 128), F32), V((6, FF, 128), F32), V((2, STATES, D2), F32), V((2, STATES, D2), F32),
            V((2, 48, wide), BF), V((2, 48, wide), BF), V((2, wide, 48), F32), V((2, wide, 48), F32),
            V((D, canvas), F32), V((1, canvas), F32), V((canvas, D2), F32), V((3, canvas, 128), F32),
            V((canvas + 24, D), F32), V((SMAX, 24, D), F32), V((DIRS, 24, D), F32),
            V((SMAX, 24, D2), F32), V((SMAX, wide, D2), F32), V((SMAX, wide, D2), F32),
            V((SMAX, wide, D2), BF), V((2, 3, STATES, D2), F32),
            V((D, D), BF), V((FF, D), BF), V((D, FF), BF),
            V((tall, D), BF), V((tall, D), BF), V((tall, D), BF), V((tall, D), BF),
            V((tall, D), F32), V((tall, D), F32), V((tall, D), F32), V((tall, D), F32),
            V((PROB_ROWS, 384), F32), V((FF, canvas), BF), V((FF, canvas), BF),
            V((D, canvas), BF), V((D, canvas), BF), V((D, canvas), F32),
        ],
        compiler_params=pltpu.CompilerParams(vmem_limit_bytes=58 << 20),
    )(sides, tok, cot, *flats)


MESH = pl.DeviceIdType.MESH
SMALL_ROW = 3
HALF_LANES = 32


def xor_stages(count):
    out = []
    weight = 1
    while weight < count:
        radix = 4 if weight * 4 <= count else 2
        out.append((weight, radix))
        weight *= radix
    return out


def greet(dp, head, stages):
    barrier = pltpu.get_barrier_semaphore()
    peers = [(dp ^ (w * k), head) for w, r in stages for k in range(1, r)] + [(dp, 1 - head)]
    for peer in peers:
        pl.semaphore_signal(barrier, inc=1, device_id=peer, device_id_type=MESH)
    pl.semaphore_wait(barrier, len(peers))


def gather_blocks(count, buf, send, recv):
    dp = lax.axis_index("dp")
    head = lax.axis_index("head")
    stages = xor_stages(count)[::-1]
    greet(dp, head, stages)
    started = []

    def copy_of(block, n, slot, peer):
        return pltpu.make_async_remote_copy(
            src_ref=block, dst_ref=block, send_sem=send.at[n], recv_sem=recv.at[slot],
            device_id=peer, device_id_type=MESH,
        )

    def push(off, lands, other):
        block = buf.at[(dp ^ off) * 2 + head]
        peer = (dp, 1 - head) if other else (dp ^ off ^ lands, head)
        copy = copy_of(block, len(started), lands + count * other, peer)
        copy.start()
        started.append(copy)

    def arrived(off, other):
        block = buf.at[(dp ^ off) * 2 + (1 - head if other else head)]
        copy_of(block, 0, off + count * other, (dp, 1 - head)).wait_recv()

    held = [(0, 0)]
    at = 0
    while at < len(held):
        off, stage = held[at]
        at += 1
        if off:
            arrived(off, 0)
        for t in range(stage, len(stages)):
            w, r = stages[t]
            for k in range(1, r):
                push(off, off ^ (w * k), 0)
                held.append((off ^ (w * k), t + 1))
        push(off, off, 1)
    for off in range(count):
        arrived(off, 1)
    for copy in started:
        copy.wait_send()


def scatter_blocks(count, x, out, total, sends, lands, send, recv, shape_row):
    dp = lax.axis_index("dp")
    head = lax.axis_index("head")
    stages = xor_stages(count)
    greet(dp, head, stages)
    started = []
    slots = {}
    for off in range(count):
        slots[(-1, off)] = len(slots)
    for t, (w, r) in enumerate(stages):
        for k in range(1, r):
            for high in range(0, count, w * r):
                slots[(t, k * w + high)] = len(slots)

    def copy_of(n, peer):
        return pltpu.make_async_remote_copy(
            src_ref=sends.at[n], dst_ref=lands.at[n], send_sem=send.at[n], recv_sem=recv.at[n],
            device_id=peer, device_id_type=MESH,
        )

    def push(t, off, peer, value):
        n = slots[(t, off)]
        sends[n] = shape_row(value).astype(BF)
        copy = copy_of(n, peer)
        copy.start()
        started.append(copy)

    def take(t, off):
        n = slots[(t, off)]
        copy_of(n, (dp, 1 - head)).wait_recv()
        return lands[n].astype(F32)

    level = {}

    def settle(off, t):
        if off not in level:
            total[off] = x[(dp ^ off) * 2 + head] + take(-1, off)
            level[off] = 0
        while level[off] < t:
            w, r = stages[level[off]]
            value = total[off]
            for k in range(1, r):
                value = value + take(level[off], off ^ (k * w))
            total[off] = value
            level[off] += 1

    def rank(off):
        return tuple(0 if (off // w) % r else 1 for w, r in stages)

    for off in sorted(range(count), key=rank):
        push(-1, off, (dp, 1 - head), x[(dp ^ off) * 2 + 1 - head])
    for t, (w, r) in enumerate(stages):
        for k in range(1, r):
            for high in range(0, count, w * r):
                off = k * w + high
                settle(off, t)
                push(t, off, (dp ^ (k * w), head), total[off])
    settle(0, len(stages))
    out[...] = total[0]
    for copy in started:
        copy.wait_send()


def two_parts(block):
    row = block[SMALL_ROW : SMALL_ROW + 1]
    value = row[:, 0:HALF_LANES] + row[:, HALF_LANES : 2 * HALF_LANES]
    high = value.astype(BF).astype(F32)
    rest = jnp.zeros((1, 128 - 2 * HALF_LANES), F32)
    row = jnp.concatenate([high, value - high, rest], axis=1)
    return jnp.concatenate([block[0:SMALL_ROW], row, block[SMALL_ROW + 1 :]], axis=0)


def block_rows(rows):
    starts = []
    at = 0
    for r in rows:
        starts.append(at)
        at += r
    return starts, -(-at // 16) * 16


def gather_pieces_body(count, rows, *refs):
    pieces = refs[0:6]
    flats = refs[6:12]
    buf, send, recv = refs[12:15]
    opened = refs[15:]
    devices = 2 * count
    starts, tall = block_rows(rows)
    mine = lax.axis_index("dp") * 2 + lax.axis_index("head")
    small = pieces[1][...].astype(F32)
    per = small.shape[1]
    parts = [p[...].astype(F32) for p in pieces]
    parts[1] = jnp.concatenate([small, jnp.zeros((1, 128 - per), F32)], axis=1)
    spare = tall - starts[-1] - rows[-1]
    if spare:
        parts.append(jnp.zeros((spare, 128), F32))
    buf[mine] = jnp.concatenate(parts, axis=0).astype(BF)
    gather_blocks(count, buf, send, recv)
    line = []
    for i in range(devices):
        block = buf[i].astype(F32)
        for j in range(6):
            if j != 1:
                opened[j][rows[j] * i : rows[j] * (i + 1)] = block[starts[j] : starts[j] + rows[j]]
        line.append(block[starts[1] : starts[1] + 1, 0:per])
    each = 128 // per
    for r in range(devices // each):
        opened[1][r : r + 1] = jnp.concatenate(line[r * each : (r + 1) * each], axis=1)
    for j in range(6):
        flats[j][...] = opened[j][...].astype(BF)


def gather_pieces(count, pieces):
    devices = 2 * count
    rows = [p.shape[0] for p in pieces]
    tall = block_rows(rows)[1]
    shapes = [(devices * r, 128) for r in rows]
    shapes[1] = (devices * pieces[1].shape[1] // 128, 128)
    vm = pl.BlockSpec(memory_space=pltpu.VMEM)
    return pl.pallas_call(
        functools.partial(gather_pieces_body, count, rows),
        out_shape=tuple(jax.ShapeDtypeStruct(s, BF) for s in shapes),
        in_specs=[vm] * 6,
        out_specs=(vm,) * 6,
        scratch_shapes=[
            pltpu.VMEM((devices, tall, 128), BF),
            pltpu.SemaphoreType.DMA((devices - 1,)),
            pltpu.SemaphoreType.DMA((devices,)),
        ]
        + [pltpu.VMEM(s, F32) for s in shapes],
        compiler_params=pltpu.CompilerParams(collective_id=0, has_side_effects=True),
    )(*pieces)


def scatter_pieces_body(count, rows, per, *refs):
    flats = refs[0:6]
    out, x, total, sends, lands, send, recv = refs[6:]
    devices = 2 * count
    starts, tall = block_rows(rows)
    squares = flats[1][4:5, 0:DIRS]
    blank = jnp.zeros((1, 128 - per - DIRS), F32)
    spare = tall - starts[-1] - rows[-1]
    each = 128 // per
    for i in range(devices):
        at = per * (i % each)
        own = flats[1][i // each : i // each + 1, at : at + per]
        parts = [jnp.concatenate([own, squares, blank], axis=1)]
        parts += [flats[j][rows[j] * i : rows[j] * (i + 1)] for j in range(2, 6)]
        parts.insert(0, flats[0][rows[0] * i : rows[0] * (i + 1)])
        if spare:
            parts.append(jnp.zeros((spare, 128), F32))
        x[i] = jnp.concatenate(parts, axis=0)
    scatter_blocks(count, x, out, total, sends, lands, send, recv, two_parts)


def scatter_pieces(count, rows, per, flats):
    devices = 2 * count
    tall = block_rows(rows)[1]
    vm = pl.BlockSpec(memory_space=pltpu.VMEM)
    return pl.pallas_call(
        functools.partial(scatter_pieces_body, count, rows, per),
        out_shape=jax.ShapeDtypeStruct((tall, 128), F32),
        in_specs=[vm] * 6,
        out_specs=vm,
        scratch_shapes=scatter_scratch(devices, tall, True),
        compiler_params=pltpu.CompilerParams(
            collective_id=1, has_side_effects=True, vmem_limit_bytes=32 << 20
        ),
    )(*flats)


def scatter_scratch(devices, tall, own):
    V = pltpu.VMEM
    kept = [V((devices, tall, 128), F32)] if own else []
    return kept + [
        V((devices // 2, tall, 128), F32),
        V((devices - 1, tall, 128), BF),
        V((devices - 1, tall, 128), BF),
        pltpu.SemaphoreType.DMA((devices - 1,)),
        pltpu.SemaphoreType.DMA((devices - 1,)),
    ]


def finish_body(rows, per, slots, block, *outs):
    starts = block_rows(rows)[0]
    for j in (0, 2, 3, 4, 5):
        outs[j][...] = block[starts[j] : starts[j] + rows[j]]
    row = block[starts[1] : starts[1] + 1]
    value = row[:, 0:HALF_LANES] + row[:, HALF_LANES : 2 * HALF_LANES]
    outs[1][...] = value[:, 0:per]
    roots = jnp.sqrt(value[:, per : per + DIRS] * (1.0 / slots) + 1e-06)
    outs[6][...] = jnp.sum(roots, axis=1, keepdims=True)


def finish(rows, per, slots, block):
    vm = pl.BlockSpec(memory_space=pltpu.VMEM)
    shapes = [(r, 128) for r in rows]
    shapes[1] = (1, per)
    shapes.append((1, 1))
    return pl.pallas_call(
        functools.partial(finish_body, rows, per, slots),
        out_shape=tuple(jax.ShapeDtypeStruct(s, F32) for s in shapes),
        in_specs=[vm],
        out_specs=(vm,) * 7,
    )(block)


def gather_whole_body(count, x, buf, send, recv):
    mine = lax.axis_index("dp") * 2 + lax.axis_index("head")
    buf[mine] = x[...]
    gather_blocks(count, buf, send, recv)


def gather_whole(count, x):
    devices = 2 * count
    vm = pl.BlockSpec(memory_space=pltpu.VMEM)
    return pl.pallas_call(
        functools.partial(gather_whole_body, count),
        out_shape=jax.ShapeDtypeStruct((devices,) + x.shape, x.dtype),
        in_specs=[vm],
        out_specs=vm,
        scratch_shapes=[
            pltpu.SemaphoreType.DMA((devices - 1,)),
            pltpu.SemaphoreType.DMA((devices,)),
        ],
        compiler_params=pltpu.CompilerParams(collective_id=0, has_side_effects=True),
    )(x)


def scatter_whole_body(count, x, out, total, sends, lands, send, recv):
    scatter_blocks(count, x, out, total, sends, lands, send, recv, lambda block: block)


def scatter_whole(count, x):
    vm = pl.BlockSpec(memory_space=pltpu.VMEM)
    return pl.pallas_call(
        functools.partial(scatter_whole_body, count),
        out_shape=jax.ShapeDtypeStruct(x.shape[1:], F32),
        in_specs=[vm],
        out_specs=vm,
        scratch_shapes=scatter_scratch(2 * count, x.shape[1], False),
        compiler_params=pltpu.CompilerParams(
            collective_id=1, has_side_effects=True, vmem_limit_bytes=32 << 20
        ),
    )(x)


def fill_rows(flat):
    rows = -(-flat.shape[-1] // 2048) * 16
    pad = [(0, 0)] * (flat.ndim - 1) + [(0, rows * 128 - flat.shape[-1])]
    return jnp.pad(flat, pad).reshape(flat.shape[:-1] + (rows, 128))


def per_device(count, tokens, cotangent, image_sides, *parts):
    canvas = tokens.shape[0]
    devices = 2 * count
    lengths = [p.shape[0] for p in parts]
    per = lengths[1]
    whole_rows = all(n % 128 == 0 for n in lengths[0:1] + lengths[2:])
    whole_rows = whole_rows and 128 % per == 0 and per + DIRS <= HALF_LANES
    whole_rows = whole_rows and lengths[0] == SMALL_ROW * 128
    rows = [n // 128 for n in lengths]
    rows[1] = 1
    if whole_rows:
        pieces = [p.reshape((1, per) if j == 1 else (-1, 128)) for j, p in enumerate(parts)]
        flats = gather_pieces(count, pieces)
    else:
        blocks = gather_whole(count, fill_rows(jnp.concatenate(parts))).reshape(devices, -1)
        flats = []
        at = 0
        for n in lengths:
            flats.append(blocks[:, at : at + n].reshape(-1, 128))
            at += n
    result, gtok, *grads = run_block(image_sides, tokens.T, cotangent.T, flats)
    slots = float(devices * canvas * D)
    if whole_rows:
        block = scatter_pieces(count, rows, per, grads)
        *outs, penalty = finish(rows, per, slots, block)
        outs = [o.reshape(-1) for o in outs]
        penalty = penalty.reshape(())
    else:
        squares = grads[1][4, 0:DIRS]
        grads[1] = grads[1][0:4]
        pieces = [g.reshape(devices, -1) for g in grads]
        pieces.append(jnp.broadcast_to(squares[None], (devices, DIRS)))
        block = scatter_whole(count, fill_rows(jnp.concatenate(pieces, axis=1))).reshape(-1)
        outs = []
        at = 0
        for n in lengths:
            outs.append(block[at : at + n])
            at += n
        penalty = jnp.sum(jnp.sqrt(block[at : at + DIRS] * (1.0 / slots) + 1e-06))
    return (result.T, gtok.T, penalty, *outs)


def solution(mesh):
    both = P(("dp", "head"))
    plane = P(("dp", "head"), None)
    return jax.shard_map(
        functools.partial(per_device, mesh.shape["dp"]),
        mesh=mesh,
        in_specs=(plane,) * 3 + (both,) * 6,
        out_specs=(plane,) * 2 + (P(),) + (both,) * 6,
        check_vma=False,
    )
```

```python
import functools
import math

import jax
import jax.numpy as jnp
from jax import lax
from jax.experimental import pallas as pl
from jax.experimental.pallas import tpu as pltpu
from jax.sharding import PartitionSpec as P

D = 192
D2 = 2 * D
DIRS = 4
STATES = 16
HEADS = 3
HEAD_DIM = 64
FF = 768
SLOTS = 10
SMAX = 18
EPSILON = 1e-05
ROOT_HALF = 1.0 / math.sqrt(2.0)
DENSITY = 1.0 / math.sqrt(2.0 * math.pi)
F32 = jnp.float32
BF = jnp.bfloat16
PAD_ROWS = {10: 16, 14: 16, 18: 24}
WINDOW = {10: 128, 14: 256, 18: 384}
SPARE = 64
TILE = 256
PROB_ROWS = 4096


def contract_second(left, right):
    return lax.dot_general(left, right, (((1,), (1,)), ((), ())), preferred_element_type=F32)


def product(left, right):
    return jnp.dot(left, right, preferred_element_type=F32)


def iota(shape, axis):
    return lax.broadcasted_iota(jnp.int32, shape, axis)


def open_flat(flat, n, width, lanes):
    chunks = -(-width // 128)
    if width % 128 == 0:
        return jnp.concatenate(
            [flat[pl.ds(j, n, stride=chunks), :] for j in range(chunks)], axis=1
        )
    step = width // 64
    half = step // 2
    piece = [flat[pl.ds(j, n // 2, stride=step), :] for j in range(step)]
    piece.append(piece[-1])
    for c in range(chunks):
        lanes[c, pl.ds(0, n // 2, stride=2), :] = piece[c]
        lanes[c, pl.ds(1, n // 2, stride=2), :] = jnp.concatenate(
            [piece[half + c][:, 64:], piece[half + c + 1][:, :64]], axis=1
        )
    return jnp.concatenate([lanes[c, 0:n, :] for c in range(chunks)], axis=1)[:, 0:width]


def close_flat(flat, matrix, lanes):
    n, width = matrix.shape
    chunks = -(-width // 128)
    if width % 128 == 0:
        for j in range(chunks):
            flat[pl.ds(j, n, stride=chunks), :] = matrix[:, 128 * j : 128 * j + 128]
        return
    step = width // 64
    half = step // 2
    for c in range(chunks):
        part = matrix[:, 128 * c : min(width, 128 * c + 128)]
        lanes[c, 0:n, 0 : part.shape[1]] = part
    even = [lanes[c, pl.ds(0, n // 2, stride=2), :] for c in range(chunks)]
    odd = [lanes[c, pl.ds(1, n // 2, stride=2), :] for c in range(chunks)]
    piece = even[:half] + [jnp.concatenate([even[half][:, :64], odd[0][:, :64]], axis=1)]
    piece += [jnp.concatenate([odd[c][:, 64:], odd[c + 1][:, :64]], axis=1) for c in range(half)]
    for j in range(step):
        flat[pl.ds(j, n // 2, stride=step), :] = piece[j]


def as_column(row):
    return jnp.broadcast_to(row, (8, row.shape[1])).T[:, 0:1]


def as_row(column):
    return jnp.broadcast_to(column, (column.shape[0], 128)).T[0:1, :]


def state_column(row, at):
    hit = iota((STATES, 128), 1) == at + iota((STATES, 128), 0)
    return jnp.sum(jnp.where(hit, row, 0.0), axis=1, keepdims=True)


def state_row(column, at):
    hit = iota((STATES, 128), 1) == at + iota((STATES, 128), 0)
    return jnp.sum(jnp.where(hit, column, 0.0), axis=0, keepdims=True)


def pair_lanes(first, second):
    return jnp.where(iota((STATES, D2), 1) < D, first, second)


def column_decay(rates, swap):
    width = SMAX * STATES
    shape = (48, width)
    state = iota((STATES, width), 1) % STATES == iota((STATES, width), 0)
    spread = [jnp.sum(jnp.where(state, r, 0.0), axis=0, keepdims=True) for r in rates]
    rows = iota(shape, 0)
    first = rows < 24
    here = jnp.where(first, rows, rows - 24)
    there = iota(shape, 1) // STATES
    gap = there - here if swap else here - there
    far = jnp.abs(gap).astype(F32)
    value = jnp.exp(-jnp.where(first, spread[0], spread[1]) * far)
    return jnp.where(jnp.where(first, 1, -1) * gap >= 0, value, 0.0), far


def normalize(values):
    centered = values - jnp.mean(values, axis=0, keepdims=True)
    scale = lax.rsqrt(jnp.mean(centered * centered, axis=0, keepdims=True) + EPSILON)
    return centered * scale, scale


def normalize_back(grad, unit, scale, gain):
    scaled = grad * gain
    inner = jnp.mean(scaled * unit, axis=0, keepdims=True)
    return scale * (scaled - jnp.mean(scaled, axis=0, keepdims=True) - unit * inner)


def for_images(sides, body):
    def each(k, carry):
        start, row = carry
        side = sides[0, k]
        for s in (10, 14, 18):

            @pl.when(side == s)
            def _():
                body(s, start, row)

        used = jnp.where(side == 10, 128, jnp.where(side == 14, 256, 384)) * HEADS
        return start + side * side, row + jnp.where(side > 0, used, 0)

    return lax.fori_loop(0, SLOTS, each, (0, 0))[0]


def trim(matrix, s):
    if s == SMAX:
        return matrix
    depth = s * STATES
    return jnp.concatenate([matrix[0:16, 0:depth], matrix[24:40, 0:depth]], axis=0)


def scan_forward(s, start, p, c, xx, m, a, work):
    at = pl.ds(pl.multiple_of(c * STATES, STATES), STATES)
    state = None
    for step in range(s):
        r = step if p == 0 else s - 1 - step
        term = m * xx[pl.ds(start + r * s + c, 1), :]
        state = term if state is None else state * a + term
        work[r, at, :] = state.astype(BF)


def rows_forward(s, p, r, left, work, ypad, squares):
    rows = PAD_ROWS[s]
    depth = s * STATES
    both = jnp.concatenate([work[r, 0:depth, :], work[r + 1, 0:depth, :]], axis=1)
    out = product(left, both)
    first, second = squares
    for h in range(2):
        at = h * D2
        one = out[0:s, at : at + D]
        two = out[rows : rows + s, at + D : at + D2]
        if p == 0:
            ypad[r + h, 0:s] = one + two
        else:
            ypad[r + h, 0:s] += one + two
        first = first + one * one
        second = second + two * two
    return first, second


def state_forward(s, start, xx, mix, alpha, cols, work, ypad, sums, canvas):
    for p in range(2):

        def scan(j, _):
            for h in range(2):
                scan_forward(s, start, p, 2 * j + h, xx, mix[p], alpha[p], work)
            return 0

        lax.fori_loop(0, s // 2, scan, 0)
        left = trim(cols[p], s)
        squares = (sums[2 * p, 0:s], sums[2 * p + 1, 0:s])
        for r in range(0, s, 2):
            squares = rows_forward(s, p, r, left, work, ypad, squares)
        sums[2 * p, 0:s] = squares[0]
        sums[2 * p + 1, 0:s] = squares[1]
    place_rows(s, start, ypad, canvas)


def place_rows(s, start, ypad, canvas):
    def place(r, _):
        for c in range(s):
            canvas[pl.ds(start + r * s + c, 1), :] = ypad[r, pl.ds(c, 1), :]
        return 0

    lax.fori_loop(0, s, place, 0)


def scan_backward(s, start, p, q, gg, mix, alpha, xi, xd, work, acc):
    ch = slice(q * 128, (q + 1) * 128)
    m = mix[p, :, ch]
    a = alpha[p, :, ch]

    def scan(j, sums):
        one, two, three = sums
        for h in range(2):
            c = 2 * j + h
            at = pl.ds(pl.multiple_of(c * STATES, STATES), STATES)
            mu = nu = None
            for step in range(s):
                r = s - 1 - step if p == 0 else step
                g = gg[q, pl.ds(start + r * s + c, 1), :]
                e = xi[r, at, ch]
                if step == 0:
                    mu = jnp.broadcast_to(g, (STATES, 128))
                else:
                    decayed = mu * a
                    nu = decayed if nu is None else nu * a + decayed
                    mu = g + decayed
                    two = two + nu * e
                one = one + mu * e
                three = three + mu * xd[r, at, ch]
                work[r, at, ch] = (m * mu).astype(BF)
        return one, two, three

    sums = lax.fori_loop(0, s // 2, scan, tuple(acc[p, i, :, ch] for i in range(3)))
    for i in range(3):
        acc[p, i, :, ch] = sums[i]


def state_backward(
    s, start, xx, gg, mix, alpha, back, fan, fan_far, blocks, xi, xd, work, ypad, acc, canvas
):
    rows = PAD_ROWS[s]
    depth = s * STATES
    lane = iota((depth, 48), 1)
    keep = jnp.where(lane < 24, lane, lane - 24) < s
    low = iota((24, D2), 1) < D
    lefts = [
        [jnp.where(keep, f[p, 0:depth], 0.0).astype(BF) for f in (fan, fan_far)] for p in range(2)
    ]

    def gather_rows(r, _):
        for c in range(s):
            blocks[r, pl.ds(c, 1), :] = xx[pl.ds(start + r * s + c, 1), :]
        return 0

    lax.fori_loop(0, s, gather_rows, 0)
    for p in range(2):
        for r in range(s):
            b = blocks[r]
            b = jnp.concatenate([jnp.where(low, b, 0.0), jnp.where(low, 0.0, b)], axis=0)
            b = b.astype(BF)
            xi[r, 0:depth] = product(lefts[p][0], b)
            xd[r, 0:depth] = product(lefts[p][1], b)
        for q in range(3):
            scan_backward(s, start, p, q, gg, mix, alpha, xi, xd, work, acc)
        left = trim(back[p], s)
        for r in range(0, s, 2):
            both = jnp.concatenate([work[r, 0:depth, :], work[r + 1, 0:depth, :]], axis=1)
            out = product(left, both)
            for h in range(2):
                at = h * D2
                y = out[0:s, at : at + D] + out[rows : rows + s, at + D : at + D2]
                if p == 0:
                    ypad[r + h, 0:s] = y
                else:
                    ypad[r + h, 0:s] += y
    place_rows(s, start, ypad, canvas)


def head_lanes(shape, axis, h):
    return iota(shape, axis) // HEAD_DIM == h


def attend_forward(s, start, row, queries, keys, values, probs, heads):
    size = WINDOW[s]
    a = pl.multiple_of((start // 16) * 16, 16)
    rows = pl.ds(a, size)
    q = queries[rows, :]
    k = keys[rows, :]
    vt = values[rows, :].astype(F32).T
    column = a + iota((size, 1), 0)
    line = a + iota((1, size), 1)
    ok_u = (column >= start) & (column < start + s * s)
    ok_t = (line >= start) & (line < start + s * s)
    ps = []
    vs = []
    for h in range(HEADS):
        qh = jnp.where(head_lanes((size, D), 1, h), q, jnp.zeros_like(q))
        score = jnp.where(ok_u, contract_second(k, qh), -1e30)
        e = jnp.exp(score - jnp.max(score, axis=0, keepdims=True))
        p = e * jnp.where(ok_t, 1.0 / jnp.sum(e, axis=0, keepdims=True), 0.0)
        probs[pl.ds(pl.multiple_of(row + h * size, 128), size), 0:size] = p
        ps.append(p.astype(BF))
        vs.append(jnp.where(head_lanes((D, size), 0, h), vt, 0.0).astype(BF))
    out = product(jnp.concatenate(vs, axis=1), jnp.concatenate(ps, axis=0))
    heads[rows, :] += out.T


def attend_backward(s, start, row, queries, keys, values, probs, grads, gq, gk, gv):
    size = WINDOW[s]
    rows = pl.ds(pl.multiple_of((start // 16) * 16, 16), size)
    q = queries[rows, :]
    k = keys[rows, :]
    v = values[rows, :]
    g = grads[rows, :]
    kt = k.astype(F32).T
    zero = jnp.zeros_like(q)
    ps = []
    ds = []
    gs = []
    qs = []
    ks = []
    for h in range(HEADS):
        lanes = head_lanes((size, D), 1, h)
        p = probs[pl.ds(pl.multiple_of(row + h * size, 128), size), 0:size]
        dp = contract_second(jnp.where(lanes, v, zero), g)
        inner = jnp.sum(dp * p, axis=0, keepdims=True)
        ds.append((p * (dp - inner)).astype(BF))
        ps.append(p.astype(BF))
        gs.append(jnp.where(lanes, g, zero))
        qs.append(jnp.where(lanes, q, zero))
        ks.append(jnp.where(head_lanes((D, size), 0, h), kt, 0.0).astype(BF))
    gv[rows, :] += product(jnp.concatenate(ps, axis=1), jnp.concatenate(gs, axis=0))
    gk[rows, :] += product(jnp.concatenate(ds, axis=1), jnp.concatenate(qs, axis=0))
    out = product(jnp.concatenate(ks, axis=1), jnp.concatenate(ds, axis=0))
    gq[rows, :] += out.T * 0.125


def block_body(
    rows, sides, tok, cot, *refs
):
    if rows is None:
        inputs = refs[0:6]
        outputs = refs[6:14]
        refs = refs[14:]
    else:
        inputs = None
        source = refs[0]
        outputs = refs[1:4]
        refs = refs[4:]
    result, gtok = outputs[0:2]
    (flat, lanes, kept, mix, alpha, cols, back, fan, fan_far, unit_one, scale_one, gain_row, xx, gg,
     canvas_buf, ypad, sums, work, acc, after_grad) = refs
    V = pltpu.VMEM
    devices = None if rows is None else source.shape[0]
    if rows is not None:
        per = 128 * 4 // devices
        starts, tall_block = block_rows(rows)
        line = []
        for i in range(devices):
            block = source[i].astype(F32)
            at = 0
            for piece in (0, 2, 3, 4, 5):
                n = rows[piece]
                kept[at + n * i : at + n * (i + 1)] = block[starts[piece] : starts[piece] + n]
                at += n * devices
            line.append(block[starts[1] : starts[1] + 1, 0:per])
        each = 128 // per
        small_values = jnp.concatenate(
            [
                jnp.concatenate(line[r * each : (r + 1) * each], axis=1)
                for r in range(devices // each)
            ],
            axis=0,
        )
    else:
        small_values = inputs[1][...].astype(F32)
        at = 0
        for piece in (0, 2, 3, 4, 5):
            n = inputs[piece].shape[0]
            kept[at : at + n] = inputs[piece][...].astype(F32)
            at += n
    canvas = tok.shape[1]
    rates = small_values[0:1]
    gain_one = as_column(
        jnp.concatenate([small_values[1:2], small_values[2:3, 0:64]], axis=1)
    )
    gain_two = as_column(
        jnp.concatenate([small_values[2:3, 64:128], small_values[3:4]], axis=1)
    )

    sizes = [DIRS * STATES * D, D * 3 * D, D * D, D * FF, FF * D]

    def opened(piece, n, width):
        at = sum(sizes[:piece]) // 128
        return open_flat(kept.at[at : at + n * width // 128], n, width, lanes)

    def closed(piece, matrix):
        n = matrix.shape[0] * matrix.shape[1] // 128
        close_flat(flat, matrix, lanes)
        if rows is None:
            outputs[(2, 4, 5, 6, 7)[piece]][...] = flat[0:n]
        else:
            r = rows[(0, 2, 3, 4, 5)[piece]]
            here = starts[(0, 2, 3, 4, 5)[piece]]
            for i in range(devices):
                outputs[2][i, here : here + r] = flat[r * i : r * (i + 1)]

    coefficients = opened(0, DIRS * STATES, D)
    for p in range(2):
        at = 2 * p * STATES
        mix[p] = jnp.concatenate(
            [coefficients[at : at + STATES], coefficients[at + STATES : at + 2 * STATES]], axis=1
        )
        down = [state_column(rates, at + d * STATES) for d in range(2)]
        across = [state_column(rates, DIRS * STATES + at + d * STATES) for d in range(2)]
        alpha[p] = jnp.exp(-pair_lanes(down[0], down[1]))
        cols[p] = column_decay(across, False)[0].astype(BF)
        value, far = column_decay(across, True)
        back[p] = value.astype(BF)
        fan[p] = value.T
        fan_far[p] = (value * far).T
    unit, scale = normalize(tok[...].astype(F32))
    unit_one[...] = unit
    scale_one[...] = scale
    normed = (unit * gain_one).astype(BF).astype(F32).T
    xx[:, 0:D] = normed
    xx[:, D:D2] = normed
    canvas_buf[...] = jnp.zeros_like(canvas_buf)
    sums[...] = jnp.zeros_like(sums)
    end = for_images(
        sides,
        lambda s, start, row: state_forward(
            s, start, xx, mix, alpha, cols, work, ypad, sums, canvas_buf
        ),
    )
    mixed_values = canvas_buf[0:canvas, :]
    mixed = mixed_values.astype(BF)
    mixed_t = mixed_values.T.astype(BF)
    def middle(queries, keys, values, grads, heads, gq, gk, gv, probs, act, hid, nrm, gml,
               w_out_t, w_up_t, w_down_t):
        w_in = opened(1, D, 3 * D).astype(BF)
        w_q = w_in[:, 0:D]
        w_k = w_in[:, D : 2 * D]
        w_v = w_in[:, 2 * D : 3 * D]
        for ref in (queries, keys, values, grads):
            ref[canvas : canvas + SPARE, :] = jnp.zeros((SPARE, D), BF)
        for ref in (heads, gq, gk, gv):
            ref[...] = jnp.zeros_like(ref)
        queries[0:canvas, :] = (product(mixed, w_q).astype(BF) * 0.125).astype(BF)
        keys[0:canvas, :] = product(mixed, w_k).astype(BF)
        values[0:canvas, :] = product(mixed, w_v).astype(BF)
        for_images(
            sides,
            lambda s, start, row: attend_forward(
                s, start, row, queries, keys, values, probs, heads
            ),
        )
        heads_t = heads[0:canvas, :].T.astype(BF)
        w_out = opened(2, D, D)
        w_out_t[...] = w_out.T.astype(BF)
        w_out = w_out.astype(BF)
        w_up = opened(3, D, FF)
        w_up_t[...] = w_up.T.astype(BF)
        w_up = w_up.astype(BF)
        w_down = opened(4, FF, D)
        w_down_t[...] = w_down.T.astype(BF)
        w_down = w_down.astype(BF)
        grad_gain = jnp.zeros((D, 1), F32)
        for i in range(canvas // TILE):
            here = slice(i * TILE, (i + 1) * TILE)
            live = (i * TILE + iota((1, TILE), 1) < end).astype(F32)
            after = tok[:, here].astype(F32) + live * product(w_out_t[...], heads_t[:, here])
            unit, scale = normalize(after)
            n2 = (unit * gain_two).astype(BF)
            nrm[:, here] = n2
            pre = product(w_up_t[...], n2)
            half = 0.5 * (1.0 + lax.erf(pre * ROOT_HALF))
            bent = (pre * half).astype(BF)
            act[:, here] = bent
            result[:, here] = (after + live * product(w_down_t[...], bent)).astype(BF)
            incoming = cot[:, here].astype(F32)
            gm = (live * incoming).astype(BF)
            gml[:, here] = gm
            slope = half + pre * jnp.exp(-0.5 * pre * pre) * DENSITY
            gh = (product(w_down, gm) * slope).astype(BF)
            hid[:, here] = gh
            gn = product(w_up, gh)
            grad_gain += jnp.sum(gn * unit, axis=1, keepdims=True)
            after_grad[:, here] = incoming + normalize_back(gn, unit, scale, gain_two)
        gain_row[...] = as_row(grad_gain)
        closed(4, contract_second(act[...], gml[...]))
        closed(3, contract_second(nrm[...], hid[...]))
        branch = jnp.where(iota((1, canvas), 1) < end, after_grad[...], 0.0).astype(BF)
        closed(2, contract_second(heads_t, branch))
        grads[0:canvas, :] = product(w_out, branch).T.astype(BF)
        for_images(
            sides,
            lambda s, start, row: attend_backward(
                s, start, row, queries, keys, values, probs, grads, gq, gk, gv
            ),
        )
        gq_low = gq[0:canvas, :].astype(BF)
        gk_low = gk[0:canvas, :].astype(BF)
        gv_low = gv[0:canvas, :].astype(BF)
        grad_in = [product(mixed_t, part) for part in (gq_low, gk_low, gv_low)]
        closed(1, jnp.concatenate(grad_in, axis=1))
        g = contract_second(gq_low, w_q) + contract_second(gk_low, w_k) + contract_second(gv_low, w_v)
        gg[0] = g[:, 0:128]
        gg[1] = jnp.concatenate([g[:, 128:D], g[:, 0:64]], axis=1)
        gg[2] = g[:, 64:D]

    tall = canvas + SPARE
    pl.run_scoped(
        middle,
        V((tall, D), BF), V((tall, D), BF), V((tall, D), BF), V((tall, D), BF),
        V((tall, D), F32), V((tall, D), F32), V((tall, D), F32), V((tall, D), F32),
        V((PROB_ROWS, 384), F32), V((FF, canvas), BF), V((FF, canvas), BF),
        V((D, canvas), BF), V((D, canvas), BF),
        V((D, D), BF), V((FF, D), BF), V((D, FF), BF),
    )
    acc[...] = jnp.zeros_like(acc)

    def adjoint(blocks, xi, xd):
        blocks[...] = jnp.zeros_like(blocks)
        for_images(
            sides,
            lambda s, start, row: state_backward(
                s, start, xx, gg, mix, alpha, back, fan, fan_far, blocks, xi, xd, work, ypad, acc,
                canvas_buf,
            ),
        )

    wide = SMAX * STATES
    pl.run_scoped(
        adjoint,
        V((SMAX, 24, D2), F32), V((SMAX, wide, D2), F32), V((SMAX, wide, D2), F32),
    )
    gn = canvas_buf[0:canvas, :].T
    unit = unit_one[...]
    rows_gain_one = as_row(jnp.sum(gn * unit, axis=1, keepdims=True))
    gtok[...] = after_grad[...] + normalize_back(gn, unit, scale_one[...], gain_one)
    grad_mix = []
    rate_grads = jnp.zeros((1, 128), F32)
    for p in range(2):
        by_row = mix[p] * acc[p, 1]
        by_col = mix[p] * acc[p, 2]
        for d in range(2):
            ch = slice(d * D, (d + 1) * D)
            at = (2 * p + d) * STATES
            grad_mix.append(acc[p, 0, :, ch])
            rate_grads -= state_row(jnp.sum(by_row[:, ch], axis=1, keepdims=True), at)
            rate_grads -= state_row(
                jnp.sum(by_col[:, ch], axis=1, keepdims=True), DIRS * STATES + at
            )
    closed(0, jnp.concatenate(grad_mix, axis=0))
    rows_gain_two = gain_row[...]
    grad_small = [
        rate_grads,
        rows_gain_one[:, 0:128],
        jnp.concatenate([rows_gain_one[:, 128:D], rows_gain_two[:, 0:64]], axis=1),
        rows_gain_two[:, 64:D],
    ]
    lane = iota((1, 128), 1)
    total = jnp.zeros((1, 128), F32)
    for d in range(DIRS):
        square = jnp.sum(jnp.sum(sums[d], axis=1, keepdims=True), axis=0, keepdims=True)
        total += jnp.where(lane == d, square, 0.0)
    if rows is None:
        for r in range(4):
            outputs[3][r : r + 1] = grad_small[r]
        outputs[3][4:5] = total
        outputs[3][5:8] = jnp.zeros((3, 128), F32)
    else:
        blank = jnp.zeros((1, 128 - per - DIRS), F32)
        spare = tall_block - starts[5] - rows[5]
        for i in range(devices):
            at = per * (i % each)
            own = grad_small[i // each][:, at : at + per]
            outputs[2][i, starts[1] : starts[1] + 1] = jnp.concatenate(
                [own, total[:, 0:DIRS], blank], axis=1
            )
            if spare:
                outputs[2][i, tall_block - spare :] = jnp.zeros((spare, 128), F32)


def run_block(rows, sides, tok, cot, inputs):
    canvas = tok.shape[1]
    vm = pl.BlockSpec(memory_space=pltpu.VMEM)
    V = pltpu.VMEM
    sh = jax.ShapeDtypeStruct
    wide = SMAX * STATES
    if rows is None:
        grads = tuple(sh((8, 128) if j == 1 else f.shape, F32) for j, f in enumerate(inputs))
    else:
        grads = (sh(inputs[0].shape, F32),)
    states = DIRS * STATES * D // 128
    most = D * FF // 128
    kept = states + D * 4 * D // 128 + 2 * most
    return pl.pallas_call(
        functools.partial(block_body, rows),
        out_shape=(sh((D, canvas), BF), sh((D, canvas), F32)) + grads,
        in_specs=[pl.BlockSpec(memory_space=pltpu.SMEM)] + [vm] * (2 + len(inputs)),
        out_specs=(vm,) * (2 + len(grads)),
        scratch_shapes=[
            V((most, 128), F32), V((5, FF, 128), F32), V((kept, 128), F32),
            V((2, STATES, D2), F32), V((2, STATES, D2), F32),
            V((2, 48, wide), BF), V((2, 48, wide), BF), V((2, wide, 48), F32), V((2, wide, 48), F32),
            V((D, canvas), F32), V((1, canvas), F32), V((1, D), F32),
            V((canvas, D2), F32), V((3, canvas, 128), F32),
            V((canvas + 24, D), F32), V((SMAX, 24, D), F32), V((DIRS, 24, D), F32),
            V((SMAX, wide, D2), BF), V((2, 3, STATES, D2), F32), V((D, canvas), F32),
        ],
        compiler_params=pltpu.CompilerParams(vmem_limit_bytes=60 << 20),
    )(sides, tok, cot, *inputs)


MESH = pl.DeviceIdType.MESH
SMALL_ROW = 3
HALF_LANES = 32


def xor_stages(count):
    out = []
    weight = 1
    while weight < count:
        radix = 4 if weight * 4 <= count else 2
        out.append((weight, radix))
        weight *= radix
    return out


def greet(dp, head, stages):
    barrier = pltpu.get_barrier_semaphore()
    peers = [(dp ^ (w * k), head) for w, r in stages for k in range(1, r)] + [(dp, 1 - head)]
    for peer in peers:
        pl.semaphore_signal(barrier, inc=1, device_id=peer, device_id_type=MESH)
    pl.semaphore_wait(barrier, len(peers))


def gather_blocks(count, buf, send, recv):
    dp = lax.axis_index("dp")
    head = lax.axis_index("head")
    stages = xor_stages(count)[::-1]
    greet(dp, head, stages)
    started = []

    def copy_of(block, n, slot, peer):
        return pltpu.make_async_remote_copy(
            src_ref=block, dst_ref=block, send_sem=send.at[n], recv_sem=recv.at[slot],
            device_id=peer, device_id_type=MESH,
        )

    def push(off, lands, other):
        block = buf.at[(dp ^ off) * 2 + head]
        peer = (dp, 1 - head) if other else (dp ^ off ^ lands, head)
        copy = copy_of(block, len(started), lands + count * other, peer)
        copy.start()
        started.append(copy)

    def arrived(off, other):
        block = buf.at[(dp ^ off) * 2 + (1 - head if other else head)]
        copy_of(block, 0, off + count * other, (dp, 1 - head)).wait_recv()

    held = [(0, 0)]
    at = 0
    while at < len(held):
        off, stage = held[at]
        at += 1
        if off:
            arrived(off, 0)
        for t in range(stage, len(stages)):
            w, r = stages[t]
            for k in range(1, r):
                push(off, off ^ (w * k), 0)
                held.append((off ^ (w * k), t + 1))
        push(off, off, 1)
    for off in range(count):
        arrived(off, 1)
    for copy in started:
        copy.wait_send()


def scatter_blocks(count, x, out, total, sends, lands, send, recv, shape_row):
    dp = lax.axis_index("dp")
    head = lax.axis_index("head")
    stages = xor_stages(count)
    greet(dp, head, stages)
    started = []
    slots = {}
    for off in range(count):
        slots[(-1, off)] = len(slots)
    for t, (w, r) in enumerate(stages):
        for k in range(1, r):
            for high in range(0, count, w * r):
                slots[(t, k * w + high)] = len(slots)

    def copy_of(n, peer):
        return pltpu.make_async_remote_copy(
            src_ref=sends.at[n], dst_ref=lands.at[n], send_sem=send.at[n], recv_sem=recv.at[n],
            device_id=peer, device_id_type=MESH,
        )

    def push(t, off, peer, value):
        n = slots[(t, off)]
        sends[n] = shape_row(value).astype(BF)
        copy = copy_of(n, peer)
        copy.start()
        started.append(copy)

    def take(t, off):
        n = slots[(t, off)]
        copy_of(n, (dp, 1 - head)).wait_recv()
        return lands[n].astype(F32)

    level = {}

    def settle(off, t):
        if off not in level:
            total[off] = x[(dp ^ off) * 2 + head] + take(-1, off)
            level[off] = 0
        while level[off] < t:
            w, r = stages[level[off]]
            value = total[off]
            for k in range(1, r):
                value = value + take(level[off], off ^ (k * w))
            total[off] = value
            level[off] += 1

    def rank(off):
        return tuple(0 if (off // w) % r else 1 for w, r in stages)

    for off in sorted(range(count), key=rank):
        push(-1, off, (dp, 1 - head), x[(dp ^ off) * 2 + 1 - head])
    for t, (w, r) in enumerate(stages):
        for k in range(1, r):
            for high in range(0, count, w * r):
                off = k * w + high
                settle(off, t)
                push(t, off, (dp ^ (k * w), head), total[off])
    settle(0, len(stages))
    out[...] = total[0]
    for copy in started:
        copy.wait_send()


def two_parts(block):
    row = block[SMALL_ROW : SMALL_ROW + 1]
    value = row[:, 0:HALF_LANES] + row[:, HALF_LANES : 2 * HALF_LANES]
    high = value.astype(BF).astype(F32)
    rest = jnp.zeros((1, 128 - 2 * HALF_LANES), F32)
    row = jnp.concatenate([high, value - high, rest], axis=1)
    return jnp.concatenate([block[0:SMALL_ROW], row, block[SMALL_ROW + 1 :]], axis=0)


def block_rows(rows):
    starts = []
    at = 0
    for r in rows:
        starts.append(at)
        at += r
    return starts, -(-at // 16) * 16


def gather_pieces_body(count, rows, *refs):
    pieces = refs[0:6]
    buf, send, recv = refs[6:]
    starts, tall = block_rows(rows)
    mine = lax.axis_index("dp") * 2 + lax.axis_index("head")
    parts = [p[...].astype(F32) for p in pieces]
    parts[1] = jnp.concatenate([parts[1], jnp.zeros((1, 128 - parts[1].shape[1]), F32)], axis=1)
    spare = tall - starts[-1] - rows[-1]
    if spare:
        parts.append(jnp.zeros((spare, 128), F32))
    buf[mine] = jnp.concatenate(parts, axis=0).astype(BF)
    gather_blocks(count, buf, send, recv)


def gather_pieces(count, rows, pieces):
    devices = 2 * count
    vm = pl.BlockSpec(memory_space=pltpu.VMEM)
    return pl.pallas_call(
        functools.partial(gather_pieces_body, count, rows),
        out_shape=jax.ShapeDtypeStruct((devices, block_rows(rows)[1], 128), BF),
        in_specs=[vm] * 6,
        out_specs=vm,
        scratch_shapes=[
            pltpu.SemaphoreType.DMA((devices - 1,)),
            pltpu.SemaphoreType.DMA((devices,)),
        ],
        compiler_params=pltpu.CompilerParams(collective_id=0, has_side_effects=True),
    )(*pieces)


def scatter_body(count, split, x, out, total, sends, lands, send, recv):
    shape_row = two_parts if split else lambda block: block
    scatter_blocks(count, x, out, total, sends, lands, send, recv, shape_row)


def scatter(count, split, x):
    devices, tall = x.shape[0:2]
    vm = pl.BlockSpec(memory_space=pltpu.VMEM)
    V = pltpu.VMEM
    return pl.pallas_call(
        functools.partial(scatter_body, count, split),
        out_shape=jax.ShapeDtypeStruct((tall, 128), F32),
        in_specs=[vm],
        out_specs=vm,
        scratch_shapes=[
            V((devices // 2, tall, 128), F32),
            V((devices - 1, tall, 128), BF),
            V((devices - 1, tall, 128), BF),
            pltpu.SemaphoreType.DMA((devices - 1,)),
            pltpu.SemaphoreType.DMA((devices - 1,)),
        ],
        compiler_params=pltpu.CompilerParams(
            collective_id=1, has_side_effects=True, vmem_limit_bytes=58 << 20
        ),
    )(x)


def finish_body(rows, per, slots, block, *outs):
    starts = block_rows(rows)[0]
    for j in (0, 2, 3, 4, 5):
        outs[j][...] = block[starts[j] : starts[j] + rows[j]]
    row = block[starts[1] : starts[1] + 1]
    value = row[:, 0:HALF_LANES] + row[:, HALF_LANES : 2 * HALF_LANES]
    outs[1][...] = value[:, 0:per]
    roots = jnp.sqrt(value[:, per : per + DIRS] * (1.0 / slots) + 1e-06)
    outs[6][...] = jnp.sum(roots, axis=1, keepdims=True)


def finish(rows, per, slots, block):
    vm = pl.BlockSpec(memory_space=pltpu.VMEM)
    shapes = [(r, 128) for r in rows]
    shapes[1] = (1, per)
    shapes.append((1, 1))
    return pl.pallas_call(
        functools.partial(finish_body, rows, per, slots),
        out_shape=tuple(jax.ShapeDtypeStruct(s, F32) for s in shapes),
        in_specs=[vm],
        out_specs=(vm,) * 7,
    )(block)


def gather_whole_body(count, x, buf, send, recv):
    mine = lax.axis_index("dp") * 2 + lax.axis_index("head")
    buf[mine] = x[...]
    gather_blocks(count, buf, send, recv)


def gather_whole(count, x):
    devices = 2 * count
    vm = pl.BlockSpec(memory_space=pltpu.VMEM)
    return pl.pallas_call(
        functools.partial(gather_whole_body, count),
        out_shape=jax.ShapeDtypeStruct((devices,) + x.shape, x.dtype),
        in_specs=[vm],
        out_specs=vm,
        scratch_shapes=[
            pltpu.SemaphoreType.DMA((devices - 1,)),
            pltpu.SemaphoreType.DMA((devices,)),
        ],
        compiler_params=pltpu.CompilerParams(collective_id=0, has_side_effects=True),
    )(x)


def fill_rows(flat):
    rows = -(-flat.shape[-1] // 2048) * 16
    pad = [(0, 0)] * (flat.ndim - 1) + [(0, rows * 128 - flat.shape[-1])]
    return jnp.pad(flat, pad).reshape(flat.shape[:-1] + (rows, 128))


def per_device(count, tokens, cotangent, image_sides, *parts):
    canvas = tokens.shape[0]
    devices = 2 * count
    lengths = [p.shape[0] for p in parts]
    per = lengths[1]
    whole_rows = all(n % 128 == 0 for n in lengths[0:1] + lengths[2:])
    whole_rows = whole_rows and 128 % per == 0 and per + DIRS <= HALF_LANES
    whole_rows = whole_rows and lengths[0] == SMALL_ROW * 128
    rows = [n // 128 for n in lengths]
    rows[1] = 1
    if whole_rows:
        pieces = [p.reshape((1, per) if j == 1 else (-1, 128)) for j, p in enumerate(parts)]
        inputs = [gather_pieces(count, rows, pieces)]
    else:
        blocks = gather_whole(count, fill_rows(jnp.concatenate(parts))).reshape(devices, -1)
        inputs = []
        at = 0
        for n in lengths:
            inputs.append(blocks[:, at : at + n].reshape(-1, 128))
            at += n
    result, gtok, *grads = run_block(
        rows if whole_rows else None, image_sides, tokens.T, cotangent.T, inputs
    )
    slots = float(devices * canvas * D)
    if whole_rows:
        block = scatter(count, True, grads[0])
        *outs, penalty = finish(rows, per, slots, block)
        outs = [o.reshape(-1) for o in outs]
        penalty = penalty.reshape(())
    else:
        squares = grads[1][4, 0:DIRS]
        grads[1] = grads[1][0:4]
        pieces = [g.reshape(devices, -1) for g in grads]
        pieces.append(jnp.broadcast_to(squares[None], (devices, DIRS)))
        block = scatter(count, False, fill_rows(jnp.concatenate(pieces, axis=1))).reshape(-1)
        outs = []
        at = 0
        for n in lengths:
            outs.append(block[at : at + n])
            at += n
        penalty = jnp.sum(jnp.sqrt(block[at : at + DIRS] * (1.0 / slots) + 1e-06))
    return (result.T, gtok.T, penalty, *outs)


def solution(mesh):
    both = P(("dp", "head"))
    plane = P(("dp", "head"), None)
    return jax.shard_map(
        functools.partial(per_device, mesh.shape["dp"]),
        mesh=mesh,
        in_specs=(plane,) * 3 + (both,) * 6,
        out_specs=(plane,) * 2 + (P(),) + (both,) * 6,
        check_vma=False,
    )
```

```python
import functools
import math

import jax
import jax.numpy as jnp
from jax import lax
from jax.experimental import pallas as pl
from jax.experimental.pallas import tpu as pltpu
from jax.sharding import PartitionSpec as P

D = 192
D2 = 2 * D
DIRS = 4
STATES = 16
HEADS = 3
HEAD_DIM = 64
FF = 768
SLOTS = 10
SMAX = 18
EPSILON = 1e-05
ROOT_HALF = 1.0 / math.sqrt(2.0)
DENSITY = 1.0 / math.sqrt(2.0 * math.pi)
F32 = jnp.float32
BF = jnp.bfloat16
PAD_ROWS = {10: 16, 14: 16, 18: 32}
COLUMNS = {10: 5, 14: 7, 18: 6}
WINDOW = {10: 128, 14: 256, 18: 384}
SPARE = 64
TILE = 256
PROB_ROWS = 4096


def contract_second(left, right):
    return lax.dot_general(left, right, (((1,), (1,)), ((), ())), preferred_element_type=F32)


def product(left, right):
    return jnp.dot(left, right, preferred_element_type=F32)


def iota(shape, axis):
    return lax.broadcasted_iota(jnp.int32, shape, axis)


def open_flat(flat, n, width, lanes):
    chunks = -(-width // 128)
    if width % 128 == 0:
        return jnp.concatenate(
            [flat[pl.ds(j, n, stride=chunks), :] for j in range(chunks)], axis=1
        )
    step = width // 64
    half = step // 2
    piece = [flat[pl.ds(j, n // 2, stride=step), :] for j in range(step)]
    piece.append(piece[-1])
    for c in range(chunks):
        lanes[c, pl.ds(0, n // 2, stride=2), :] = piece[c]
        lanes[c, pl.ds(1, n // 2, stride=2), :] = jnp.concatenate(
            [piece[half + c][:, 64:], piece[half + c + 1][:, :64]], axis=1
        )
    return jnp.concatenate([lanes[c, 0:n, :] for c in range(chunks)], axis=1)[:, 0:width]


def close_flat(flat, matrix, lanes):
    n, width = matrix.shape
    chunks = -(-width // 128)
    if width % 128 == 0:
        for j in range(chunks):
            flat[pl.ds(j, n, stride=chunks), :] = matrix[:, 128 * j : 128 * j + 128]
        return
    step = width // 64
    half = step // 2
    for c in range(chunks):
        part = matrix[:, 128 * c : min(width, 128 * c + 128)]
        lanes[c, 0:n, 0 : part.shape[1]] = part
    even = [lanes[c, pl.ds(0, n // 2, stride=2), :] for c in range(chunks)]
    odd = [lanes[c, pl.ds(1, n // 2, stride=2), :] for c in range(chunks)]
    piece = even[:half] + [jnp.concatenate([even[half][:, :64], odd[0][:, :64]], axis=1)]
    piece += [jnp.concatenate([odd[c][:, 64:], odd[c + 1][:, :64]], axis=1) for c in range(half)]
    for j in range(step):
        flat[pl.ds(j, n // 2, stride=step), :] = piece[j]


def as_column(row):
    return jnp.broadcast_to(row, (8, row.shape[1])).T[:, 0:1]


def as_row(column):
    return jnp.broadcast_to(column, (column.shape[0], 128)).T[0:1, :]


def state_column(row, at):
    hit = iota((STATES, 128), 1) == at + iota((STATES, 128), 0)
    return jnp.sum(jnp.where(hit, row, 0.0), axis=1, keepdims=True)


def state_row(column, at):
    hit = iota((STATES, 128), 1) == at + iota((STATES, 128), 0)
    return jnp.sum(jnp.where(hit, column, 0.0), axis=0, keepdims=True)


def pair_lanes(first, second):
    return jnp.where(iota((STATES, D2), 1) < D, first, second)


def spread_rates(rates):
    shape = (STATES, SMAX * STATES)
    state = iota(shape, 1) % STATES == iota(shape, 0)
    return [jnp.sum(jnp.where(state, r, 0.0), axis=0, keepdims=True) for r in rates]


def column_decay(rate, sign):
    shape = (32, SMAX * STATES)
    gap = sign * (iota(shape, 0) - iota(shape, 1) // STATES)
    return jnp.where(gap >= 0, jnp.exp(-rate * jnp.abs(gap).astype(F32)), 0.0)


def normalize(values):
    centered = values - jnp.mean(values, axis=0, keepdims=True)
    scale = lax.rsqrt(jnp.mean(centered * centered, axis=0, keepdims=True) + EPSILON)
    return centered * scale, scale


def normalize_back(grad, unit, scale, gain):
    scaled = grad * gain
    inner = jnp.mean(scaled * unit, axis=0, keepdims=True)
    return scale * (scaled - jnp.mean(scaled, axis=0, keepdims=True) - unit * inner)


def for_images(sides, body):
    def each(k, carry):
        start, row = carry
        side = sides[0, k]
        for s in (10, 14, 18):

            @pl.when(side == s)
            def _():
                body(s, start, row)

        used = jnp.where(side == 10, 128, jnp.where(side == 14, 256, 384)) * HEADS
        return start + side * side, row + jnp.where(side > 0, used, 0)

    return lax.fori_loop(0, SLOTS, each, (0, 0))[0]


def pick_left(q, first, second):
    if q == 0:
        return first
    if q == 2:
        return second
    return jnp.concatenate([first, second], axis=0)


def rows_product(work, rows, depth, left):
    return product(left, jnp.concatenate([work[r, 0:depth, :] for r in rows], axis=1))


def keep_rows(s, u, rows, out, ypad, squares):
    p, q = divmod(u, 3)
    pad = PAD_ROWS[s]
    for i, r in enumerate(rows):
        one = out[0:s, 128 * i : 128 * i + 128]
        if q == 1:
            two = out[pad : pad + s, 128 * i : 128 * i + 128]
            one = jnp.where(iota((s, 128), 1) < HEAD_DIM, one, two)
        at = pl.ds(r, s, stride=24)
        if p == 0:
            ypad[q, at, :] = one
        else:
            ypad[q, at, :] += one
        if squares is not None:
            squares = squares + one * one
    return squares


def place_rows(s, start, ypad, canvas):
    for c in range(s):
        for q in range(3):
            canvas[q, pl.ds(start + c, s, stride=s), :] = ypad[q, pl.ds(24 * c, s), :]


def add_directions(chunks):
    return jnp.concatenate(
        [
            chunks[0] + jnp.concatenate([chunks[1][:, 64:], chunks[2][:, :64]], axis=1),
            chunks[1][:, :64] + chunks[2][:, 64:],
        ],
        axis=1,
    )


def state_forward(s, start, xq, mix, alpha, cols, works, ypad, sums, canvas):
    depth = s * STATES
    pad = PAD_ROWS[s]
    count = COLUMNS[s]

    def left_of(u):
        p, q = divmod(u, 3)
        return pick_left(q, cols[p, 0, 0:pad, 0:depth], cols[p, 1, 0:pad, 0:depth])

    for u in range(6):
        p, q = divmod(u, 3)
        ch = slice(q * 128, (q + 1) * 128)
        m = mix[p, :, ch]
        a = alpha[p, :, ch]
        work = works[u % 2]
        if u:
            out = rows_product(works[(u - 1) % 2], range(s), depth, left_of(u - 1))
        for j in range(s // count):
            state = [None] * count
            for step in range(s):
                r = step if p == 0 else s - 1 - step
                for h in range(count):
                    c = count * j + h
                    term = m * xq[q, pl.ds(start + r * s + c, 1), :]
                    state[h] = term if step == 0 else state[h] * a + term
                    work[r, c * STATES : (c + 1) * STATES, :] = state[h].astype(BF)
        if u:
            sums[u - 1, 0:s] = keep_rows(s, u - 1, range(s), out, ypad, sums[u - 1, 0:s])
    out = rows_product(works[1], range(s), depth, left_of(5))
    sums[5, 0:s] = keep_rows(s, 5, range(s), out, ypad, sums[5, 0:s])
    place_rows(s, start, ypad, canvas)


def column_back(s, d, rate):
    shape = (PAD_ROWS[s], s * STATES)
    there = iota(shape, 1) // STATES
    gap = iota(shape, 0) - (s - 1 - there) if d else there - iota(shape, 0)
    value = jnp.exp(-rate[:, 0 : s * STATES] * gap.astype(F32))
    return jnp.where(gap >= 0, value, 0.0).astype(BF)


def state_backward(s, start, gg, xq, mix, alpha, beta, spread, state, works, ypad, acc, canvas):
    depth = s * STATES
    low = iota((8, 128), 1) < HEAD_DIM
    count = COLUMNS[s]

    def left_of(u):
        p, q = divmod(u, 3)
        first = column_back(s, 0, spread[p, 0:1]) if q < 2 else None
        second = column_back(s, 1, spread[p, 1:2]) if q > 0 else None
        return pick_left(q, first, second)

    for u in range(6):
        p, q = divmod(u, 3)
        ch = slice(q * 128, (q + 1) * 128)
        m = mix[p, :, ch]
        a = alpha[p, :, ch]
        b = beta[p, :, ch]
        work = works[u % 2]
        left = left_of(u - 1) if u else None
        state[...] = jnp.zeros_like(state)

        def at_column(ref, row, c):
            ahead = pl.ds(row + c, 1)
            behind = pl.ds(row + s - 1 - c, 1)
            if q == 0:
                return ref[0, ahead, :]
            if q == 2:
                return ref[2, behind, :]
            one = jnp.broadcast_to(ref[1, ahead, :], (8, 128))
            two = jnp.broadcast_to(ref[1, behind, :], (8, 128))
            value = jnp.where(low, one, two)
            return jnp.concatenate([value, value], axis=0)

        def scan(j, sums):
            one, two, three = sums
            rows = [count * j + h for h in range(count)]
            if u:
                out = rows_product(works[(u - 1) % 2], rows, depth, left)
            mu = [None] * count
            nu = [None] * count
            for step in range(s):
                r = s - 1 - step if p == 0 else step
                e = state[0, r]
                f = state[1, r]
                for h in range(count):
                    c = count * j + h
                    at = pl.ds(pl.multiple_of(c * STATES, STATES), STATES)
                    g = at_column(gg, start + r * s, c)
                    x = at_column(xq, start + r * s, c)
                    decayed = e * b
                    f = f * b + decayed
                    e = x + decayed
                    if step == 0:
                        mu[h] = jnp.broadcast_to(g, (STATES, 128))
                    else:
                        decayed = mu[h] * a
                        nu[h] = decayed if step == 1 else nu[h] * a + decayed
                        mu[h] = g + decayed
                        two = two + nu[h] * e
                    one = one + mu[h] * e
                    three = three + mu[h] * f
                    work[r, at, :] = (m * mu[h]).astype(BF)
                state[0, r] = e
                state[1, r] = f
            if u:
                keep_rows(s, u - 1, rows, out, ypad, None)
            return one, two, three

        sums = lax.fori_loop(0, s // count, scan, tuple(acc[p, i, :, ch] for i in range(3)))
        for i in range(3):
            acc[p, i, :, ch] = sums[i]
    out = rows_product(works[1], range(s), depth, left_of(5))
    keep_rows(s, 5, range(s), out, ypad, None)
    place_rows(s, start, ypad, canvas)


def head_lanes(shape, axis, h):
    return iota(shape, axis) // HEAD_DIM == h


def attend_forward(s, start, row, queries, keys, values, probs, heads):
    size = WINDOW[s]
    a = pl.multiple_of((start // 16) * 16, 16)
    rows = pl.ds(a, size)
    q = queries[rows, :]
    k = keys[rows, :]
    vt = values[rows, :].astype(F32).T
    column = a + iota((size, 1), 0)
    line = a + iota((1, size), 1)
    ok_u = (column >= start) & (column < start + s * s)
    ok_t = (line >= start) & (line < start + s * s)
    ps = []
    vs = []
    for h in range(HEADS):
        qh = jnp.where(head_lanes((size, D), 1, h), q, jnp.zeros_like(q))
        score = jnp.where(ok_u, contract_second(k, qh), -1e30)
        e = jnp.exp(score - jnp.max(score, axis=0, keepdims=True))
        p = e * jnp.where(ok_t, 1.0 / jnp.sum(e, axis=0, keepdims=True), 0.0)
        probs[pl.ds(pl.multiple_of(row + h * size, 128), size), 0:size] = p
        ps.append(p.astype(BF))
        vs.append(jnp.where(head_lanes((D, size), 0, h), vt, 0.0).astype(BF))
    out = product(jnp.concatenate(vs, axis=1), jnp.concatenate(ps, axis=0))
    heads[rows, :] += out.T


def attend_backward(s, start, row, queries, keys, values, probs, grads, gq, gk, gv):
    size = WINDOW[s]
    rows = pl.ds(pl.multiple_of((start // 16) * 16, 16), size)
    q = queries[rows, :]
    k = keys[rows, :]
    v = values[rows, :]
    g = grads[rows, :]
    kt = k.astype(F32).T
    zero = jnp.zeros_like(q)
    ps = []
    ds = []
    gs = []
    qs = []
    ks = []
    for h in range(HEADS):
        lanes = head_lanes((size, D), 1, h)
        p = probs[pl.ds(pl.multiple_of(row + h * size, 128), size), 0:size]
        dp = contract_second(jnp.where(lanes, v, zero), g)
        inner = jnp.sum(dp * p, axis=0, keepdims=True)
        ds.append((p * (dp - inner)).astype(BF))
        ps.append(p.astype(BF))
        gs.append(jnp.where(lanes, g, zero))
        qs.append(jnp.where(lanes, q, zero))
        ks.append(jnp.where(head_lanes((D, size), 0, h), kt, 0.0).astype(BF))
    gv[rows, :] += product(jnp.concatenate(ps, axis=1), jnp.concatenate(gs, axis=0))
    gk[rows, :] += product(jnp.concatenate(ds, axis=1), jnp.concatenate(qs, axis=0))
    out = product(jnp.concatenate(ks, axis=1), jnp.concatenate(ds, axis=0))
    gq[rows, :] += out.T * 0.125


def block_body(
    rows, sides, tok, cot, *refs
):
    if rows is None:
        inputs = refs[0:6]
        outputs = refs[6:14]
        refs = refs[14:]
    else:
        inputs = None
        source = refs[0]
        outputs = refs[1:4]
        refs = refs[4:]
    result, gtok = outputs[0:2]
    (flat, lanes, kept, terms, mix, alpha, beta, cols, spread, unit_one, scale_one, gain_row, xq, gg,
     canvas_buf, ypad, sums, state, work_one, work_two, acc, after_grad) = refs
    V = pltpu.VMEM
    works = (work_one, work_two)
    devices = 32
    if rows is not None:
        per = 128 * 4 // devices
        starts, tall_block = block_rows(rows)
        line = []
        for i in range(devices):
            head, low, high = place_of(i) // 16, place_of(i) // 4 % 4, place_of(i) % 4
            block = source[head, low, high].astype(F32)
            at = 0
            for piece in (0, 2, 3, 4, 5):
                n = rows[piece]
                kept[at + n * i : at + n * (i + 1)] = block[starts[piece] : starts[piece] + n]
                at += n * devices
            line.append(block[starts[1] : starts[1] + 1, 0:per])
        each = 128 // per
        small_values = jnp.concatenate(
            [
                jnp.concatenate(line[r * each : (r + 1) * each], axis=1)
                for r in range(devices // each)
            ],
            axis=0,
        )
    else:
        small_values = inputs[1][...].astype(F32)
        at = 0
        for piece in (0, 2, 3, 4, 5):
            n = inputs[piece].shape[0]
            kept[at : at + n] = inputs[piece][...].astype(F32)
            at += n
    canvas = tok.shape[1]
    rates = small_values[0:1]
    gain_one = as_column(
        jnp.concatenate([small_values[1:2], small_values[2:3, 0:64]], axis=1)
    )
    gain_two = as_column(
        jnp.concatenate([small_values[2:3, 64:128], small_values[3:4]], axis=1)
    )

    sizes = [DIRS * STATES * D, D * 3 * D, D * D, D * FF, FF * D]

    def opened(piece, n, width):
        at = sum(sizes[:piece]) // 128
        return open_flat(kept.at[at : at + n * width // 128], n, width, lanes)

    def closed(piece, matrix):
        n = matrix.shape[0] * matrix.shape[1] // 128
        close_flat(flat, matrix, lanes)
        if rows is None:
            outputs[(2, 4, 5, 6, 7)[piece]][...] = flat[0:n]
        else:
            r = rows[(0, 2, 3, 4, 5)[piece]]
            here = starts[(0, 2, 3, 4, 5)[piece]]
            for i in range(devices):
                terms[i, here : here + r] = flat[r * i : r * (i + 1)]

    coefficients = opened(0, DIRS * STATES, D)
    for p in range(2):
        at = 2 * p * STATES
        mix[p] = jnp.concatenate(
            [coefficients[at : at + STATES], coefficients[at + STATES : at + 2 * STATES]], axis=1
        )
        down = [state_column(rates, at + d * STATES) for d in range(2)]
        across = [state_column(rates, DIRS * STATES + at + d * STATES) for d in range(2)]
        alpha[p] = jnp.exp(-pair_lanes(down[0], down[1]))
        beta[p] = jnp.exp(-pair_lanes(across[0], across[1]))
        rates_over = spread_rates(across)
        for d in range(2):
            cols[p, d] = column_decay(rates_over[d], 1 - 2 * d).astype(BF)
        spread[p, 0:1] = rates_over[0]
        spread[p, 1:2] = rates_over[1]
    unit, scale = normalize(tok[...].astype(F32))
    unit_one[...] = unit
    scale_one[...] = scale
    normed = (unit * gain_one).astype(BF).astype(F32).T
    xq[0] = normed[:, 0:128]
    xq[1] = jnp.concatenate([normed[:, 128:D], normed[:, 0:64]], axis=1)
    xq[2] = normed[:, 64:D]
    canvas_buf[...] = jnp.zeros_like(canvas_buf)
    sums[...] = jnp.zeros_like(sums)
    end = for_images(
        sides,
        lambda s, start, row: state_forward(
            s, start, xq, mix, alpha, cols, works, ypad, sums, canvas_buf
        ),
    )
    mixed_values = add_directions([canvas_buf[q, 0:canvas] for q in range(3)])
    mixed = mixed_values.astype(BF)
    mixed_t = mixed_values.T.astype(BF)
    def middle(queries, keys, values, grads, heads, gq, gk, gv, probs, act, hid, nrm, gml,
               w_out_t, w_up_t, w_down_t):
        w_in = opened(1, D, 3 * D).astype(BF)
        w_q = w_in[:, 0:D]
        w_k = w_in[:, D : 2 * D]
        w_v = w_in[:, 2 * D : 3 * D]
        for ref in (queries, keys, values, grads):
            ref[canvas : canvas + SPARE, :] = jnp.zeros((SPARE, D), BF)
        for ref in (heads, gq, gk, gv):
            ref[...] = jnp.zeros_like(ref)
        queries[0:canvas, :] = (product(mixed, w_q).astype(BF) * 0.125).astype(BF)
        keys[0:canvas, :] = product(mixed, w_k).astype(BF)
        values[0:canvas, :] = product(mixed, w_v).astype(BF)
        for_images(
            sides,
            lambda s, start, row: attend_forward(
                s, start, row, queries, keys, values, probs, heads
            ),
        )
        heads_t = heads[0:canvas, :].T.astype(BF)
        w_out = opened(2, D, D)
        w_out_t[...] = w_out.T.astype(BF)
        w_out = w_out.astype(BF)
        w_up = opened(3, D, FF)
        w_up_t[...] = w_up.T.astype(BF)
        w_up = w_up.astype(BF)
        w_down = opened(4, FF, D)
        w_down_t[...] = w_down.T.astype(BF)
        w_down = w_down.astype(BF)
        grad_gain = jnp.zeros((D, 1), F32)
        for i in range(canvas // TILE):
            here = slice(i * TILE, (i + 1) * TILE)
            live = (i * TILE + iota((1, TILE), 1) < end).astype(F32)
            after = tok[:, here].astype(F32) + live * product(w_out_t[...], heads_t[:, here])
            unit, scale = normalize(after)
            n2 = (unit * gain_two).astype(BF)
            nrm[:, here] = n2
            pre = product(w_up_t[...], n2)
            half = 0.5 * (1.0 + lax.erf(pre * ROOT_HALF))
            bent = (pre * half).astype(BF)
            act[:, here] = bent
            result[:, here] = (after + live * product(w_down_t[...], bent)).astype(BF)
            incoming = cot[:, here].astype(F32)
            gm = (live * incoming).astype(BF)
            gml[:, here] = gm
            slope = half + pre * jnp.exp(-0.5 * pre * pre) * DENSITY
            gh = (product(w_down, gm) * slope).astype(BF)
            hid[:, here] = gh
            gn = product(w_up, gh)
            grad_gain += jnp.sum(gn * unit, axis=1, keepdims=True)
            after_grad[:, here] = incoming + normalize_back(gn, unit, scale, gain_two)
        gain_row[...] = as_row(grad_gain)
        closed(4, contract_second(act[...], gml[...]))
        closed(3, contract_second(nrm[...], hid[...]))
        branch = jnp.where(iota((1, canvas), 1) < end, after_grad[...], 0.0).astype(BF)
        closed(2, contract_second(heads_t, branch))
        grads[0:canvas, :] = product(w_out, branch).T.astype(BF)
        for_images(
            sides,
            lambda s, start, row: attend_backward(
                s, start, row, queries, keys, values, probs, grads, gq, gk, gv
            ),
        )
        gq_low = gq[0:canvas, :].astype(BF)
        gk_low = gk[0:canvas, :].astype(BF)
        gv_low = gv[0:canvas, :].astype(BF)
        grad_in = [product(mixed_t, part) for part in (gq_low, gk_low, gv_low)]
        closed(1, jnp.concatenate(grad_in, axis=1))
        g = contract_second(gq_low, w_q) + contract_second(gk_low, w_k) + contract_second(gv_low, w_v)
        gg[0] = g[:, 0:128]
        gg[1] = jnp.concatenate([g[:, 128:D], g[:, 0:64]], axis=1)
        gg[2] = g[:, 64:D]

    tall = canvas + SPARE
    pl.run_scoped(
        middle,
        V((tall, D), BF), V((tall, D), BF), V((tall, D), BF), V((tall, D), BF),
        V((tall, D), F32), V((tall, D), F32), V((tall, D), F32), V((tall, D), F32),
        V((PROB_ROWS, 384), F32), V((FF, canvas), BF), V((FF, canvas), BF),
        V((D, canvas), BF), V((D, canvas), BF),
        V((D, D), BF), V((FF, D), BF), V((D, FF), BF),
    )
    acc[...] = jnp.zeros_like(acc)
    for_images(
        sides,
        lambda s, start, row: state_backward(
            s, start, gg, xq, mix, alpha, beta, spread, state, works, ypad, acc, canvas_buf
        ),
    )
    gn = add_directions([canvas_buf[q, 0:canvas] for q in range(3)]).T
    unit = unit_one[...]
    rows_gain_one = as_row(jnp.sum(gn * unit, axis=1, keepdims=True))
    gtok[...] = after_grad[...] + normalize_back(gn, unit, scale_one[...], gain_one)
    grad_mix = []
    rate_grads = jnp.zeros((1, 128), F32)
    for p in range(2):
        by_row = mix[p] * acc[p, 1]
        by_col = mix[p] * acc[p, 2]
        for d in range(2):
            ch = slice(d * D, (d + 1) * D)
            at = (2 * p + d) * STATES
            grad_mix.append(acc[p, 0, :, ch])
            rate_grads -= state_row(jnp.sum(by_row[:, ch], axis=1, keepdims=True), at)
            rate_grads -= state_row(
                jnp.sum(by_col[:, ch], axis=1, keepdims=True), DIRS * STATES + at
            )
    closed(0, jnp.concatenate(grad_mix, axis=0))
    rows_gain_two = gain_row[...]
    grad_small = [
        rate_grads,
        rows_gain_one[:, 0:128],
        jnp.concatenate([rows_gain_one[:, 128:D], rows_gain_two[:, 0:64]], axis=1),
        rows_gain_two[:, 64:D],
    ]
    lane = iota((1, 128), 1)
    total = jnp.zeros((1, 128), F32)
    for p in range(2):
        by_lane = [jnp.sum(sums[3 * p + q], axis=0, keepdims=True) for q in range(3)]
        firsts = by_lane[0] + jnp.where(lane < HEAD_DIM, by_lane[1], 0.0)
        seconds = by_lane[2] + jnp.where(lane < HEAD_DIM, 0.0, by_lane[1])
        for d, row in enumerate((firsts, seconds)):
            square = jnp.sum(row, axis=1, keepdims=True)
            total += jnp.where(lane == 2 * p + d, square, 0.0)
    if rows is None:
        for r in range(4):
            outputs[3][r : r + 1] = grad_small[r]
        outputs[3][4:5] = total
        outputs[3][5:8] = jnp.zeros((3, 128), F32)
    else:
        blank = jnp.zeros((1, 128 - per - DIRS), F32)
        for i in range(devices):
            at = per * (i % each)
            own = grad_small[i // each][:, at : at + per]
            row = split_row(jnp.concatenate([own, total[:, 0:DIRS], blank], axis=1))
            terms[i, starts[1] : starts[1] + 1] = row
            block = terms[i]
            if tall_block > starts[5] + rows[5]:
                used = starts[5] + rows[5]
                block = jnp.concatenate(
                    [block[0:used], jnp.zeros((tall_block - used, 128), F32)], axis=0
                )
            head, low, high = place_of(i) // 16, place_of(i) // 4 % 4, place_of(i) % 4
            outputs[2][head, low, high] = block.astype(BF)


def run_block(rows, sides, tok, cot, inputs):
    canvas = tok.shape[1]
    vm = pl.BlockSpec(memory_space=pltpu.VMEM)
    V = pltpu.VMEM
    sh = jax.ShapeDtypeStruct
    wide = SMAX * STATES
    if rows is None:
        grads = tuple(sh((8, 128) if j == 1 else f.shape, F32) for j, f in enumerate(inputs))
    else:
        grads = (sh(inputs[0].shape, BF),)
    states = DIRS * STATES * D // 128
    most = D * FF // 128
    kept = states + D * 4 * D // 128 + 2 * most
    return pl.pallas_call(
        functools.partial(block_body, rows),
        out_shape=(sh((D, canvas), BF), sh((D, canvas), F32)) + grads,
        in_specs=[pl.BlockSpec(memory_space=pltpu.SMEM)] + [vm] * (2 + len(inputs)),
        out_specs=(vm,) * (2 + len(grads)),
        scratch_shapes=[
            V((most, 128), F32), V((5, FF, 128), F32), V((kept, 128), F32),
            V((1, 8, 128) if rows is None else (32,) + inputs[0].shape[3:], F32),
            V((2, STATES, D2), F32), V((2, STATES, D2), F32), V((2, STATES, D2), F32),
            V((2, 2, 32, wide), BF), V((2, 2, wide), F32),
            V((D, canvas), F32), V((1, canvas), F32), V((1, D), F32),
            V((3, canvas, 128), F32), V((3, canvas, 128), F32),
            V((3, canvas + 24, 128), F32), V((3, SMAX * 24, 128), F32), V((6, 24, 128), F32), V((2, SMAX, STATES, 128), F32),
            V((SMAX, wide, 128), BF), V((SMAX, wide, 128), BF), V((2, 3, STATES, D2), F32), V((D, canvas), F32),
        ],
        compiler_params=pltpu.CompilerParams(vmem_limit_bytes=60 << 20),
    )(sides, tok, cot, *inputs)


MESH = pl.DeviceIdType.MESH
SMALL_ROW = 3
HALF_LANES = 32


def xor_stages(count):
    out = []
    weight = 1
    while weight < count:
        radix = 4 if weight * 4 <= count else 2
        out.append((weight, radix))
        weight *= radix
    return out


def greet(dp, head, stages):
    barrier = pltpu.get_barrier_semaphore()
    peers = [(dp ^ (w * k), head) for w, r in stages for k in range(1, r)] + [(dp, 1 - head)]
    for peer in peers:
        pl.semaphore_signal(barrier, inc=1, device_id=peer, device_id_type=MESH)
    pl.semaphore_wait(barrier, len(peers))


def gather_blocks(count, buf, send, recv):
    dp = lax.axis_index("dp")
    head = lax.axis_index("head")
    stages = xor_stages(count)[::-1]
    greet(dp, head, stages)
    started = []

    def copy_of(block, n, slot, peer):
        return pltpu.make_async_remote_copy(
            src_ref=block, dst_ref=block, send_sem=send.at[n], recv_sem=recv.at[slot],
            device_id=peer, device_id_type=MESH,
        )

    def push(off, lands, other):
        block = buf.at[(dp ^ off) * 2 + head]
        peer = (dp, 1 - head) if other else (dp ^ off ^ lands, head)
        copy = copy_of(block, len(started), lands + count * other, peer)
        copy.start()
        started.append(copy)

    def arrived(off, other):
        block = buf.at[(dp ^ off) * 2 + (1 - head if other else head)]
        copy_of(block, 0, off + count * other, (dp, 1 - head)).wait_recv()

    held = [(0, 0)]
    at = 0
    while at < len(held):
        off, stage = held[at]
        at += 1
        if off:
            arrived(off, 0)
        for t in range(stage, len(stages)):
            w, r = stages[t]
            for k in range(1, r):
                push(off, off ^ (w * k), 0)
                held.append((off ^ (w * k), t + 1))
        push(off, off, 1)
    for off in range(count):
        arrived(off, 1)
    for copy in started:
        copy.wait_send()


def scatter_blocks(count, x, out, total, sends, lands, send, recv):
    dp = lax.axis_index("dp")
    head = lax.axis_index("head")
    stages = xor_stages(count)
    greet(dp, head, stages)
    started = []
    slots = {}
    for off in range(count):
        slots[(-1, off)] = len(slots)
    for t, (w, r) in enumerate(stages):
        for k in range(1, r):
            for high in range(0, count, w * r):
                slots[(t, k * w + high)] = len(slots)

    def copy_of(n, peer):
        return pltpu.make_async_remote_copy(
            src_ref=sends.at[n], dst_ref=lands.at[n], send_sem=send.at[n], recv_sem=recv.at[n],
            device_id=peer, device_id_type=MESH,
        )

    def push(t, off, peer, value):
        n = slots[(t, off)]
        sends[n] = value.astype(BF)
        copy = copy_of(n, peer)
        copy.start()
        started.append(copy)

    def take(t, off):
        n = slots[(t, off)]
        copy_of(n, (dp, 1 - head)).wait_recv()
        return lands[n].astype(F32)

    level = {}

    def settle(off, t):
        if off not in level:
            total[off] = x[(dp ^ off) * 2 + head] + take(-1, off)
            level[off] = 0
        while level[off] < t:
            w, r = stages[level[off]]
            value = total[off]
            for k in range(1, r):
                value = value + take(level[off], off ^ (k * w))
            total[off] = value
            level[off] += 1

    def rank(off):
        return tuple(0 if (off // w) % r else 1 for w, r in stages)

    for off in sorted(range(count), key=rank):
        push(-1, off, (dp, 1 - head), x[(dp ^ off) * 2 + 1 - head])
    for t, (w, r) in enumerate(stages):
        for k in range(1, r):
            for high in range(0, count, w * r):
                off = k * w + high
                settle(off, t)
                push(t, off, (dp ^ (k * w), head), total[off])
    settle(0, len(stages))
    out[...] = total[0]
    for copy in started:
        copy.wait_send()


def split_row(row):
    value = row[..., 0:HALF_LANES] + row[..., HALF_LANES : 2 * HALF_LANES]
    high = value.astype(BF).astype(F32)
    rest = jnp.zeros(value.shape[:-1] + (128 - 2 * HALF_LANES,), F32)
    return jnp.concatenate([high, value - high, rest], axis=-1)


def two_parts(block):
    row = split_row(block[..., SMALL_ROW : SMALL_ROW + 1, :])
    return jnp.concatenate(
        [block[..., 0:SMALL_ROW, :], row, block[..., SMALL_ROW + 1 :, :]], axis=-2
    )


def block_rows(rows):
    starts = []
    at = 0
    for r in rows:
        starts.append(at)
        at += r
    return starts, -(-at // 16) * 16


def place_of(device):
    dp, head = divmod(device, 2)
    return (head * 4 + dp % 4) * 4 + dp // 4


def signal_peers(dp, head):
    barrier = pltpu.get_barrier_semaphore()
    for k in range(1, 4):
        for peer in ((dp ^ k, head), (dp ^ (4 * k), head)):
            pl.semaphore_signal(barrier, inc=1, device_id=peer, device_id_type=MESH)
    pl.semaphore_signal(barrier, inc=1, device_id=(dp, 1 - head), device_id_type=MESH)
    return barrier


def gather_pieces_body(rows, *refs):
    pieces = refs[0:6]
    buf, send, recv = refs[6:]
    dp = lax.axis_index("dp")
    head = lax.axis_index("head")
    barrier = signal_peers(dp, head)
    low = dp % 4
    high = dp // 4
    starts, tall = block_rows(rows)
    parts = [p[...].astype(F32) for p in pieces]
    parts[1] = jnp.concatenate([parts[1], jnp.zeros((1, 128 - parts[1].shape[1]), F32)], axis=1)
    spare = tall - starts[-1] - rows[-1]
    if spare:
        parts.append(jnp.zeros((spare, 128), F32))
    buf[head, low, high] = jnp.concatenate(parts, axis=0).astype(BF)
    pl.semaphore_wait(barrier, 7)
    started = []

    def copy_of(block, n, slot, peer):
        return pltpu.make_async_remote_copy(
            src_ref=block, dst_ref=block, send_sem=send.at[n], recv_sem=recv.at[slot],
            device_id=peer, device_id_type=MESH,
        )

    def push(block, slot, peer):
        copy = copy_of(block, len(started), slot, peer)
        copy.start()
        started.append(copy)

    def arrived(block, slot):
        copy_of(block, 0, slot, (dp, 1 - head)).wait_recv()

    own = buf.at[head, low, high]
    for k in range(1, 4):
        push(own, k, (dp ^ (4 * k), head))
    for k in range(1, 4):
        push(own, 4 * k, (dp ^ k, head))
    for j in range(1, 4):
        block = buf.at[head, low, high ^ j]
        arrived(block, j)
        for k in range(1, 4):
            push(block, 4 * k + j, (dp ^ k, head))
    push(buf.at[head, low], 16, (dp, 1 - head))
    for k in range(1, 4):
        for j in range(4):
            arrived(buf.at[head, low ^ k, high ^ j], 4 * k + j)
        push(buf.at[head, low ^ k], 16 + k, (dp, 1 - head))
    for k in range(4):
        arrived(buf.at[1 - head, low ^ k], 16 + k)
    for copy in started:
        copy.wait_send()


def gather_pieces(rows, pieces):
    vm = pl.BlockSpec(memory_space=pltpu.VMEM)
    return pl.pallas_call(
        functools.partial(gather_pieces_body, rows),
        out_shape=jax.ShapeDtypeStruct((2, 4, 4, block_rows(rows)[1], 128), BF),
        in_specs=[vm] * 6,
        out_specs=vm,
        scratch_shapes=[pltpu.SemaphoreType.DMA((19,)), pltpu.SemaphoreType.DMA((20,))],
        compiler_params=pltpu.CompilerParams(collective_id=0, has_side_effects=True),
    )(*pieces)


def scatter_pieces_body(
    x, out, total, low_sends, high_sends, core_lands, low_lands, high_lands, send, recv
):
    dp = lax.axis_index("dp")
    head = lax.axis_index("head")
    barrier = signal_peers(dp, head)
    low = dp % 4
    high = dp // 4
    pl.semaphore_wait(barrier, 7)
    started = []

    def copy_of(source, target, n, peer):
        return pltpu.make_async_remote_copy(
            src_ref=source, dst_ref=target, send_sem=send.at[n], recv_sem=recv.at[n],
            device_id=peer, device_id_type=MESH,
        )

    def push(source, target, n, peer):
        copy = copy_of(source, target, n, peer)
        copy.start()
        started.append(copy)

    def arrived(target, n):
        copy_of(target, target, n, (dp, 1 - head)).wait_recv()

    for k in (1, 2, 3, 0):
        push(x.at[1 - head, low ^ k], core_lands.at[k], k, (dp, 1 - head))
    for k in range(1, 4):
        arrived(core_lands.at[k], k)
        value = x[head, low ^ k].astype(F32) + core_lands[k].astype(F32)
        low_sends[k - 1] = two_parts(value).astype(BF)
        push(low_sends.at[k - 1], low_lands.at[k - 1], 3 + k, (dp ^ k, head))
    arrived(core_lands.at[0], 0)
    value = x[head, low].astype(F32) + core_lands[0].astype(F32)
    for k in range(1, 4):
        arrived(low_lands.at[k - 1], 3 + k)
        value = value + low_lands[k - 1].astype(F32)
    total[...] = value
    for k in range(1, 4):
        high_sends[k - 1] = two_parts(total[high ^ k]).astype(BF)
        push(high_sends.at[k - 1], high_lands.at[k - 1], 6 + k, (dp ^ (4 * k), head))
    value = total[high]
    for k in range(1, 4):
        arrived(high_lands.at[k - 1], 6 + k)
        value = value + high_lands[k - 1].astype(F32)
    out[...] = value
    for copy in started:
        copy.wait_send()


def scatter_pieces(x):
    tall = x.shape[3]
    vm = pl.BlockSpec(memory_space=pltpu.VMEM)
    V = pltpu.VMEM
    return pl.pallas_call(
        scatter_pieces_body,
        out_shape=jax.ShapeDtypeStruct((tall, 128), F32),
        in_specs=[vm],
        out_specs=vm,
        scratch_shapes=[
            V((4, tall, 128), F32), V((3, 4, tall, 128), BF), V((3, tall, 128), BF),
            V((4, 4, tall, 128), BF), V((3, 4, tall, 128), BF), V((3, tall, 128), BF),
            pltpu.SemaphoreType.DMA((10,)), pltpu.SemaphoreType.DMA((10,)),
        ],
        compiler_params=pltpu.CompilerParams(
            collective_id=1, has_side_effects=True, vmem_limit_bytes=58 << 20
        ),
    )(x)


def scatter_body(count, x, out, total, sends, lands, send, recv):
    scatter_blocks(count, x, out, total, sends, lands, send, recv)


def scatter(count, x):
    devices, tall = x.shape[0:2]
    vm = pl.BlockSpec(memory_space=pltpu.VMEM)
    V = pltpu.VMEM
    return pl.pallas_call(
        functools.partial(scatter_body, count),
        out_shape=jax.ShapeDtypeStruct((tall, 128), F32),
        in_specs=[vm],
        out_specs=vm,
        scratch_shapes=[
            V((devices // 2, tall, 128), F32),
            V((devices - 1, tall, 128), BF),
            V((devices - 1, tall, 128), BF),
            pltpu.SemaphoreType.DMA((devices - 1,)),
            pltpu.SemaphoreType.DMA((devices - 1,)),
        ],
        compiler_params=pltpu.CompilerParams(
            collective_id=1, has_side_effects=True, vmem_limit_bytes=58 << 20
        ),
    )(x)


def finish_body(rows, per, slots, block, *outs):
    starts = block_rows(rows)[0]
    for j in (0, 2, 3, 4, 5):
        outs[j][...] = block[starts[j] : starts[j] + rows[j]]
    row = block[starts[1] : starts[1] + 1]
    value = row[:, 0:HALF_LANES] + row[:, HALF_LANES : 2 * HALF_LANES]
    outs[1][...] = value[:, 0:per]
    roots = jnp.sqrt(value[:, per : per + DIRS] * (1.0 / slots) + 1e-06)
    outs[6][...] = jnp.sum(roots, axis=1, keepdims=True)


def finish(rows, per, slots, block):
    vm = pl.BlockSpec(memory_space=pltpu.VMEM)
    shapes = [(r, 128) for r in rows]
    shapes[1] = (1, per)
    shapes.append((1, 1))
    return pl.pallas_call(
        functools.partial(finish_body, rows, per, slots),
        out_shape=tuple(jax.ShapeDtypeStruct(s, F32) for s in shapes),
        in_specs=[vm],
        out_specs=(vm,) * 7,
    )(block)


def gather_whole_body(count, x, buf, send, recv):
    mine = lax.axis_index("dp") * 2 + lax.axis_index("head")
    buf[mine] = x[...]
    gather_blocks(count, buf, send, recv)


def gather_whole(count, x):
    devices = 2 * count
    vm = pl.BlockSpec(memory_space=pltpu.VMEM)
    return pl.pallas_call(
        functools.partial(gather_whole_body, count),
        out_shape=jax.ShapeDtypeStruct((devices,) + x.shape, x.dtype),
        in_specs=[vm],
        out_specs=vm,
        scratch_shapes=[
            pltpu.SemaphoreType.DMA((devices - 1,)),
            pltpu.SemaphoreType.DMA((devices,)),
        ],
        compiler_params=pltpu.CompilerParams(collective_id=0, has_side_effects=True),
    )(x)


def fill_rows(flat):
    rows = -(-flat.shape[-1] // 2048) * 16
    pad = [(0, 0)] * (flat.ndim - 1) + [(0, rows * 128 - flat.shape[-1])]
    return jnp.pad(flat, pad).reshape(flat.shape[:-1] + (rows, 128))


def per_device(count, tokens, cotangent, image_sides, *parts):
    canvas = tokens.shape[0]
    devices = 2 * count
    lengths = [p.shape[0] for p in parts]
    per = lengths[1]
    whole_rows = all(n % 128 == 0 for n in lengths[0:1] + lengths[2:])
    whole_rows = whole_rows and 128 % per == 0 and per + DIRS <= HALF_LANES
    whole_rows = whole_rows and lengths[0] == SMALL_ROW * 128
    whole_rows = whole_rows and count == 16
    rows = [n // 128 for n in lengths]
    rows[1] = 1
    if whole_rows:
        pieces = [p.reshape((1, per) if j == 1 else (-1, 128)) for j, p in enumerate(parts)]
        inputs = [gather_pieces(rows, pieces)]
    else:
        blocks = gather_whole(count, fill_rows(jnp.concatenate(parts))).reshape(devices, -1)
        inputs = []
        at = 0
        for n in lengths:
            inputs.append(blocks[:, at : at + n].reshape(-1, 128))
            at += n
    result, gtok, *grads = run_block(
        rows if whole_rows else None, image_sides, tokens.T, cotangent.T, inputs
    )
    slots = float(devices * canvas * D)
    if whole_rows:
        block = scatter_pieces(grads[0])
        *outs, penalty = finish(rows, per, slots, block)
        outs = [o.reshape(-1) for o in outs]
        penalty = penalty.reshape(())
    else:
        squares = grads[1][4, 0:DIRS]
        grads[1] = grads[1][0:4]
        pieces = [g.reshape(devices, -1) for g in grads]
        pieces.append(jnp.broadcast_to(squares[None], (devices, DIRS)))
        block = scatter(count, fill_rows(jnp.concatenate(pieces, axis=1))).reshape(-1)
        outs = []
        at = 0
        for n in lengths:
            outs.append(block[at : at + n])
            at += n
        penalty = jnp.sum(jnp.sqrt(block[at : at + DIRS] * (1.0 / slots) + 1e-06))
    return (result.T, gtok.T, penalty, *outs)


def solution(mesh):
    both = P(("dp", "head"))
    plane = P(("dp", "head"), None)
    return jax.shard_map(
        functools.partial(per_device, mesh.shape["dp"]),
        mesh=mesh,
        in_specs=(plane,) * 3 + (both,) * 6,
        out_specs=(plane,) * 2 + (P(),) + (both,) * 6,
        check_vma=False,
    )
```

```python
import functools
import math

import jax
import jax.numpy as jnp
from jax import lax
from jax.experimental import pallas as pl
from jax.experimental.pallas import tpu as pltpu
from jax.sharding import PartitionSpec as P

D = 192
D2 = 2 * D
DIRS = 4
STATES = 16
HEADS = 3
HEAD_DIM = 64
FF = 768
SLOTS = 10
SMAX = 18
EPSILON = 1e-05
ROOT_HALF = 1.0 / math.sqrt(2.0)
DENSITY = 1.0 / math.sqrt(2.0 * math.pi)
F32 = jnp.float32
BF = jnp.bfloat16
PAD_ROWS = {10: 16, 14: 16, 18: 32}
COLUMNS = {10: 5, 14: 7, 18: 6}
WINDOW = {10: 128, 14: 256, 18: 384}
SPARE = 64
TILE = 256
PROB_ROWS = 4096


def contract_second(left, right):
    return lax.dot_general(left, right, (((1,), (1,)), ((), ())), preferred_element_type=F32)


def product(left, right):
    return jnp.dot(left, right, preferred_element_type=F32)


def iota(shape, axis):
    return lax.broadcasted_iota(jnp.int32, shape, axis)


def open_flat(flat, n, width, lanes):
    chunks = -(-width // 128)
    if width % 128 == 0:
        return jnp.concatenate(
            [flat[pl.ds(j, n, stride=chunks), :] for j in range(chunks)], axis=1
        )
    step = width // 64
    half = step // 2
    piece = [flat[pl.ds(j, n // 2, stride=step), :] for j in range(step)]
    piece.append(piece[-1])
    for c in range(chunks):
        lanes[c, pl.ds(0, n // 2, stride=2), :] = piece[c]
        lanes[c, pl.ds(1, n // 2, stride=2), :] = jnp.concatenate(
            [piece[half + c][:, 64:], piece[half + c + 1][:, :64]], axis=1
        )
    return jnp.concatenate([lanes[c, 0:n, :] for c in range(chunks)], axis=1)[:, 0:width]


def close_flat(flat, matrix, lanes):
    n, width = matrix.shape
    chunks = -(-width // 128)
    if width % 128 == 0:
        for j in range(chunks):
            flat[pl.ds(j, n, stride=chunks), :] = matrix[:, 128 * j : 128 * j + 128]
        return
    step = width // 64
    half = step // 2
    for c in range(chunks):
        part = matrix[:, 128 * c : min(width, 128 * c + 128)]
        lanes[c, 0:n, 0 : part.shape[1]] = part
    even = [lanes[c, pl.ds(0, n // 2, stride=2), :] for c in range(chunks)]
    odd = [lanes[c, pl.ds(1, n // 2, stride=2), :] for c in range(chunks)]
    piece = even[:half] + [jnp.concatenate([even[half][:, :64], odd[0][:, :64]], axis=1)]
    piece += [jnp.concatenate([odd[c][:, 64:], odd[c + 1][:, :64]], axis=1) for c in range(half)]
    for j in range(step):
        flat[pl.ds(j, n // 2, stride=step), :] = piece[j]


def as_column(row):
    return jnp.broadcast_to(row, (8, row.shape[1])).T[:, 0:1]


def as_row(column):
    return jnp.broadcast_to(column, (column.shape[0], 128)).T[0:1, :]


def state_column(row, at):
    hit = iota((STATES, 128), 1) == at + iota((STATES, 128), 0)
    return jnp.sum(jnp.where(hit, row, 0.0), axis=1, keepdims=True)


def state_row(column, at):
    hit = iota((STATES, 128), 1) == at + iota((STATES, 128), 0)
    return jnp.sum(jnp.where(hit, column, 0.0), axis=0, keepdims=True)


def pair_lanes(first, second):
    return jnp.where(iota((STATES, D2), 1) < D, first, second)


def spread_rates(rates):
    shape = (STATES, SMAX * STATES)
    state = iota(shape, 1) % STATES == iota(shape, 0)
    return [jnp.sum(jnp.where(state, r, 0.0), axis=0, keepdims=True) for r in rates]


def column_decay(rate, sign):
    shape = (32, SMAX * STATES)
    gap = sign * (iota(shape, 0) - iota(shape, 1) // STATES)
    return jnp.where(gap >= 0, jnp.exp(-rate * jnp.abs(gap).astype(F32)), 0.0)


def normalize(values):
    centered = values - jnp.mean(values, axis=0, keepdims=True)
    scale = lax.rsqrt(jnp.mean(centered * centered, axis=0, keepdims=True) + EPSILON)
    return centered * scale, scale


def normalize_back(grad, unit, scale, gain):
    scaled = grad * gain
    inner = jnp.mean(scaled * unit, axis=0, keepdims=True)
    return scale * (scaled - jnp.mean(scaled, axis=0, keepdims=True) - unit * inner)


def prob_rows(side):
    used = jnp.where(side == 10, 128, jnp.where(side == 14, 256, 384)) * HEADS
    return jnp.where(side > 0, used, 0)


def for_images(sides, body):
    def each(k, start):
        side = sides[0, k]
        for s in (10, 14, 18):

            @pl.when(side == s)
            def _():
                body(s, start)

        return start + side * side

    return lax.fori_loop(0, SLOTS, each, 0)


def for_image_pairs(sides, body):
    def each(k, carry):
        start, row = carry
        one = sides[0, 2 * k]
        two = sides[0, 2 * k + 1]
        middle = start + one * one
        later = row + prob_rows(one)
        both = (one == 10) & (two == 10)

        @pl.when(both)
        def _():
            body([(10, start, row), (10, middle, later)])

        @pl.when(jnp.logical_not(both))
        def _():
            for side, begin, at in ((one, start, row), (two, middle, later)):
                for s in (10, 14, 18):

                    @pl.when(side == s)
                    def _():
                        body([(s, begin, at)])

        return middle + two * two, later + prob_rows(two)

    return lax.fori_loop(0, SLOTS // 2, each, (0, 0))[0]


def pick_left(q, first, second):
    if q == 0:
        return first
    if q == 2:
        return second
    return jnp.concatenate([first, second], axis=0)


def rows_product(work, rows, depth, left):
    return product(left, jnp.concatenate([work[r, 0:depth, :] for r in rows], axis=1))


def keep_rows(s, u, rows, out, ypad, squares):
    p, q = divmod(u, 3)
    pad = PAD_ROWS[s]
    for i, r in enumerate(rows):
        one = out[0:s, 128 * i : 128 * i + 128]
        if q == 1:
            two = out[pad : pad + s, 128 * i : 128 * i + 128]
            one = jnp.where(iota((s, 128), 1) < HEAD_DIM, one, two)
        at = pl.ds(r, s, stride=24)
        if p == 0:
            ypad[q, at, :] = one
        else:
            ypad[q, at, :] += one
        if squares is not None:
            squares = squares + one * one
    return squares


def place_rows(s, start, ypad, canvas):
    for c in range(s):
        for q in range(3):
            canvas[q, pl.ds(start + c, s, stride=s), :] = ypad[q, pl.ds(24 * c, s), :]


def add_directions(chunks):
    return jnp.concatenate(
        [
            chunks[0] + jnp.concatenate([chunks[1][:, 64:], chunks[2][:, :64]], axis=1),
            chunks[1][:, :64] + chunks[2][:, 64:],
        ],
        axis=1,
    )


def state_forward(s, start, xq, mix, alpha, cols, works, ypad, sums, canvas):
    depth = s * STATES
    pad = PAD_ROWS[s]
    count = COLUMNS[s]

    def left_of(u):
        p, q = divmod(u, 3)
        return pick_left(q, cols[p, 0, 0:pad, 0:depth], cols[p, 1, 0:pad, 0:depth])

    for u in range(6):
        p, q = divmod(u, 3)
        ch = slice(q * 128, (q + 1) * 128)
        m = mix[p, :, ch]
        a = alpha[p, :, ch]
        work = works[u % 2]
        if u:
            out = rows_product(works[(u - 1) % 2], range(s), depth, left_of(u - 1))
        for j in range(s // count):
            state = [None] * count
            for step in range(s):
                r = step if p == 0 else s - 1 - step
                for h in range(count):
                    c = count * j + h
                    term = m * xq[q, pl.ds(start + r * s + c, 1), :]
                    state[h] = term if step == 0 else state[h] * a + term
                    work[r, c * STATES : (c + 1) * STATES, :] = state[h].astype(BF)
        if u:
            sums[u - 1, 0:s] = keep_rows(s, u - 1, range(s), out, ypad, sums[u - 1, 0:s])
    out = rows_product(works[1], range(s), depth, left_of(5))
    sums[5, 0:s] = keep_rows(s, 5, range(s), out, ypad, sums[5, 0:s])
    place_rows(s, start, ypad, canvas)


def column_back(s, d, rate):
    shape = (PAD_ROWS[s], s * STATES)
    there = iota(shape, 1) // STATES
    gap = iota(shape, 0) - (s - 1 - there) if d else there - iota(shape, 0)
    value = jnp.exp(-rate[:, 0 : s * STATES] * gap.astype(F32))
    return jnp.where(gap >= 0, value, 0.0).astype(BF)


def state_backward(s, start, gg, xq, mix, alpha, beta, lefts, state, works, ypad, acc, canvas):
    depth = s * STATES
    low = iota((8, 128), 1) < HEAD_DIM
    count = COLUMNS[s]

    def left_of(u):
        p, q = divmod(u, 3)
        return pick_left(q, lefts[s][p, 0], lefts[s][p, 1])

    for u in range(6):
        p, q = divmod(u, 3)
        ch = slice(q * 128, (q + 1) * 128)
        m = mix[p, :, ch]
        a = alpha[p, :, ch]
        b = beta[p, :, ch]
        work = works[u % 2]
        left = left_of(u - 1) if u else None
        state[:, 0:s] = jnp.zeros((2, s, STATES, 128), F32)

        def at_column(ref, row, c):
            ahead = pl.ds(row + c, 1)
            behind = pl.ds(row + s - 1 - c, 1)
            if q == 0:
                return ref[0, ahead, :]
            if q == 2:
                return ref[2, behind, :]
            one = jnp.broadcast_to(ref[1, ahead, :], (8, 128))
            two = jnp.broadcast_to(ref[1, behind, :], (8, 128))
            value = jnp.where(low, one, two)
            return jnp.concatenate([value, value], axis=0)

        def scan(j, sums):
            one, two, three = sums
            rows = [count * j + h for h in range(count)]
            if u:
                out = rows_product(works[(u - 1) % 2], rows, depth, left)
            mu = [None] * count
            nu = [None] * count
            for step in range(s):
                r = s - 1 - step if p == 0 else step
                e = state[0, r]
                f = state[1, r]
                for h in range(count):
                    c = count * j + h
                    at = pl.ds(pl.multiple_of(c * STATES, STATES), STATES)
                    g = at_column(gg, start + r * s, c)
                    x = at_column(xq, start + r * s, c)
                    decayed = e * b
                    f = f * b + decayed
                    e = x + decayed
                    if step == 0:
                        mu[h] = jnp.broadcast_to(g, (STATES, 128))
                    else:
                        decayed = mu[h] * a
                        nu[h] = decayed if step == 1 else nu[h] * a + decayed
                        mu[h] = g + decayed
                        two = two + nu[h] * e
                    one = one + mu[h] * e
                    three = three + mu[h] * f
                    work[r, at, :] = (m * mu[h]).astype(BF)
                state[0, r] = e
                state[1, r] = f
            if u:
                keep_rows(s, u - 1, rows, out, ypad, None)
            return one, two, three

        sums = lax.fori_loop(0, s // count, scan, tuple(acc[p, i, :, ch] for i in range(3)))
        for i in range(3):
            acc[p, i, :, ch] = sums[i]
    out = rows_product(works[1], range(s), depth, left_of(5))
    keep_rows(s, 5, range(s), out, ypad, None)
    place_rows(s, start, ypad, canvas)


def head_lanes(shape, axis, h):
    return iota(shape, axis) // HEAD_DIM == h


def attend_forward(images, queries, keys, values, probs, heads):
    held = []
    for s, start, row in images:
        size = WINDOW[s]
        a = pl.multiple_of((start // 16) * 16, 16)
        rows = pl.ds(a, size)
        held.append((size, a, rows, queries[rows, :], keys[rows, :], values[rows, :]))
    outs = []
    for (s, start, row), (size, a, rows, q, k, v) in zip(images, held):
        vt = v.astype(F32).T
        column = a + iota((size, 1), 0)
        line = a + iota((1, size), 1)
        ok_u = (column >= start) & (column < start + s * s)
        ok_t = (line >= start) & (line < start + s * s)
        ps = []
        vs = []
        kept = []
        for h in range(HEADS):
            qh = jnp.where(head_lanes((size, D), 1, h), q, jnp.zeros_like(q))
            score = jnp.where(ok_u, contract_second(k, qh), -1e30)
            e = jnp.exp(score - jnp.max(score, axis=0, keepdims=True))
            p = e * jnp.where(ok_t, 1.0 / jnp.sum(e, axis=0, keepdims=True), 0.0)
            kept.append(p)
            ps.append(p.astype(BF))
            vs.append(jnp.where(head_lanes((D, size), 0, h), vt, 0.0).astype(BF))
        out = product(jnp.concatenate(vs, axis=1), jnp.concatenate(ps, axis=0)).T
        outs.append((out, kept))
    for (s, start, row), (size, a, rows, q, k, v), (out, kept) in zip(images, held, outs):
        for h in range(HEADS):
            probs[pl.ds(pl.multiple_of(row + h * size, 128), size), 0:size] = kept[h]
        heads[rows, :] += out


def attend_backward(images, queries, keys, values, probs, grads, gq, gk, gv):
    held = []
    for s, start, row in images:
        size = WINDOW[s]
        rows = pl.ds(pl.multiple_of((start // 16) * 16, 16), size)
        ps = [
            probs[pl.ds(pl.multiple_of(row + h * size, 128), size), 0:size] for h in range(HEADS)
        ]
        refs = (queries, keys, values, grads)
        held.append((size, rows, ps, *[ref[rows, :] for ref in refs]))
    outs = []
    for size, rows, probabilities, q, k, v, g in held:
        kt = k.astype(F32).T
        zero = jnp.zeros_like(q)
        ps = []
        ds = []
        gs = []
        qs = []
        ks = []
        for h in range(HEADS):
            lanes = head_lanes((size, D), 1, h)
            p = probabilities[h]
            dp = contract_second(jnp.where(lanes, v, zero), g)
            inner = jnp.sum(dp * p, axis=0, keepdims=True)
            ds.append((p * (dp - inner)).astype(BF))
            ps.append(p.astype(BF))
            gs.append(jnp.where(lanes, g, zero))
            qs.append(jnp.where(lanes, q, zero))
            ks.append(jnp.where(head_lanes((D, size), 0, h), kt, 0.0).astype(BF))
        value_part = product(jnp.concatenate(ps, axis=1), jnp.concatenate(gs, axis=0))
        key_part = product(jnp.concatenate(ds, axis=1), jnp.concatenate(qs, axis=0))
        query_part = product(jnp.concatenate(ks, axis=1), jnp.concatenate(ds, axis=0)).T * 0.125
        outs.append((value_part, key_part, query_part))
    for one, (value_part, key_part, query_part) in zip(held, outs):
        rows = one[1]
        gv[rows, :] += value_part
        gk[rows, :] += key_part
        gq[rows, :] += query_part


def block_body(
    rows, sides, tok, cot, *refs
):
    if rows is None:
        inputs = refs[0:6]
        outputs = refs[6:14]
        refs = refs[14:]
    else:
        inputs = None
        source = refs[0]
        outputs = refs[1:4]
        refs = refs[4:]
    result, gtok = outputs[0:2]
    (flat, lanes, kept, terms, mix, alpha, beta, cols, left_10, left_14, left_18, unit_one, scale_one, gain_row, xq, gg,
     canvas_buf, ypad, sums, state, work_one, work_two, acc, after_grad) = refs
    V = pltpu.VMEM
    works = (work_one, work_two)
    lefts = {10: left_10, 14: left_14, 18: left_18}
    devices = 32
    if rows is not None:
        per = 128 * 4 // devices
        starts, tall_block = block_rows(rows)
        line = []
        for i in range(devices):
            head, low, high = place_of(i) // 16, place_of(i) // 4 % 4, place_of(i) % 4
            block = source[head, low, high].astype(F32)
            at = 0
            for piece in (0, 2, 3, 4, 5):
                n = rows[piece]
                kept[at + n * i : at + n * (i + 1)] = block[starts[piece] : starts[piece] + n]
                at += n * devices
            line.append(block[starts[1] : starts[1] + 1, 0:per])
        each = 128 // per
        small_values = jnp.concatenate(
            [
                jnp.concatenate(line[r * each : (r + 1) * each], axis=1)
                for r in range(devices // each)
            ],
            axis=0,
        )
    else:
        small_values = inputs[1][...].astype(F32)
        at = 0
        for piece in (0, 2, 3, 4, 5):
            n = inputs[piece].shape[0]
            kept[at : at + n] = inputs[piece][...].astype(F32)
            at += n
    canvas = tok.shape[1]
    rates = small_values[0:1]
    gain_one = as_column(
        jnp.concatenate([small_values[1:2], small_values[2:3, 0:64]], axis=1)
    )
    gain_two = as_column(
        jnp.concatenate([small_values[2:3, 64:128], small_values[3:4]], axis=1)
    )

    sizes = [DIRS * STATES * D, D * 3 * D, D * D, D * FF, FF * D]

    def opened(piece, n, width):
        at = sum(sizes[:piece]) // 128
        return open_flat(kept.at[at : at + n * width // 128], n, width, lanes)

    def closed(piece, matrix):
        n = matrix.shape[0] * matrix.shape[1] // 128
        close_flat(flat, matrix, lanes)
        if rows is None:
            outputs[(2, 4, 5, 6, 7)[piece]][...] = flat[0:n]
        else:
            r = rows[(0, 2, 3, 4, 5)[piece]]
            here = starts[(0, 2, 3, 4, 5)[piece]]
            for i in range(devices):
                terms[i, here : here + r] = flat[r * i : r * (i + 1)]

    coefficients = opened(0, DIRS * STATES, D)
    for p in range(2):
        at = 2 * p * STATES
        mix[p] = jnp.concatenate(
            [coefficients[at : at + STATES], coefficients[at + STATES : at + 2 * STATES]], axis=1
        )
        down = [state_column(rates, at + d * STATES) for d in range(2)]
        across = [state_column(rates, DIRS * STATES + at + d * STATES) for d in range(2)]
        alpha[p] = jnp.exp(-pair_lanes(down[0], down[1]))
        beta[p] = jnp.exp(-pair_lanes(across[0], across[1]))
        rates_over = spread_rates(across)
        for d in range(2):
            cols[p, d] = column_decay(rates_over[d], 1 - 2 * d).astype(BF)
        for s in lefts:
            for d in range(2):
                lefts[s][p, d] = column_back(s, d, rates_over[d])
    unit, scale = normalize(tok[...].astype(F32))
    unit_one[...] = unit
    scale_one[...] = scale
    normed = (unit * gain_one).astype(BF).astype(F32).T
    xq[0] = normed[:, 0:128]
    xq[1] = jnp.concatenate([normed[:, 128:D], normed[:, 0:64]], axis=1)
    xq[2] = normed[:, 64:D]
    canvas_buf[...] = jnp.zeros_like(canvas_buf)
    sums[...] = jnp.zeros_like(sums)
    end = for_images(
        sides,
        lambda s, start: state_forward(
            s, start, xq, mix, alpha, cols, works, ypad, sums, canvas_buf
        ),
    )
    mixed_values = add_directions([canvas_buf[q, 0:canvas] for q in range(3)])
    mixed = mixed_values.astype(BF)
    mixed_t = mixed_values.T.astype(BF)
    def middle(queries, keys, values, grads, heads, gq, gk, gv, probs, act, hid, nrm, gml,
               w_out_t, w_up_t, w_down_t):
        w_in = opened(1, D, 3 * D).astype(BF)
        w_q = w_in[:, 0:D]
        w_k = w_in[:, D : 2 * D]
        w_v = w_in[:, 2 * D : 3 * D]
        for ref in (queries, keys, values, grads):
            ref[canvas : canvas + SPARE, :] = jnp.zeros((SPARE, D), BF)
        for ref in (heads, gq, gk, gv):
            ref[...] = jnp.zeros_like(ref)
        queries[0:canvas, :] = (product(mixed, w_q).astype(BF) * 0.125).astype(BF)
        keys[0:canvas, :] = product(mixed, w_k).astype(BF)
        values[0:canvas, :] = product(mixed, w_v).astype(BF)
        for_image_pairs(
            sides,
            lambda images: attend_forward(
                images, queries, keys, values, probs, heads
            ),
        )
        heads_t = heads[0:canvas, :].T.astype(BF)
        w_out = opened(2, D, D)
        w_out_t[...] = w_out.T.astype(BF)
        w_out = w_out.astype(BF)
        w_up = opened(3, D, FF)
        w_up_t[...] = w_up.T.astype(BF)
        w_up = w_up.astype(BF)
        w_down = opened(4, FF, D)
        w_down_t[...] = w_down.T.astype(BF)
        w_down = w_down.astype(BF)
        grad_gain = jnp.zeros((D, 1), F32)
        for i in range(canvas // TILE):
            here = slice(i * TILE, (i + 1) * TILE)
            live = (i * TILE + iota((1, TILE), 1) < end).astype(F32)
            after = tok[:, here].astype(F32) + live * product(w_out_t[...], heads_t[:, here])
            unit, scale = normalize(after)
            n2 = (unit * gain_two).astype(BF)
            nrm[:, here] = n2
            pre = product(w_up_t[...], n2)
            half = 0.5 * (1.0 + lax.erf(pre * ROOT_HALF))
            bent = (pre * half).astype(BF)
            act[:, here] = bent
            result[:, here] = (after + live * product(w_down_t[...], bent)).astype(BF)
            incoming = cot[:, here].astype(F32)
            gm = (live * incoming).astype(BF)
            gml[:, here] = gm
            slope = half + pre * jnp.exp(-0.5 * pre * pre) * DENSITY
            gh = (product(w_down, gm) * slope).astype(BF)
            hid[:, here] = gh
            gn = product(w_up, gh)
            grad_gain += jnp.sum(gn * unit, axis=1, keepdims=True)
            after_grad[:, here] = incoming + normalize_back(gn, unit, scale, gain_two)
        gain_row[...] = as_row(grad_gain)
        closed(4, contract_second(act[...], gml[...]))
        closed(3, contract_second(nrm[...], hid[...]))
        branch = jnp.where(iota((1, canvas), 1) < end, after_grad[...], 0.0).astype(BF)
        closed(2, contract_second(heads_t, branch))
        grads[0:canvas, :] = product(w_out, branch).T.astype(BF)
        for_image_pairs(
            sides,
            lambda images: attend_backward(
                images, queries, keys, values, probs, grads, gq, gk, gv
            ),
        )
        gq_low = gq[0:canvas, :].astype(BF)
        gk_low = gk[0:canvas, :].astype(BF)
        gv_low = gv[0:canvas, :].astype(BF)
        grad_in = [product(mixed_t, part) for part in (gq_low, gk_low, gv_low)]
        closed(1, jnp.concatenate(grad_in, axis=1))
        g = contract_second(gq_low, w_q) + contract_second(gk_low, w_k) + contract_second(gv_low, w_v)
        gg[0] = g[:, 0:128]
        gg[1] = jnp.concatenate([g[:, 128:D], g[:, 0:64]], axis=1)
        gg[2] = g[:, 64:D]

    tall = canvas + SPARE
    pl.run_scoped(
        middle,
        V((tall, D), BF), V((tall, D), BF), V((tall, D), BF), V((tall, D), BF),
        V((tall, D), F32), V((tall, D), F32), V((tall, D), F32), V((tall, D), F32),
        V((PROB_ROWS, 384), F32), V((FF, canvas), BF), V((FF, canvas), BF),
        V((D, canvas), BF), V((D, canvas), BF),
        V((D, D), BF), V((FF, D), BF), V((D, FF), BF),
    )
    acc[...] = jnp.zeros_like(acc)
    for_images(
        sides,
        lambda s, start: state_backward(
            s, start, gg, xq, mix, alpha, beta, lefts, state, works, ypad, acc, canvas_buf
        ),
    )
    gn = add_directions([canvas_buf[q, 0:canvas] for q in range(3)]).T
    unit = unit_one[...]
    rows_gain_one = as_row(jnp.sum(gn * unit, axis=1, keepdims=True))
    gtok[...] = after_grad[...] + normalize_back(gn, unit, scale_one[...], gain_one)
    grad_mix = []
    rate_grads = jnp.zeros((1, 128), F32)
    for p in range(2):
        by_row = mix[p] * acc[p, 1]
        by_col = mix[p] * acc[p, 2]
        for d in range(2):
            ch = slice(d * D, (d + 1) * D)
            at = (2 * p + d) * STATES
            grad_mix.append(acc[p, 0, :, ch])
            rate_grads -= state_row(jnp.sum(by_row[:, ch], axis=1, keepdims=True), at)
            rate_grads -= state_row(
                jnp.sum(by_col[:, ch], axis=1, keepdims=True), DIRS * STATES + at
            )
    closed(0, jnp.concatenate(grad_mix, axis=0))
    rows_gain_two = gain_row[...]
    grad_small = [
        rate_grads,
        rows_gain_one[:, 0:128],
        jnp.concatenate([rows_gain_one[:, 128:D], rows_gain_two[:, 0:64]], axis=1),
        rows_gain_two[:, 64:D],
    ]
    lane = iota((1, 128), 1)
    total = jnp.zeros((1, 128), F32)
    for p in range(2):
        by_lane = [jnp.sum(sums[3 * p + q], axis=0, keepdims=True) for q in range(3)]
        firsts = by_lane[0] + jnp.where(lane < HEAD_DIM, by_lane[1], 0.0)
        seconds = by_lane[2] + jnp.where(lane < HEAD_DIM, 0.0, by_lane[1])
        for d, row in enumerate((firsts, seconds)):
            square = jnp.sum(row, axis=1, keepdims=True)
            total += jnp.where(lane == 2 * p + d, square, 0.0)
    if rows is None:
        for r in range(4):
            outputs[3][r : r + 1] = grad_small[r]
        outputs[3][4:5] = total
        outputs[3][5:8] = jnp.zeros((3, 128), F32)
    else:
        blank = jnp.zeros((1, 128 - per - DIRS), F32)
        for i in range(devices):
            at = per * (i % each)
            own = grad_small[i // each][:, at : at + per]
            row = split_row(jnp.concatenate([own, total[:, 0:DIRS], blank], axis=1))
            terms[i, starts[1] : starts[1] + 1] = row
            block = terms[i]
            if tall_block > starts[5] + rows[5]:
                used = starts[5] + rows[5]
                block = jnp.concatenate(
                    [block[0:used], jnp.zeros((tall_block - used, 128), F32)], axis=0
                )
            head, low, high = place_of(i) // 16, place_of(i) // 4 % 4, place_of(i) % 4
            outputs[2][head, low, high] = block.astype(BF)


def run_block(rows, sides, tok, cot, inputs):
    canvas = tok.shape[1]
    vm = pl.BlockSpec(memory_space=pltpu.VMEM)
    V = pltpu.VMEM
    sh = jax.ShapeDtypeStruct
    wide = SMAX * STATES
    if rows is None:
        grads = tuple(sh((8, 128) if j == 1 else f.shape, F32) for j, f in enumerate(inputs))
    else:
        grads = (sh(inputs[0].shape, BF),)
    states = DIRS * STATES * D // 128
    most = D * FF // 128
    kept = states + D * 4 * D // 128 + 2 * most
    return pl.pallas_call(
        functools.partial(block_body, rows),
        out_shape=(sh((D, canvas), BF), sh((D, canvas), F32)) + grads,
        in_specs=[pl.BlockSpec(memory_space=pltpu.SMEM)] + [vm] * (2 + len(inputs)),
        out_specs=(vm,) * (2 + len(grads)),
        scratch_shapes=[
            V((most, 128), F32), V((5, FF, 128), F32), V((kept, 128), F32),
            V((1, 8, 128) if rows is None else (32,) + inputs[0].shape[3:], F32),
            V((2, STATES, D2), F32), V((2, STATES, D2), F32), V((2, STATES, D2), F32),
            V((2, 2, 32, wide), BF),
            *[V((2, 2, PAD_ROWS[s], s * STATES), BF) for s in (10, 14, 18)],
            V((D, canvas), F32), V((1, canvas), F32), V((1, D), F32),
            V((3, canvas, 128), F32), V((3, canvas, 128), F32),
            V((3, canvas + 24, 128), F32), V((3, SMAX * 24, 128), F32), V((6, 24, 128), F32), V((2, SMAX, STATES, 128), F32),
            V((SMAX, wide, 128), BF), V((SMAX, wide, 128), BF), V((2, 3, STATES, D2), F32), V((D, canvas), F32),
        ],
        compiler_params=pltpu.CompilerParams(vmem_limit_bytes=60 << 20),
    )(sides, tok, cot, *inputs)


MESH = pl.DeviceIdType.MESH
SMALL_ROW = 3
HALF_LANES = 32


def xor_stages(count):
    out = []
    weight = 1
    while weight < count:
        radix = 4 if weight * 4 <= count else 2
        out.append((weight, radix))
        weight *= radix
    return out


def greet(dp, head, stages):
    barrier = pltpu.get_barrier_semaphore()
    peers = [(dp ^ (w * k), head) for w, r in stages for k in range(1, r)] + [(dp, 1 - head)]
    for peer in peers:
        pl.semaphore_signal(barrier, inc=1, device_id=peer, device_id_type=MESH)
    pl.semaphore_wait(barrier, len(peers))


def gather_blocks(count, buf, send, recv):
    dp = lax.axis_index("dp")
    head = lax.axis_index("head")
    stages = xor_stages(count)[::-1]
    greet(dp, head, stages)
    started = []

    def copy_of(block, n, slot, peer):
        return pltpu.make_async_remote_copy(
            src_ref=block, dst_ref=block, send_sem=send.at[n], recv_sem=recv.at[slot],
            device_id=peer, device_id_type=MESH,
        )

    def push(off, lands, other):
        block = buf.at[(dp ^ off) * 2 + head]
        peer = (dp, 1 - head) if other else (dp ^ off ^ lands, head)
        copy = copy_of(block, len(started), lands + count * other, peer)
        copy.start()
        started.append(copy)

    def arrived(off, other):
        block = buf.at[(dp ^ off) * 2 + (1 - head if other else head)]
        copy_of(block, 0, off + count * other, (dp, 1 - head)).wait_recv()

    held = [(0, 0)]
    at = 0
    while at < len(held):
        off, stage = held[at]
        at += 1
        if off:
            arrived(off, 0)
        for t in range(stage, len(stages)):
            w, r = stages[t]
            for k in range(1, r):
                push(off, off ^ (w * k), 0)
                held.append((off ^ (w * k), t + 1))
        push(off, off, 1)
    for off in range(count):
        arrived(off, 1)
    for copy in started:
        copy.wait_send()


def scatter_blocks(count, x, out, total, sends, lands, send, recv):
    dp = lax.axis_index("dp")
    head = lax.axis_index("head")
    stages = xor_stages(count)
    greet(dp, head, stages)
    started = []
    slots = {}
    for off in range(count):
        slots[(-1, off)] = len(slots)
    for t, (w, r) in enumerate(stages):
        for k in range(1, r):
            for high in range(0, count, w * r):
                slots[(t, k * w + high)] = len(slots)

    def copy_of(n, peer):
        return pltpu.make_async_remote_copy(
            src_ref=sends.at[n], dst_ref=lands.at[n], send_sem=send.at[n], recv_sem=recv.at[n],
            device_id=peer, device_id_type=MESH,
        )

    def push(t, off, peer, value):
        n = slots[(t, off)]
        sends[n] = value.astype(BF)
        copy = copy_of(n, peer)
        copy.start()
        started.append(copy)

    def take(t, off):
        n = slots[(t, off)]
        copy_of(n, (dp, 1 - head)).wait_recv()
        return lands[n].astype(F32)

    level = {}

    def settle(off, t):
        if off not in level:
            total[off] = x[(dp ^ off) * 2 + head] + take(-1, off)
            level[off] = 0
        while level[off] < t:
            w, r = stages[level[off]]
            value = total[off]
            for k in range(1, r):
                value = value + take(level[off], off ^ (k * w))
            total[off] = value
            level[off] += 1

    def rank(off):
        return tuple(0 if (off // w) % r else 1 for w, r in stages)

    for off in sorted(range(count), key=rank):
        push(-1, off, (dp, 1 - head), x[(dp ^ off) * 2 + 1 - head])
    for t, (w, r) in enumerate(stages):
        for k in range(1, r):
            for high in range(0, count, w * r):
                off = k * w + high
                settle(off, t)
                push(t, off, (dp ^ (k * w), head), total[off])
    settle(0, len(stages))
    out[...] = total[0]
    for copy in started:
        copy.wait_send()


def split_row(row):
    value = row[..., 0:HALF_LANES] + row[..., HALF_LANES : 2 * HALF_LANES]
    high = value.astype(BF).astype(F32)
    rest = jnp.zeros(value.shape[:-1] + (128 - 2 * HALF_LANES,), F32)
    return jnp.concatenate([high, value - high, rest], axis=-1)


def two_parts(block):
    row = split_row(block[..., SMALL_ROW : SMALL_ROW + 1, :])
    return jnp.concatenate(
        [block[..., 0:SMALL_ROW, :], row, block[..., SMALL_ROW + 1 :, :]], axis=-2
    )


def block_rows(rows):
    starts = []
    at = 0
    for r in rows:
        starts.append(at)
        at += r
    return starts, -(-at // 16) * 16


def place_of(device):
    dp, head = divmod(device, 2)
    return (head * 4 + dp % 4) * 4 + dp // 4


def signal_peers(dp, head):
    barrier = pltpu.get_barrier_semaphore()
    for k in range(1, 4):
        for peer in ((dp ^ k, head), (dp ^ (4 * k), head)):
            pl.semaphore_signal(barrier, inc=1, device_id=peer, device_id_type=MESH)
    pl.semaphore_signal(barrier, inc=1, device_id=(dp, 1 - head), device_id_type=MESH)
    return barrier


def gather_pieces_body(rows, *refs):
    pieces = refs[0:6]
    buf, send, recv = refs[6:]
    dp = lax.axis_index("dp")
    head = lax.axis_index("head")
    barrier = signal_peers(dp, head)
    low = dp % 4
    high = dp // 4
    starts, tall = block_rows(rows)
    parts = [p[...].astype(F32) for p in pieces]
    parts[1] = jnp.concatenate([parts[1], jnp.zeros((1, 128 - parts[1].shape[1]), F32)], axis=1)
    spare = tall - starts[-1] - rows[-1]
    if spare:
        parts.append(jnp.zeros((spare, 128), F32))
    buf[head, low, high] = jnp.concatenate(parts, axis=0).astype(BF)
    pl.semaphore_wait(barrier, 7)
    started = []

    def copy_of(block, n, slot, peer):
        return pltpu.make_async_remote_copy(
            src_ref=block, dst_ref=block, send_sem=send.at[n], recv_sem=recv.at[slot],
            device_id=peer, device_id_type=MESH,
        )

    def push(block, slot, peer):
        copy = copy_of(block, len(started), slot, peer)
        copy.start()
        started.append(copy)

    def arrived(block, slot):
        copy_of(block, 0, slot, (dp, 1 - head)).wait_recv()

    own = buf.at[head, low, high]
    for k in range(1, 4):
        push(own, k, (dp ^ (4 * k), head))
    for k in range(1, 4):
        push(own, 4 * k, (dp ^ k, head))
    for j in range(1, 4):
        block = buf.at[head, low, high ^ j]
        arrived(block, j)
        for k in range(1, 4):
            push(block, 4 * k + j, (dp ^ k, head))
    push(buf.at[head, low], 16, (dp, 1 - head))
    for k in range(1, 4):
        for j in range(4):
            arrived(buf.at[head, low ^ k, high ^ j], 4 * k + j)
        push(buf.at[head, low ^ k], 16 + k, (dp, 1 - head))
    for k in range(4):
        arrived(buf.at[1 - head, low ^ k], 16 + k)
    for copy in started:
        copy.wait_send()


def gather_pieces(rows, pieces):
    vm = pl.BlockSpec(memory_space=pltpu.VMEM)
    return pl.pallas_call(
        functools.partial(gather_pieces_body, rows),
        out_shape=jax.ShapeDtypeStruct((2, 4, 4, block_rows(rows)[1], 128), BF),
        in_specs=[vm] * 6,
        out_specs=vm,
        scratch_shapes=[pltpu.SemaphoreType.DMA((19,)), pltpu.SemaphoreType.DMA((20,))],
        compiler_params=pltpu.CompilerParams(collective_id=0, has_side_effects=True),
    )(*pieces)


def scatter_pieces_body(
    x, out, total, low_sends, high_sends, core_lands, low_lands, high_lands, send, recv
):
    dp = lax.axis_index("dp")
    head = lax.axis_index("head")
    barrier = signal_peers(dp, head)
    low = dp % 4
    high = dp // 4
    pl.semaphore_wait(barrier, 7)
    started = []

    def copy_of(source, target, n, peer):
        return pltpu.make_async_remote_copy(
            src_ref=source, dst_ref=target, send_sem=send.at[n], recv_sem=recv.at[n],
            device_id=peer, device_id_type=MESH,
        )

    def push(source, target, n, peer):
        copy = copy_of(source, target, n, peer)
        copy.start()
        started.append(copy)

    def arrived(target, n):
        copy_of(target, target, n, (dp, 1 - head)).wait_recv()

    for k in (1, 2, 3, 0):
        push(x.at[1 - head, low ^ k], core_lands.at[k], k, (dp, 1 - head))
    for k in range(1, 4):
        arrived(core_lands.at[k], k)
        value = x[head, low ^ k].astype(F32) + core_lands[k].astype(F32)
        low_sends[k - 1] = two_parts(value).astype(BF)
        push(low_sends.at[k - 1], low_lands.at[k - 1], 3 + k, (dp ^ k, head))
    arrived(core_lands.at[0], 0)
    value = x[head, low].astype(F32) + core_lands[0].astype(F32)
    for k in range(1, 4):
        arrived(low_lands.at[k - 1], 3 + k)
        value = value + low_lands[k - 1].astype(F32)
    total[...] = value
    for k in range(1, 4):
        high_sends[k - 1] = two_parts(total[high ^ k]).astype(BF)
        push(high_sends.at[k - 1], high_lands.at[k - 1], 6 + k, (dp ^ (4 * k), head))
    value = total[high]
    for k in range(1, 4):
        arrived(high_lands.at[k - 1], 6 + k)
        value = value + high_lands[k - 1].astype(F32)
    out[...] = value
    for copy in started:
        copy.wait_send()


def scatter_pieces(x):
    tall = x.shape[3]
    vm = pl.BlockSpec(memory_space=pltpu.VMEM)
    V = pltpu.VMEM
    return pl.pallas_call(
        scatter_pieces_body,
        out_shape=jax.ShapeDtypeStruct((tall, 128), F32),
        in_specs=[vm],
        out_specs=vm,
        scratch_shapes=[
            V((4, tall, 128), F32), V((3, 4, tall, 128), BF), V((3, tall, 128), BF),
            V((4, 4, tall, 128), BF), V((3, 4, tall, 128), BF), V((3, tall, 128), BF),
            pltpu.SemaphoreType.DMA((10,)), pltpu.SemaphoreType.DMA((10,)),
        ],
        compiler_params=pltpu.CompilerParams(
            collective_id=1, has_side_effects=True, vmem_limit_bytes=58 << 20
        ),
    )(x)


def scatter_body(count, x, out, total, sends, lands, send, recv):
    scatter_blocks(count, x, out, total, sends, lands, send, recv)


def scatter(count, x):
    devices, tall = x.shape[0:2]
    vm = pl.BlockSpec(memory_space=pltpu.VMEM)
    V = pltpu.VMEM
    return pl.pallas_call(
        functools.partial(scatter_body, count),
        out_shape=jax.ShapeDtypeStruct((tall, 128), F32),
        in_specs=[vm],
        out_specs=vm,
        scratch_shapes=[
            V((devices // 2, tall, 128), F32),
            V((devices - 1, tall, 128), BF),
            V((devices - 1, tall, 128), BF),
            pltpu.SemaphoreType.DMA((devices - 1,)),
            pltpu.SemaphoreType.DMA((devices - 1,)),
        ],
        compiler_params=pltpu.CompilerParams(
            collective_id=1, has_side_effects=True, vmem_limit_bytes=58 << 20
        ),
    )(x)


def finish_body(rows, per, slots, block, *outs):
    starts = block_rows(rows)[0]
    for j in (0, 2, 3, 4, 5):
        outs[j][...] = block[starts[j] : starts[j] + rows[j]]
    row = block[starts[1] : starts[1] + 1]
    value = row[:, 0:HALF_LANES] + row[:, HALF_LANES : 2 * HALF_LANES]
    outs[1][...] = value[:, 0:per]
    roots = jnp.sqrt(value[:, per : per + DIRS] * (1.0 / slots) + 1e-06)
    outs[6][...] = jnp.sum(roots, axis=1, keepdims=True)


def finish(rows, per, slots, block):
    vm = pl.BlockSpec(memory_space=pltpu.VMEM)
    shapes = [(r, 128) for r in rows]
    shapes[1] = (1, per)
    shapes.append((1, 1))
    return pl.pallas_call(
        functools.partial(finish_body, rows, per, slots),
        out_shape=tuple(jax.ShapeDtypeStruct(s, F32) for s in shapes),
        in_specs=[vm],
        out_specs=(vm,) * 7,
    )(block)


def gather_whole_body(count, x, buf, send, recv):
    mine = lax.axis_index("dp") * 2 + lax.axis_index("head")
    buf[mine] = x[...]
    gather_blocks(count, buf, send, recv)


def gather_whole(count, x):
    devices = 2 * count
    vm = pl.BlockSpec(memory_space=pltpu.VMEM)
    return pl.pallas_call(
        functools.partial(gather_whole_body, count),
        out_shape=jax.ShapeDtypeStruct((devices,) + x.shape, x.dtype),
        in_specs=[vm],
        out_specs=vm,
        scratch_shapes=[
            pltpu.SemaphoreType.DMA((devices - 1,)),
            pltpu.SemaphoreType.DMA((devices,)),
        ],
        compiler_params=pltpu.CompilerParams(collective_id=0, has_side_effects=True),
    )(x)


def fill_rows(flat):
    rows = -(-flat.shape[-1] // 2048) * 16
    pad = [(0, 0)] * (flat.ndim - 1) + [(0, rows * 128 - flat.shape[-1])]
    return jnp.pad(flat, pad).reshape(flat.shape[:-1] + (rows, 128))


def per_device(count, tokens, cotangent, image_sides, *parts):
    canvas = tokens.shape[0]
    devices = 2 * count
    lengths = [p.shape[0] for p in parts]
    per = lengths[1]
    whole_rows = all(n % 128 == 0 for n in lengths[0:1] + lengths[2:])
    whole_rows = whole_rows and 128 % per == 0 and per + DIRS <= HALF_LANES
    whole_rows = whole_rows and lengths[0] == SMALL_ROW * 128
    whole_rows = whole_rows and count == 16
    rows = [n // 128 for n in lengths]
    rows[1] = 1
    if whole_rows:
        pieces = [p.reshape((1, per) if j == 1 else (-1, 128)) for j, p in enumerate(parts)]
        inputs = [gather_pieces(rows, pieces)]
    else:
        blocks = gather_whole(count, fill_rows(jnp.concatenate(parts))).reshape(devices, -1)
        inputs = []
        at = 0
        for n in lengths:
            inputs.append(blocks[:, at : at + n].reshape(-1, 128))
            at += n
    result, gtok, *grads = run_block(
        rows if whole_rows else None, image_sides, tokens.T, cotangent.T, inputs
    )
    slots = float(devices * canvas * D)
    if whole_rows:
        block = scatter_pieces(grads[0])
        *outs, penalty = finish(rows, per, slots, block)
        outs = [o.reshape(-1) for o in outs]
        penalty = penalty.reshape(())
    else:
        squares = grads[1][4, 0:DIRS]
        grads[1] = grads[1][0:4]
        pieces = [g.reshape(devices, -1) for g in grads]
        pieces.append(jnp.broadcast_to(squares[None], (devices, DIRS)))
        block = scatter(count, fill_rows(jnp.concatenate(pieces, axis=1))).reshape(-1)
        outs = []
        at = 0
        for n in lengths:
            outs.append(block[at : at + n])
            at += n
        penalty = jnp.sum(jnp.sqrt(block[at : at + DIRS] * (1.0 / slots) + 1e-06))
    return (result.T, gtok.T, penalty, *outs)


def solution(mesh):
    both = P(("dp", "head"))
    plane = P(("dp", "head"), None)
    return jax.shard_map(
        functools.partial(per_device, mesh.shape["dp"]),
        mesh=mesh,
        in_specs=(plane,) * 3 + (both,) * 6,
        out_specs=(plane,) * 2 + (P(),) + (both,) * 6,
        check_vma=False,
    )
```
